128 devices in a mesh: gx: 4 (over z), gy: 32 (over x, y, core).
Axes of the slice: x: 4, y: 4, z: 4, core: 2. Of those that a mesh axis runs over, the one named last changes fastest.
Arguments:
- positions: float32 [3, 2097152], P(None, ('gx', 'gy')), may hold values from -0.5 to 0.5, as said below
- charges: float32 [2097152], P(('gx', 'gy')), may hold values from -0.36 to 0.36
- near_leaves: int32 [16384, 27], P(('gx', 'gy')), may hold values from -1 to 16383, as said below
- near_offsets: int32 [16384, 27], P(('gx', 'gy')), may hold values from 0 to 26, as said below
- far_leaves: int32 [16384, 189], P(('gx', 'gy')), may hold values from -1 to 2175, as said below
- far_leaf_class: int32 [16384, 189], P(('gx', 'gy')), may hold values from 0 to 15
- leaf_plan: int32 [128, 128, 16], P(('gx', 'gy')), may hold values from -1 to 127, as said below
- far_parents: int32 [2048, 189], P(('gx', 'gy')), may hold values from -1 to 527, as said below
- far_parent_class: int32 [2048, 189], P(('gx', 'gy')), may hold values from 0 to 15
- parent_plan: int32 [128, 128, 4], P(('gx', 'gy')), may hold values from -1 to 15, as said below
- coarse_lists: int32 [32, 7], replicated, may hold values from 0 to 31, as said below
- coarse_class: int32 [32, 7], replicated, may hold values from 0 to 15
- up_shift: float32 [8, 286, 286], replicated, may hold values from -4 to 4
- down_shift: float32 [8, 286, 286], replicated, may hold values from -4 to 4
- far_shift: float32 [16, 286, 286], replicated, may hold values from -2 to 2
Outputs:
- potential: float32 [2097152], P(('gx', 'gy'))
The draws below stay inside these ranges and needn't reach their ends.
Inputs may be any that keep to these rules, and one draw needn't show every extreme that they name: `positions`: each coordinate lies within half a leaf width of its leaf centre. `near_leaves`: entry 0 of every list is the leaf itself with offset class 13; the other entries name leaves at most 32 before the first leaf or after the last leaf of the list's own device; -1 pads a list's tail. `near_offsets`: entry 0 is 13. `leaf_plan`: row d, column o lists distinct local indices of leaves of device o that device d names, then -1; at most 16 a pair, reached in every draw; a device names none of its own. `far_leaves`: slots name only own leaves or filled entries of the device's row of leaf_plan; -1 pads a list's tail. `parent_plan`: as leaf_plan, for parent cells, at most 4 a pair, reached in every draw. `far_parents`: slots name only own parents or filled entries of the device's row of parent_plan; -1 pads a list's tail. `coarse_lists`: each row names distinct cells other than its own.
All inputs are finite; a program needn't handle non-finite values.
Results may differ from the reference program's by a relative error of at most 0.0003.
Values sent between devices are 32-bit elements; how exact they have to be, the bound alone decides.
No kernel may reach another device: no remote copies, remote signals or barrier semaphores. Data moves between devices by JAX's collectives and lax.ppermute only.
A program may use at most 192 MiB of HBM per device.

```python
import math
import jax
import jax.numpy as jnp
import numpy as np
from jax import lax

ORDER = 10
COEF = 286
LEAF_SIZE = 128
LEAF_DEV = 128
K_NEAR = 27
K_FAR = 189
K_COARSE = 7
OFFSETS = 16
CAP_L = 16
CAP_P = 4
RIM = 32
P_DEV = 16
LEAVES = 16384
PARENTS = 2048
NCOARSE = 32
PARTICLES = 2097152


def degree_table(order):
    spreads = []
    for degree in range(order + 1):
        for first_power in range(degree, -1, -1):
            for second_power in range(degree - first_power, -1, -1):
                third_power = degree - first_power - second_power
                product = (2 * first_power + 1) * (2 * second_power + 1) * (2 * third_power + 1)
                spreads.append(1.0 / math.sqrt(product))
    return jnp.asarray(np.array(spreads, dtype=np.float32))


def draw_positions(key, part):
    key = jax.random.fold_in(key, 41)
    return jax.random.uniform(key, (3, PARTICLES), jnp.float32, -0.5, 0.5)


def draw_up_shift(key, part):
    key = jax.random.fold_in(key, 42)
    scales = degree_table(ORDER)
    entries = jax.random.truncated_normal(key, -3.0, 3.0, (8, COEF, COEF), jnp.float32)
    return entries * (scales[None, :, None] / scales[None, None, :]) * (8.0 * COEF) ** (-0.5)


def draw_down_shift(key, part):
    key = jax.random.fold_in(key, 43)
    scales = degree_table(ORDER)
    entries = jax.random.truncated_normal(key, -3.0, 3.0, (8, COEF, COEF), jnp.float32)
    return entries * (scales[None, None, :] / scales[None, :, None]) * (1.0 * COEF) ** (-0.5)


def draw_far_shift(key, part):
    key = jax.random.fold_in(key, 44)
    scales = degree_table(ORDER)
    entries = jax.random.truncated_normal(key, -3.0, 3.0, (OFFSETS, COEF, COEF), jnp.float32)
    return entries / (scales[None, :, None] * scales[None, None, :]) * (1.0 * COEF * COEF * K_FAR) ** (-0.5)


def let_plan(key, salt, cells_dev, capacity, list_width):
    key = jax.random.fold_in(key, salt)
    device_count = LEAVES // LEAF_DEV
    keys = jax.random.split(key, 6)
    device_range = jnp.arange(device_count, dtype=jnp.int32)
    counts = jax.random.randint(keys[0], (device_count, device_count), 1, capacity + 1)
    stride = jax.random.randint(keys[1], (device_count,), 1, device_count)
    stride = stride.at[0].set(device_count - 1)
    fullest = (device_range + stride) % device_count
    counts = jnp.where(device_range[None, :] == fullest[:, None], capacity, counts)
    counts = jnp.where(device_range[None, :] == device_range[:, None], 0, counts)
    scores = jax.random.randint(keys[2], (device_count, device_count, cells_dev), 0, 1 << 20) * cells_dev + jnp.arange(cells_dev, dtype=jnp.int32)
    scores = scores.at[0, device_count - 1, cells_dev - 1].set(-1)
    ranking = jnp.argsort(scores, axis=-1)[:, :, :capacity].astype(jnp.int32)
    plan = jnp.where(jnp.arange(capacity, dtype=jnp.int32) < counts[:, :, None], ranking, -1)
    owner = jax.random.randint(keys[3], (device_count, cells_dev, list_width), 0, device_count)
    owner = owner.at[0, 0, 1].set(device_count - 1)
    picks = jax.random.randint(keys[4], (device_count, cells_dev, list_width), 0, 1 << 20)
    picks = picks.at[0, 0, 1].set(capacity - 1)
    own_cell = owner == device_range[:, None, None]
    available = counts[device_range[:, None, None], owner]
    chosen = picks % jnp.where(own_cell, cells_dev, jnp.maximum(available, 1))
    slots = jnp.where(own_cell, chosen, cells_dev + owner * capacity + chosen)
    filled = jax.random.randint(keys[5], (device_count, cells_dev), list_width // 2, list_width + 1)
    filled = filled.at[:, 0].set(list_width).at[0, 1].set(list_width // 2)
    slots = jnp.where(jnp.arange(list_width, dtype=jnp.int32) < filled[:, :, None], slots, -1)
    return (plan.astype(jnp.int32), slots.reshape(device_count * cells_dev, list_width).astype(jnp.int32))


def draw_leaf_plan(key, part):
    return let_plan(key, 11, LEAF_DEV, CAP_L, K_FAR)[0]


def draw_far_leaves(key, part):
    return let_plan(key, 11, LEAF_DEV, CAP_L, K_FAR)[1]


def draw_parent_plan(key, part):
    return let_plan(key, 12, P_DEV, CAP_P, K_FAR)[0]


def draw_far_parents(key, part):
    return let_plan(key, 12, P_DEV, CAP_P, K_FAR)[1]


def draw_near_leaves(key, part):
    key = jax.random.fold_in(key, 21)
    keys = jax.random.split(key, 2)
    leaf_ids = jnp.arange(LEAVES, dtype=jnp.int32)
    owner = leaf_ids // LEAF_DEV
    lowest = jnp.maximum(owner * LEAF_DEV - RIM, 0)
    highest_leaf = jnp.minimum((owner + 1) * LEAF_DEV + RIM, LEAVES)
    picks = jax.random.randint(keys[0], (LEAVES, K_NEAR), 0, 1 << 20)
    named = lowest[:, None] + picks % (highest_leaf - lowest)[:, None]
    first_leaf = leaf_ids % LEAF_DEV == 0
    last_leaf = leaf_ids % LEAF_DEV == LEAF_DEV - 1
    reach = jnp.where(first_leaf, owner * LEAF_DEV - RIM, jnp.where(last_leaf, (owner + 1) * LEAF_DEV + RIM - 1, named[:, 1]))
    reach = jnp.clip(reach, 0, LEAVES - 1)
    named = named.at[:, 1].set(reach).at[:, 0].set(leaf_ids)
    filled = jax.random.randint(keys[1], (LEAVES,), 8, K_NEAR + 1)
    filled = filled.at[1].set(8)
    return jnp.where(jnp.arange(K_NEAR, dtype=jnp.int32) < filled[:, None], named, -1).astype(jnp.int32)


def draw_near_offsets(key, part):
    key = jax.random.fold_in(key, 22)
    classes = jax.random.randint(key, (LEAVES, K_NEAR), 0, 27)
    return classes.at[:, 0].set(13).astype(jnp.int32)


def draw_coarse_lists(key, part):
    key = jax.random.fold_in(key, 31)
    scores = jax.random.randint(key, (NCOARSE, NCOARSE - 1), 0, 1 << 20) * (NCOARSE - 1) + jnp.arange(NCOARSE - 1, dtype=jnp.int32)
    scores = scores.at[0, NCOARSE - 2].set(-1).at[NCOARSE - 1, 0].set(-1)
    ranking = jnp.argsort(scores, axis=-1)[:, :K_COARSE].astype(jnp.int32)
    return ((jnp.arange(NCOARSE, dtype=jnp.int32)[:, None] + 1 + ranking) % NCOARSE).astype(jnp.int32)


def place_ends(drawn, stream_key, low, top_value):
    longest = drawn.shape.index(max(drawn.shape))
    spots = []
    for shift in (0, 1):
        where = [jax.random.randint(jax.random.fold_in(stream_key, axis), (), 0, length) for axis, length in enumerate(drawn.shape)]
        where[longest] = (where[longest] + shift) % drawn.shape[longest]
        spots.append(tuple(where))
    return drawn.at[spots[0]].set(low).at[spots[1]].set(top_value)


def levels(key, dims, cuts, smallest, top_value):
    def one(dim, parts):
        heights = jax.random.uniform(jax.random.fold_in(jax.random.fold_in(key, 6), dim), (parts,), jnp.float32, smallest / len(cuts), top_value / len(cuts))
        return jnp.repeat(jnp.exp(heights), dims[dim] // parts).reshape((-1,) + (1,) * (len(dims) - dim - 1))

    loudness = one(*cuts[0])
    for cut in cuts[1:]:
        loudness = loudness * one(*cut)
    return loudness


def scatter_about(key, shape, scale, most, cuts=(), held_as=jnp.bfloat16):
    values = scale * jax.random.normal(key, shape, jnp.float32)
    if cuts:
        values = values * levels(key, shape, cuts, -0.22, 0.18)
    return jnp.clip(values, -most, most).astype(held_as)


def setup_inputs(seed: int = 0) -> dict:
    key_list = jax.random.split(jax.random.key(seed), 16)
    positions = draw_positions(jax.random.fold_in(key_list[15], 71), 0)
    charges = scatter_about(key_list[1], (PARTICLES,), 0.06, 0.36, ((0, 128),), jnp.float32)
    near_leaves = draw_near_leaves(jax.random.fold_in(key_list[15], 71), 0)
    near_offsets = draw_near_offsets(jax.random.fold_in(key_list[15], 71), 0)
    far_leaves = draw_far_leaves(jax.random.fold_in(key_list[15], 71), 0)
    far_leaf_class = place_ends(jax.random.randint(key_list[5], (LEAVES, K_FAR), 0, OFFSETS), jax.random.fold_in(key_list[5], 1), 0, OFFSETS - 1).astype(jnp.int32)
    leaf_plan = draw_leaf_plan(jax.random.fold_in(key_list[15], 71), 0)
    far_parents = draw_far_parents(jax.random.fold_in(key_list[15], 71), 0)
    far_parent_class = place_ends(jax.random.randint(key_list[8], (PARENTS, K_FAR), 0, OFFSETS), jax.random.fold_in(key_list[8], 1), 0, OFFSETS - 1).astype(jnp.int32)
    parent_plan = draw_parent_plan(jax.random.fold_in(key_list[15], 71), 0)
    coarse_lists = draw_coarse_lists(jax.random.fold_in(key_list[15], 71), 0)
    coarse_class = place_ends(jax.random.randint(key_list[11], (NCOARSE, K_COARSE), 0, OFFSETS), jax.random.fold_in(key_list[11], 1), 0, OFFSETS - 1).astype(jnp.int32)
    up_shift = draw_up_shift(jax.random.fold_in(key_list[15], 71), 0)
    down_shift = draw_down_shift(jax.random.fold_in(key_list[15], 71), 0)
    far_shift = draw_far_shift(jax.random.fold_in(key_list[15], 71), 0)
    return dict(positions=positions, charges=charges, near_leaves=near_leaves, near_offsets=near_offsets, far_leaves=far_leaves, far_leaf_class=far_leaf_class, leaf_plan=leaf_plan, far_parents=far_parents, far_parent_class=far_parent_class, parent_plan=parent_plan, coarse_lists=coarse_lists, coarse_class=coarse_class, up_shift=up_shift, down_shift=down_shift, far_shift=far_shift)


softening = 0.05
highest = lax.Precision.HIGHEST

def exponents(order):
    entries = []
    for degree in range(order + 1):
        for first_power in range(degree, -1, -1):
            for second_power in range(degree - first_power, -1, -1):
                entries.append((first_power, second_power, degree - first_power - second_power))
    return np.array(entries, dtype=np.int32).T

def basis(coords):
    scaled = 2.0 * coords
    powers = [jnp.ones_like(scaled)]
    for degree in range(ORDER):
        powers.append(powers[-1] * scaled)
    stacked = jnp.stack(powers)
    exponent_table = exponents(ORDER)
    return stacked[exponent_table[0], 0] * stacked[exponent_table[1], 1] * stacked[exponent_table[2], 2]

def upward(children, up_shift):
    grouped = children.reshape(children.shape[0], -1, 8)
    return jnp.einsum('cab,bnc->an', up_shift, grouped, precision=highest)

def downward(parents, down_shift):
    spread = jnp.einsum('cab,bn->anc', down_shift, parents, precision=highest)
    return spread.reshape(spread.shape[0], -1)

def far_field(sources, slots, classes, far_shift, block):
    targets, list_width = slots.shape
    operator_count = far_shift.shape[0]

    def one_block(pieces):
        slot_block, class_block = pieces
        present = slot_block >= 0
        columns = sources[:, jnp.maximum(slot_block, 0)]
        selector = ((class_block[..., None] == jnp.arange(operator_count, dtype=jnp.int32)) & present[..., None]).astype(jnp.float32)
        grouped = jnp.einsum('ctk,tko->otc', columns, selector, precision=highest)
        return jnp.einsum('oac,otc->at', far_shift, grouped, precision=highest)
    if targets <= block:
        return one_block((slots, classes))
    results = lax.map(one_block, (slots.reshape(-1, block, list_width), classes.reshape(-1, block, list_width)))
    return jnp.moveaxis(results, 0, 1).reshape(sources.shape[0], targets)

def near_sum(sources, targets, source_index, present, near_leaves, near_offsets, target_ids):
    leaf_count, leaf_size = (targets.shape[1], targets.shape[2])
    diagonal = jnp.eye(leaf_size, dtype=bool)

    def add_slot(entry_slot, running):
        source_rows = lax.dynamic_index_in_dim(source_index, entry_slot, 1, keepdims=False)
        neighbour = lax.dynamic_index_in_dim(near_leaves, entry_slot, 1, keepdims=False)
        counted_slot = lax.dynamic_index_in_dim(present, entry_slot, 1, keepdims=False)
        offset_class = lax.dynamic_index_in_dim(near_offsets, entry_slot, 1, keepdims=False)
        gathered = sources[:, source_rows]
        shift_x = (offset_class // 9 - 1).astype(jnp.float32)
        shift_y = (offset_class // 3 % 3 - 1).astype(jnp.float32)
        shift_z = (offset_class % 3 - 1).astype(jnp.float32)
        step_x = gathered[0][:, None, :] + shift_x[:, None, None] - targets[0][:, :, None]
        step_y = gathered[1][:, None, :] + shift_y[:, None, None] - targets[1][:, :, None]
        step_z = gathered[2][:, None, :] + shift_z[:, None, None] - targets[2][:, :, None]
        squared = step_x * step_x + step_y * step_y + step_z * step_z + softening * softening
        itself = (neighbour == target_ids) & (offset_class == 13)
        counted = counted_slot[:, None, None] & jnp.logical_not(itself[:, None, None] & diagonal[None])
        contributions = jnp.where(counted, gathered[3][:, None, :] * lax.rsqrt(squared), 0.0)
        return running + lax.optimization_barrier(jnp.sum(contributions, axis=2))
    return lax.fori_loop(0, near_leaves.shape[1], add_slot, jnp.zeros((leaf_count, leaf_size), jnp.float32))

def decode(slots, plan, cells_dev):
    capacity = plan.shape[2]
    owner_row = (jnp.arange(slots.shape[0], dtype=jnp.int32) // cells_dev)[:, None]
    ghost = jnp.maximum(slots - cells_dev, 0)
    owner = ghost // capacity
    position = ghost % capacity
    remote = owner * cells_dev + plan[owner_row, owner, position]
    return jnp.where(slots < 0, -1, jnp.where(slots < cells_dev, owner_row * cells_dev + slots, remote))

def reference(positions, charges, near_leaves, near_offsets, far_leaves, far_leaf_class, leaf_plan, far_parents, far_parent_class, parent_plan, coarse_lists, coarse_class, up_shift, down_shift, far_shift):
    coef_count = up_shift.shape[1]
    blocks = LEAVES // 512
    span = 512 * LEAF_SIZE
    coords = jnp.moveaxis(positions.reshape(3, blocks, span), 1, 0)
    weights = charges.reshape(blocks, span)

    def moments(pieces):
        block_coords, block_weights = pieces
        return (basis(block_coords) * block_weights).reshape(coef_count, 512, LEAF_SIZE).sum(axis=2)
    leaf_multipoles = jnp.moveaxis(lax.map(moments, (coords, weights)), 0, 1).reshape(coef_count, LEAVES)
    parent_multipoles = upward(leaf_multipoles, up_shift)
    grand_multipoles = upward(parent_multipoles, up_shift)
    coarse_multipoles = upward(grand_multipoles, up_shift)
    coarse_locals = far_field(coarse_multipoles, coarse_lists, coarse_class, far_shift, 256)
    grand_locals = downward(coarse_locals, down_shift)
    source_parent = decode(far_parents, parent_plan, P_DEV)
    parent_locals = downward(grand_locals, down_shift) + far_field(parent_multipoles, source_parent, far_parent_class, far_shift, 256)
    source_leaf = decode(far_leaves, leaf_plan, LEAF_DEV)
    leaf_locals = downward(parent_locals, down_shift) + far_field(leaf_multipoles, source_leaf, far_leaf_class, far_shift, 256)
    local_blocks = jnp.moveaxis(leaf_locals.reshape(coef_count, blocks, 512), 1, 0)

    def evaluate(pieces):
        block_coords, block_locals = pieces
        values = basis(block_coords).reshape(coef_count, 512, LEAF_SIZE)
        return jnp.einsum('alp,al->lp', values, block_locals, precision=highest)
    far_potential = lax.map(evaluate, (coords, local_blocks))
    particle_data = jnp.concatenate([positions, charges[None]], 0).reshape(4, LEAVES, LEAF_SIZE)

    def near_block(index):
        start = (index * 512).astype(jnp.int32)
        targets = lax.dynamic_slice_in_dim(particle_data, start, 512, 1)
        rows = lax.dynamic_slice_in_dim(near_leaves, start, 512, 0)
        offsets = lax.dynamic_slice_in_dim(near_offsets, start, 512, 0)
        target_ids = start + jnp.arange(512, dtype=jnp.int32)
        return near_sum(particle_data, targets, jnp.maximum(rows, 0), rows >= 0, rows, offsets, target_ids)
    near_potential = lax.map(near_block, jnp.arange(blocks, dtype=jnp.int32))
    return near_potential.reshape(-1) + far_potential.reshape(-1)
```

```python
import jax
import jax.numpy as jnp
import numpy as np
from jax import lax
from jax.experimental import pallas as pl
from jax.experimental.pallas import tpu as pltpu
from jax.sharding import PartitionSpec as P

ORDER = 10
COEF = 286
RIM = 32
LEAF = 128
K_NEAR = 27
CAP_L = 16
CAP_P = 4
ROWS = 48
TARGETS = 160
GROUP = 8
SOFT = 0.05 * 0.05
AXES = ("gx", "gy")
F32 = jnp.float32
BF16 = jnp.bfloat16
VMEM = pl.BlockSpec(memory_space=pltpu.VMEM)
SMEM = pl.BlockSpec(memory_space=pltpu.SMEM)


def exponents(order):
    entries = []
    for degree in range(order + 1):
        for first_power in range(degree, -1, -1):
            for second_power in range(degree - first_power, -1, -1):
                entries.append((first_power, second_power, degree - first_power - second_power))
    return entries


INDEX = {powers: number for number, powers in enumerate(exponents(ORDER))}


def split(x):
    high = x.astype(BF16)
    return high, (x - high.astype(F32)).astype(BF16)


def nt(a, b):
    return lax.dot_general(a, b, (((1,), (1,)), ((), ())), preferred_element_type=F32)


def nn(a, b):
    return jnp.dot(a, b, preferred_element_type=F32)


def apply_operator(rows, operator):
    row_high, row_low = split(rows)
    high, low = split(operator)
    return nt(row_high, high) + (nt(row_low, high) + nt(row_high, low))


def joined(ref, rows):
    return jnp.concatenate([ref[h, rows, :] for h in range(3)], axis=1)[:, :COEF]


def upward_kernel(dev_ref, pos_ref, chg_ref, up_ref, lt_ref, pt_ref, lift_ref, moments, wide):
    x, y, z = [2.0 * pos_ref[d].T for d in range(3)]
    with_x = chg_ref[...].T
    z_powers = [None, z]
    for k in range(ORDER - 1):
        z_powers.append(z_powers[-1] * z)
    moments[COEF - 6 : 384, :] = jnp.zeros((384 - COEF + 6, LEAF), F32)
    for i in range(ORDER + 1):
        if i:
            with_x = with_x * x
        with_xy = with_x
        for j in range(ORDER + 1 - i):
            if j:
                with_xy = with_xy * y
            for k in range(ORDER + 1 - i - j):
                term = with_xy * z_powers[k] if k else with_xy
                a = INDEX[(i, j, k)]
                moments[a : a + 1, :] = jnp.sum(term, axis=0, keepdims=True)
    for h in range(3):
        lt_ref[h] = moments[128 * h : 128 * h + 128, :].T
    wide[...] = jnp.zeros_like(wide)
    total = jnp.zeros((16, COEF), F32)
    for c in range(8):
        total = total + apply_operator(joined(lt_ref, pl.ds(c, 16, stride=8)), up_ref[c])
    wide[:, :COEF] = total
    for h in range(3):
        pt_ref[h] = wide[:, 128 * h : 128 * h + 128]
    grand = jnp.zeros((2, COEF), F32)
    for c in range(8):
        rows = jnp.concatenate([wide[c : c + 1, :COEF], wide[8 + c : 9 + c, :COEF]], axis=0)
        grand = grand + apply_operator(rows, up_ref[c])
    first = lax.rem(2 * dev_ref[0], 8)
    lifted = apply_operator(grand[0:1], up_ref[first]) + apply_operator(grand[1:2], up_ref[first + 1])
    wide[0:1, :COEF] = lifted
    for h in range(3):
        lift_ref[h : h + 1, :] = wide[0:1, 128 * h : 128 * h + 128]


def pack_kernel(asked_ref, lt_ref, pt_ref, lift_ref, out_ref):
    lane = lax.broadcasted_iota(jnp.int32, (128, 128), 1)
    leaf_rows = jnp.concatenate([lt_ref[h] for h in range(3)], axis=1)
    parent_rows = jnp.concatenate([pt_ref[h] for h in range(3)], axis=1)
    parent_rows = jnp.concatenate([parent_rows, jnp.zeros((112, 384), F32)], axis=0)
    leaf_rows = jnp.concatenate(split(leaf_rows), axis=0)
    parent_rows = jnp.concatenate(split(parent_rows), axis=0)
    for q in range(5):
        tail = jnp.zeros((128, 128), F32)
        for p in range(4):
            j = 4 * q + p
            chosen = jnp.where(asked_ref[:, j : j + 1] == lane, 1.0, 0.0).astype(BF16)
            chosen = jnp.concatenate([chosen, chosen], axis=1)
            rows = nn(chosen, leaf_rows if q < 4 else parent_rows)
            out_ref[:, 2 * j, :] = rows[:, 0:128]
            out_ref[:, 2 * j + 1, :] = rows[:, 128:256]
            part = rows[:, 256:384]
            tail = tail + (pltpu.roll(part, 32 * p, 1) if p else part)
        out_ref[:, 40 + q, :] = tail
    for h in range(3):
        out_ref[:, 45 + h, :] = jnp.broadcast_to(lift_ref[h : h + 1, :], (128, 128))


def near_kernel(code_ref, count_ref, self_ref, own_ref, before_ref, after_ref, out_ref,
                eight, offsets, features, spread, sums, even, odd, plan_even, plan_odd):
    sub = lax.broadcasted_iota(jnp.int32, (8, 128), 0)
    zeros = jnp.zeros((8, 128), F32)
    eight[...] = jnp.zeros_like(eight)
    for d, row in ((0, 0), (1, 1), (2, 2), (3, 5)):
        eight[0:RIM, row, :] = before_ref[d]
        eight[RIM : RIM + LEAF, row, :] = own_ref[d]
        eight[RIM + LEAF : 2 * RIM + LEAF, row, :] = after_ref[d]
    for o in range(27):
        shift = (o // 9 - 1, o // 3 % 3 - 1, o % 3 - 1)
        table = jnp.where(sub == 3, SOFT, jnp.where(sub == 4, 1.0, zeros))
        for d in range(3):
            table = jnp.where(sub == d, -float(shift[d]), table)
        offsets[o] = table

    def thirds(v):
        high = v.astype(BF16).astype(F32)
        rest = v - high
        middle = rest.astype(BF16).astype(F32)
        return high, middle, rest - middle

    def norm(v):
        return jnp.sum(jnp.where(sub < 3, v * v, 0.0), axis=0, keepdims=True)

    def target(leaf, offset):
        v = eight[RIM + leaf] + offsets[offset]
        v = jnp.where(sub == 3, v + norm(v), v)
        high, middle, low = thirds(v)
        rows = jnp.concatenate([high, high, high, middle, middle, low], axis=0)
        rows = jnp.concatenate([rows, jnp.zeros((80, 128), F32)], axis=0)
        return rows.astype(BF16)

    def source(leaf):
        v = eight[leaf]
        v = jnp.where(sub < 3, -2.0 * v, jnp.where(sub == 3, 1.0, jnp.where(sub == 4, norm(v), 0.0)))
        high, middle, low = thirds(v)
        rows = jnp.concatenate([high, middle, low, high, middle, high], axis=0)
        rows = jnp.concatenate([rows, jnp.zeros((80, 128), F32)], axis=0)
        features[leaf] = rows.T.astype(BF16)
        charge = jnp.broadcast_to(eight[leaf, 5:6, :], (128, 128))
        spread[leaf] = charge.T

    def prepare(step, carry):
        for u in range(4):
            source(4 * step + u)
        return carry

    lax.fori_loop(0, (LEAF + 2 * RIM) // 4, prepare, 0)
    diagonal = lax.broadcasted_iota(jnp.int32, (128, 128), 0) == lax.broadcasted_iota(
        jnp.int32, (128, 128), 1
    )

    def own_leaf(step, carry):
        for u in range(4):
            leaf = 4 * step + u
            squared = nn(features[RIM + leaf], target(leaf, 13))
            terms = jnp.where(diagonal, 0.0, spread[RIM + leaf] * lax.rsqrt(squared))
            sums[leaf] = jnp.sum(terms.reshape(16, 8, 128), axis=0) * self_ref[leaf].astype(F32)
        return carry

    lax.fori_loop(0, LEAF // 4, own_leaf, 0)

    def produce(buffer, plan, state):
        leaf, entry = state
        for g in range(GROUP):
            done = entry >= count_ref[leaf]
            leaf = jnp.where(done, jnp.minimum(leaf + 1, LEAF), leaf)
            entry = jnp.where(done, 1, entry)
            code = code_ref[leaf * K_NEAR + entry]
            entry = entry + 1
            real = code >= 0
            code = jnp.maximum(code, 0)
            place = jnp.minimum(leaf, LEAF - 1)
            plan[g] = code // 32
            plan[GROUP + g] = place
            plan[2 * GROUP + g] = jnp.where(real, 1, 0)
            buffer[g] = nn(features[code // 32], target(place, lax.rem(code, 32)))
        return leaf, entry

    def consume(buffer, plan):
        for g in range(GROUP):
            terms = spread[plan[g]] * lax.rsqrt(buffer[g])
            place = plan[GROUP + g]
            part = jnp.sum(terms.reshape(16, 8, 128), axis=0)
            sums[place] = sums[place] + part * plan[2 * GROUP + g].astype(F32)

    state = produce(even, plan_even, (jnp.int32(0), jnp.int32(1)))

    def two_groups(step, state):
        state = produce(odd, plan_odd, state)
        consume(even, plan_even)
        state = produce(even, plan_even, state)
        consume(odd, plan_odd)
        return state

    total = count_ref[LEAF + 1]
    lax.fori_loop(0, (total + 2 * GROUP - 1) // (2 * GROUP), two_groups, state)
    out_ref[...] = jnp.sum(sums[...], axis=1)


def count_rows(code, low, rows):
    wide = lax.broadcasted_iota(jnp.int32, (rows, 256), 0) == code
    narrow = lax.broadcasted_iota(jnp.int32, (128, 256), 0) == low
    return nt(
        jnp.where(wide, 1.0, 0.0).astype(BF16), jnp.where(narrow, 1.0, 0.0).astype(BF16)
    ).astype(BF16)


def counts_kernel(leaf_ref, leaf_class_ref, parent_ref, parent_class_ref, s_ref, sp_ref,
                  code_scr, low_scr):
    code_scr[...] = jnp.full_like(code_scr, -1)
    low_scr[...] = jnp.full_like(low_scr, -1)

    def one_level(slot_ref, class_ref, cells, capacity, out_ref):
        slots = slot_ref[...]
        ghost = jnp.maximum(slots - cells, 0)
        own = slots < cells
        position = lax.rem(ghost, capacity)
        code = jnp.where(own, 0, 1 + position) * 16 + class_ref[...]
        code_scr[:, : slots.shape[1]] = jnp.where(slots < 0, -1, code)
        low_scr[:, : slots.shape[1]] = jnp.where(own, slots, lax.div(ghost, capacity))
        blocks = capacity + 1
        for t in range(16):
            table = count_rows(code_scr[t : t + 1, :], low_scr[t : t + 1, :], 16 * blocks)
            for b in range(blocks):
                out_ref[16 * t : 16 * t + 16, 128 * b : 128 * b + 128] = table[16 * b : 16 * b + 16]

    one_level(leaf_ref, leaf_class_ref, LEAF, CAP_L, s_ref)

    @pl.when(pl.program_id(0) == 0)
    def _():
        one_level(parent_ref, parent_class_ref, 16, CAP_P, sp_ref)


def far_kernel(dev_ref, lists_ref, class_ref, s_ref, sp_ref, lt_ref, pt_ref, arrived_ref, pos_ref,
               near_ref, down_hbm, far_hbm, out_ref,
               src, src_parent, grouped, locals_rows, wide, loc, result, down_ref, far_ref, sems):
    step = pl.program_id(0)
    lane = lax.broadcasted_iota(jnp.int32, (128, 128), 1)

    def place(ref, row, parts):
        count = parts[0].shape[0]
        (h0, l0), (h1, l1) = split(parts[0]), split(parts[1])
        tail = parts[2]
        high = tail.astype(BF16).astype(F32)
        low = pltpu.roll(tail - high, 32, 1)
        ref[row : row + count, 0:128] = h0
        ref[row : row + count, 128:256] = h1
        ref[row : row + count, 256:384] = l0
        ref[row : row + count, 384:512] = l1
        ref[row : row + count, 512:640] = (high + low).astype(BF16)

    def collect(product, row, count):
        grouped[0, pl.ds(row, count), :] = product[:, 0:128] + product[:, 256:384]
        grouped[1, pl.ds(row, count), :] = product[:, 128:256] + product[:, 384:512]
        tail = product[:, 512:640]
        grouped[2, pl.ds(row, count), :] = tail + pltpu.roll(tail, 96, 1)

    def arrived_tail(row, p):
        part = arrived_ref[:, row, :]
        part = pltpu.roll(part, 128 - 32 * p, 1) if p else part
        return jnp.where(lane < 32, part, 0.0)

    @pl.when(step == 0)
    def _():
        pltpu.make_async_copy(down_hbm, down_ref, sems.at[0]).start()
        pltpu.make_async_copy(far_hbm, far_ref, sems.at[1]).start()
        place(src, 0, [lt_ref[h] for h in range(3)])
        for c in range(CAP_L):
            place(
                src,
                128 * (c + 1),
                [arrived_ref[:, 2 * c, :], arrived_ref[:, 2 * c + 1, :], arrived_tail(40 + c // 4, c % 4)],
            )
        own = [jnp.concatenate([pt_ref[h], jnp.zeros((112, 128), F32)], axis=0) for h in range(3)]
        place(src_parent, 0, own)
        for c in range(CAP_P):
            place(
                src_parent,
                128 * (c + 1),
                [arrived_ref[:, 32 + 2 * c, :], arrived_ref[:, 33 + 2 * c, :], arrived_tail(44, c)],
            )
        collect(nn(sp_ref[...], src_parent[...]), 2048, 256)
        mine = dev_ref[0] // 4
        operator = lax.broadcasted_iota(jnp.int32, (16, 128), 0)
        cell = lax.broadcasted_iota(jnp.int32, (16, 128), 1) // 4
        chosen = jnp.zeros((16, 128), F32)
        for k in range(7):
            hit = (operator == class_ref[mine * 7 + k]) & (cell == lists_ref[mine * 7 + k])
            chosen = chosen + jnp.where(hit, 1.0, 0.0)
        chosen = chosen.astype(BF16)
        for h in range(3):
            high, low = split(arrived_ref[:, 45 + h, :])
            grouped[h, 2304:2320, :] = nn(chosen, high) + nn(chosen, low)
            grouped[h, 2320:2560, :] = jnp.zeros((240, 128), F32)

    collect(nn(s_ref[...], src[...]), pl.multiple_of(step * 256, 256), 256)

    @pl.when(step == 7)
    def _():
        pltpu.make_async_copy(far_hbm, far_ref, sems.at[1]).wait()
        total = jnp.zeros((TARGETS, COEF), F32)
        for o in range(16):
            total = total + apply_operator(
                joined(grouped, pl.ds(o, TARGETS, stride=16)), far_ref[o]
            )
        wide[...] = jnp.zeros_like(wide)
        wide[:, :COEF] = total
        for h in range(3):
            locals_rows[h] = wide[0:128, 128 * h : 128 * h + 128]
        pltpu.make_async_copy(down_hbm, down_ref, sems.at[0]).wait()
        first = lax.rem(2 * dev_ref[0], 8)
        coarse = wide[144:145, :COEF]
        grand = jnp.concatenate(
            [apply_operator(coarse, down_ref[first]), apply_operator(coarse, down_ref[first + 1])],
            axis=0,
        )
        for c in range(8):
            rows = apply_operator(grand, down_ref[c])
            wide[128 + c : 129 + c, :COEF] = wide[128 + c : 129 + c, :COEF] + rows[0:1]
            wide[136 + c : 137 + c, :COEF] = wide[136 + c : 137 + c, :COEF] + rows[1:2]
        parents = wide[128:144, :COEF]
        for c in range(8):
            wide[0:16, :COEF] = apply_operator(parents, down_ref[c])
            for h in range(3):
                rows = pl.ds(c, 16, stride=8)
                locals_rows[h, rows, :] = (
                    locals_rows[h, rows, :] + wide[0:16, 128 * h : 128 * h + 128]
                )
        for h in range(3):
            loc[128 * h : 128 * h + 128, :] = locals_rows[h].T
        x_all, y_all, z_all = [2.0 * pos_ref[d].T for d in range(3)]
        for part in range(2):
            piece = slice(64 * part, 64 * part + 64)
            x, y, z = x_all[piece], y_all[piece], z_all[piece]
            over_i = None
            for i in range(ORDER, -1, -1):
                over_j = None
                for j in range(ORDER - i, -1, -1):
                    over_k = None
                    for k in range(ORDER - i - j, -1, -1):
                        a = INDEX[(i, j, k)]
                        value = loc[a : a + 1, :]
                        over_k = value if over_k is None else over_k * z + value
                    over_j = over_k if over_j is None else over_j * y + over_k
                over_i = over_j if over_i is None else over_i * x + over_j
            result[piece, :] = over_i
        out_ref[...] = near_ref[...] + result[...].T


def cost(flops, moved):
    return pl.CostEstimate(flops=flops, bytes_accessed=moved, transcendentals=0)


def shape(*dims, dtype=F32):
    return jax.ShapeDtypeStruct(dims, dtype)


def limits(mib):
    return pltpu.CompilerParams(vmem_limit_bytes=mib * 1024 * 1024)


def upward_call(dev, pos, chg, up_shift):
    return pl.pallas_call(
        upward_kernel,
        out_shape=(shape(3, 128, 128), shape(3, 16, 128), shape(3, 128)),
        in_specs=[SMEM, VMEM, VMEM, VMEM],
        out_specs=(VMEM, VMEM, VMEM),
        scratch_shapes=[pltpu.VMEM((384, 128), F32), pltpu.VMEM((16, 384), F32)],
        compiler_params=limits(40),
        cost_estimate=cost(10**9, 3 * 10**6),
        name="upward",
    )(dev, pos, chg, up_shift)


def pack_call(asked, lt, pt, lift):
    return pl.pallas_call(
        pack_kernel,
        out_shape=shape(128, ROWS, 128),
        in_specs=[VMEM] * 4,
        out_specs=VMEM,
        compiler_params=limits(40),
        cost_estimate=cost(10**9, 4 * 10**6),
        name="pack",
    )(asked, lt, pt, lift)


def near_call(code, count, selves, own, before, after):
    return pl.pallas_call(
        near_kernel,
        out_shape=shape(128, 128),
        in_specs=[SMEM, SMEM, SMEM, VMEM, VMEM, VMEM],
        out_specs=VMEM,
        scratch_shapes=[
            pltpu.VMEM((LEAF + 2 * RIM, 8, 128), F32),
            pltpu.VMEM((27, 8, 128), F32),
            pltpu.VMEM((LEAF + 2 * RIM, 128, 128), BF16),
            pltpu.VMEM((LEAF + 2 * RIM, 128, 128), F32),
            pltpu.VMEM((LEAF, 8, 128), F32),
            pltpu.VMEM((GROUP, 128, 128), F32),
            pltpu.VMEM((GROUP, 128, 128), F32),
            pltpu.SMEM((3 * GROUP,), jnp.int32),
            pltpu.SMEM((3 * GROUP,), jnp.int32),
        ],
        compiler_params=limits(40),
        cost_estimate=cost(30 * 10**9, 10**6),
        name="near",
    )(code, count, selves, own, before, after)


def counts_call(far_leaves, far_leaf_class, far_parents, far_parent_class):
    width = far_leaves.shape[1]
    blocks = lambda i: (i, 0)
    whole = lambda i: (0, 0)
    return pl.pallas_call(
        counts_kernel,
        grid=(8,),
        out_shape=(shape(2048, 2176, dtype=BF16), shape(256, 640, dtype=BF16)),
        in_specs=[
            pl.BlockSpec((16, width), blocks),
            pl.BlockSpec((16, width), blocks),
            pl.BlockSpec((16, width), whole),
            pl.BlockSpec((16, width), whole),
        ],
        out_specs=(pl.BlockSpec((256, 2176), blocks), pl.BlockSpec((256, 640), whole)),
        scratch_shapes=[pltpu.VMEM((16, 256), jnp.int32), pltpu.VMEM((16, 256), jnp.int32)],
        compiler_params=limits(40),
        cost_estimate=cost(10 * 10**9, 9 * 10**6),
        name="counts",
    )(far_leaves, far_leaf_class, far_parents, far_parent_class)


def far_call(dev, lists, classes, s, sp, lt, pt, arrived, pos, near, down_shift, far_shift):
    def whole(*dims):
        return pl.BlockSpec(dims, lambda i: (0,) * len(dims))

    hbm = pl.BlockSpec(memory_space=pl.ANY)
    return pl.pallas_call(
        far_kernel,
        grid=(8,),
        out_shape=shape(128, 128),
        in_specs=[
            SMEM, SMEM, SMEM,
            pl.BlockSpec((256, 2176), lambda i: (i, 0)),
            whole(256, 640), whole(3, 128, 128), whole(3, 16, 128), whole(128, ROWS, 128),
            whole(3, 128, 128), whole(128, 128), hbm, hbm,
        ],
        out_specs=whole(128, 128),
        scratch_shapes=[
            pltpu.VMEM((2176, 640), BF16),
            pltpu.VMEM((640, 640), BF16),
            pltpu.VMEM((3, 16 * TARGETS, 128), F32),
            pltpu.VMEM((3, 128, 128), F32),
            pltpu.VMEM((TARGETS, 384), F32),
            pltpu.VMEM((384, 128), F32),
            pltpu.VMEM((128, 128), F32),
            pltpu.VMEM((8, COEF, COEF), F32),
            pltpu.VMEM((16, COEF, COEF), F32),
            pltpu.SemaphoreType.DMA((2,)),
        ],
        compiler_params=limits(48),
        cost_estimate=cost(10 * 10**9, 20 * 10**6),
        name="far",
    )(dev, lists, classes, s, sp, lt, pt, arrived, pos, near, down_shift, far_shift)


def near_lists(near_leaves, near_offsets, first_leaf):
    leaves = near_leaves.shape[0]
    present = near_leaves >= 0
    own = first_leaf + jnp.arange(leaves, dtype=jnp.int32)[:, None]
    itself = (near_leaves == own) & (near_offsets == 13)
    code = (near_leaves - first_leaf + RIM) * 32 + near_offsets
    code = jnp.where(present & jnp.logical_not(itself), code, -1)
    code = jnp.concatenate([code.reshape(-1), jnp.full((32,), -1, jnp.int32)])
    count = jnp.maximum(jnp.sum(present.astype(jnp.int32), axis=1), 2)
    selves = jnp.sum(itself.astype(jnp.int32), axis=1)
    extra = jnp.stack([jnp.int32(1 << 30), jnp.sum(count - 1)])
    return code, jnp.concatenate([count, extra]), selves


def per_device(
    positions,
    charges,
    near_leaves,
    near_offsets,
    far_leaves,
    far_leaf_class,
    leaf_plan,
    far_parents,
    far_parent_class,
    parent_plan,
    coarse_lists,
    coarse_class,
    up_shift,
    down_shift,
    far_shift,
):
    device = lax.axis_index(AXES)
    dev = device.reshape(1).astype(jnp.int32)
    plans = jnp.concatenate([leaf_plan[0], parent_plan[0]], 1)
    asked = lax.all_to_all(plans, AXES, split_axis=0, concat_axis=0, tiled=True)
    pos = positions.reshape(3, LEAF, 128)
    chg = charges.reshape(LEAF, 128)
    own = jnp.concatenate([pos, chg[None]], 0)
    size = lax.axis_size(AXES)
    up = [(i, i + 1) for i in range(size - 1)]
    down = [(j, i) for i, j in up]
    before = lax.ppermute(own[:, LEAF - RIM :], AXES, up)
    after = lax.ppermute(own[:, :RIM], AXES, down)
    lt, pt, lift = upward_call(dev, pos, chg, up_shift)
    outgoing = pack_call(asked, lt, pt, lift)
    arrived = lax.all_to_all(outgoing, AXES, split_axis=0, concat_axis=0, tiled=True)
    code, count, selves = near_lists(near_leaves, near_offsets, device * LEAF)
    near = near_call(code, count, selves, own, before, after)
    s, sp = counts_call(far_leaves, far_leaf_class, far_parents, far_parent_class)
    potential = far_call(
        dev, coarse_lists.reshape(-1), coarse_class.reshape(-1), s, sp, lt, pt, arrived, pos, near,
        down_shift, far_shift,
    )
    return potential.reshape(-1)


def solution(mesh):
    row = P(AXES, None)
    placed = (
        P(None, AXES), P(AXES), row, row, row, row, P(AXES, None, None), row, row,
        P(AXES, None, None), P(), P(), P(), P(), P(),
    )
    return jax.shard_map(
        per_device, mesh=mesh, in_specs=placed, out_specs=P(AXES), check_vma=False
    )
```

```python
import jax
import jax.numpy as jnp
import numpy as np
from jax import lax
from jax.experimental import pallas as pl
from jax.experimental.pallas import tpu as pltpu
from jax.sharding import PartitionSpec as P

ORDER = 10
COEF = 286
RIM = 32
LEAF = 128
K_NEAR = 27
CAP_L = 16
CAP_P = 4
ROWS = 48
TARGETS = 160
GROUP = 64
NOBODY = LEAF + 2 * RIM
SOFT = 0.05 * 0.05
AXES = ("gx", "gy")
F32 = jnp.float32
BF16 = jnp.bfloat16
VMEM = pl.BlockSpec(memory_space=pltpu.VMEM)
SMEM = pl.BlockSpec(memory_space=pltpu.SMEM)


def exponents(order):
    entries = []
    for degree in range(order + 1):
        for first_power in range(degree, -1, -1):
            for second_power in range(degree - first_power, -1, -1):
                entries.append((first_power, second_power, degree - first_power - second_power))
    return entries


INDEX = {powers: number for number, powers in enumerate(exponents(ORDER))}


def split(x):
    high = x.astype(BF16)
    return high, (x - high.astype(F32)).astype(BF16)


def nt(a, b):
    return lax.dot_general(a, b, (((1,), (1,)), ((), ())), preferred_element_type=F32)


def nn(a, b):
    return jnp.dot(a, b, preferred_element_type=F32)


def apply_operator(rows, operator):
    row_high, row_low = split(rows)
    high, low = split(operator)
    return nt(row_high, high) + (nt(row_low, high) + nt(row_high, low))


def fetches(source, chunks, tail, sems, first):
    return [
        pltpu.make_async_copy(source.at[:, 0:128], chunks.at[0], sems.at[first]),
        pltpu.make_async_copy(source.at[:, 128:256], chunks.at[1], sems.at[first + 1]),
        pltpu.make_async_copy(source.at[:, 256:COEF], tail, sems.at[first + 2]),
    ]


def arrive(copies, chunks, tail):
    for copy in copies:
        copy.wait()
    chunks[2, :, 0 : COEF - 256] = tail[...]


def operator_at(chunks, number, count):
    rows = pl.ds(number, COEF, stride=count)
    return jnp.concatenate([chunks[h, rows, :] for h in range(3)], axis=1)[:, :COEF]


def joined(ref, rows):
    return jnp.concatenate([ref[h, rows, :] for h in range(3)], axis=1)[:, :COEF]


def upward_kernel(dev_ref, pos_ref, chg_ref, up_hbm, lt_ref, pt_ref, lift_ref, moments, wide, up_ref,
                  up_tail, sems):
    copies = fetches(up_hbm, up_ref, up_tail, sems, 0)
    for copy in copies:
        copy.start()
    x, y, z = [2.0 * pos_ref[d].T for d in range(3)]
    with_x = chg_ref[...].T
    z_powers = [None, z]
    for k in range(ORDER - 1):
        z_powers.append(z_powers[-1] * z)
    moments[COEF - 6 : 384, :] = jnp.zeros((384 - COEF + 6, LEAF), F32)
    for i in range(ORDER + 1):
        if i:
            with_x = with_x * x
        with_xy = with_x
        for j in range(ORDER + 1 - i):
            if j:
                with_xy = with_xy * y
            for k in range(ORDER + 1 - i - j):
                term = with_xy * z_powers[k] if k else with_xy
                a = INDEX[(i, j, k)]
                moments[a : a + 1, :] = jnp.sum(term, axis=0, keepdims=True)
    for h in range(3):
        lt_ref[h] = moments[128 * h : 128 * h + 128, :].T
    wide[...] = jnp.zeros_like(wide)
    arrive(copies, up_ref, up_tail)
    total = jnp.zeros((16, COEF), F32)
    for c in range(8):
        total = total + apply_operator(joined(lt_ref, pl.ds(c, 16, stride=8)), operator_at(up_ref, c, 8))
    wide[:, :COEF] = total
    for h in range(3):
        pt_ref[h] = wide[:, 128 * h : 128 * h + 128]
    grand = jnp.zeros((2, COEF), F32)
    for c in range(8):
        rows = jnp.concatenate([wide[c : c + 1, :COEF], wide[8 + c : 9 + c, :COEF]], axis=0)
        grand = grand + apply_operator(rows, operator_at(up_ref, c, 8))
    first = lax.rem(2 * dev_ref[0], 8)
    lifted = apply_operator(grand[0:1], operator_at(up_ref, first, 8)) + apply_operator(grand[1:2], operator_at(up_ref, first + 1, 8))
    wide[0:1, :COEF] = lifted
    for h in range(3):
        lift_ref[h : h + 1, :] = wide[0:1, 128 * h : 128 * h + 128]


def pack_kernel(asked_ref, lt_ref, pt_ref, lift_ref, out_ref):
    lane = lax.broadcasted_iota(jnp.int32, (128, 128), 1)
    leaf_rows = jnp.concatenate([lt_ref[h] for h in range(3)], axis=1)
    parent_rows = jnp.concatenate([pt_ref[h] for h in range(3)], axis=1)
    parent_rows = jnp.concatenate([parent_rows, jnp.zeros((112, 384), F32)], axis=0)
    leaf_rows = jnp.concatenate(split(leaf_rows), axis=0)
    parent_rows = jnp.concatenate(split(parent_rows), axis=0)
    for q in range(5):
        tail = jnp.zeros((128, 128), F32)
        for p in range(4):
            j = 4 * q + p
            chosen = jnp.where(asked_ref[:, j : j + 1] == lane, 1.0, 0.0).astype(BF16)
            chosen = jnp.concatenate([chosen, chosen], axis=1)
            rows = nn(chosen, leaf_rows if q < 4 else parent_rows)
            out_ref[pl.ds(2 * j, 128, stride=ROWS), :] = rows[:, 0:128]
            out_ref[pl.ds(2 * j + 1, 128, stride=ROWS), :] = rows[:, 128:256]
            part = rows[:, 256:384]
            tail = tail + (pltpu.roll(part, 32 * p, 1) if p else part)
        out_ref[pl.ds(40 + q, 128, stride=ROWS), :] = tail
    for h in range(3):
        out_ref[pl.ds(45 + h, 128, stride=ROWS), :] = jnp.broadcast_to(lift_ref[h : h + 1, :], (128, 128))


def near_kernel(dev_ref, leaves_ref, offsets_ref, pos_ref, chg_ref, before_ref, after_ref, out_ref,
                eight, charge, offsets, features, spread, sums, ready, lists, plan, sem):
    sub = lax.broadcasted_iota(jnp.int32, (8, 128), 0)
    named = leaves_ref[...]
    first_leaf = dev_ref[0] * LEAF
    present = named >= 0
    own_id = first_leaf + lax.broadcasted_iota(jnp.int32, (K_NEAR, LEAF), 1)
    itself = (named == own_id) & (offsets_ref[...] == 13)
    counted = present & jnp.logical_not(itself)
    code = jnp.where(counted, (named - first_leaf + RIM) * 32 + offsets_ref[...], NOBODY * 32 + 13)
    count = jnp.sum(jnp.where(present, 1.0, 0.0), axis=0, keepdims=True).astype(jnp.int32)
    quads = jnp.maximum((count + 2) // 4, 1)
    selves = jnp.sum(jnp.where(itself, 1.0, 0.0), axis=0, keepdims=True).astype(jnp.int32)
    total = jnp.sum(quads.astype(F32), axis=1, keepdims=True).astype(jnp.int32)
    lists[...] = jnp.full_like(lists, NOBODY * 32 + 13)
    lists[0:K_NEAR, :] = code
    lists[37:38, :] = quads
    lists[38:39, :] = selves
    lists[39:40, :] = jnp.broadcast_to(total, (1, 128))
    copy = pltpu.make_async_copy(lists, plan, sem)
    copy.start()
    eight[:, 3, :] = jnp.full((LEAF + 2 * RIM, 128), 1.0, F32)
    eight[:, 7, :] = jnp.full((LEAF + 2 * RIM, 128), SOFT, F32)
    eight3 = ((0, 4), (1, 5), (2, 6))
    for d in range(3):
        for row in eight3[d]:
            eight[0:RIM, row, :] = before_ref[d]
            eight[RIM : RIM + LEAF, row, :] = pos_ref[d]
            eight[RIM + LEAF : 2 * RIM + LEAF, row, :] = after_ref[d]
    charge[0:RIM, :] = before_ref[3]
    charge[RIM : RIM + LEAF, :] = chg_ref[...]
    charge[RIM + LEAF : 2 * RIM + LEAF, :] = after_ref[3]
    lane = lax.broadcasted_iota(jnp.int32, (128, 128), 1)
    features[NOBODY] = jnp.where(lane == 7, 1.0, 0.0).astype(BF16)
    spread[NOBODY] = jnp.zeros((128, 128), F32)
    for o in range(27):
        shift = (o // 9 - 1, o // 3 % 3 - 1, o % 3 - 1)
        table = jnp.zeros((8, 128), F32)
        for d in range(3):
            table = jnp.where((sub == d) | (sub == d + 4), -float(shift[d]), table)
        offsets[o] = table
    squares = (sub >= 4) & (sub < 7)

    def thirds(v):
        high = v.astype(BF16).astype(F32)
        rest = v - high
        middle = rest.astype(BF16).astype(F32)
        return high, middle, rest - middle

    def target(leaf, offset):
        v = eight[RIM + leaf] + offsets[offset]
        v = jnp.where(squares, v * v, v)
        high, middle, low = thirds(v)
        return jnp.concatenate([high, high, high, middle, middle, low], axis=0).astype(BF16)

    def separations(leaf, rows):
        padded = jnp.concatenate([rows, jnp.zeros((80, 128), BF16)], axis=0)
        return nn(features[leaf], padded)

    row = lax.broadcasted_iota(jnp.int32, (128, 128), 0)
    three = jnp.where((row >= 48) & (row < 51), 1.0, 0.0).astype(BF16)
    diagonal = row == lane
    identity = jnp.where(diagonal, 1.0, 0.0).astype(BF16)

    def source(leaf):
        v = eight[leaf]
        norm = jnp.sum(jnp.where(sub < 3, v * v, 0.0), axis=0, keepdims=True)
        v = jnp.where(sub < 3, -2.0 * v, jnp.where(sub == 3, norm, 1.0))
        high, middle, low = thirds(v)
        first, second, third = thirds(charge[pl.ds(leaf, 1), :])
        parts = jnp.where(sub == 0, first, jnp.where(sub == 1, second, jnp.where(sub == 2, third, 0.0)))
        rows = jnp.concatenate([high, middle, low, high, middle, high, parts], axis=0)
        rows = jnp.concatenate([rows, jnp.zeros((72, 128), F32)], axis=0)
        rows = rows.T.astype(BF16)
        features[leaf] = rows
        spread[leaf] = nn(rows, three)

    def prepare(step, carry):
        for u in range(16):
            source(16 * step + u)
        return carry

    lax.fori_loop(0, (LEAF + 2 * RIM) // 16, prepare, 0)
    copy.wait()

    def own_leaf(step, carry):
        for u in range(16):
            leaf = 16 * step + u
            squared = separations(RIM + leaf, target(leaf, 13))
            terms = jnp.where(diagonal, 0.0, spread[RIM + leaf] * lax.rsqrt(squared))
            sums[leaf] = jnp.sum(terms.reshape(16, 8, 128), axis=0) * plan[38, leaf].astype(F32)
        return carry

    lax.fori_loop(0, LEAF // 16, own_leaf, 0)

    def advance(state):
        leaf, quad = state
        last = quad + 1 >= plan[37, leaf]
        return (
            jnp.where(last, jnp.minimum(leaf + 1, LEAF - 1), leaf),
            jnp.where(last, jnp.where(leaf == LEAF - 1, 7, 0), quad + 1),
        )

    def produce(states):
        for g, (leaf, quad) in enumerate(states):
            for u in range(4):
                code = plan[4 * quad + u + 1, leaf]
                ready[4 * g + u] = target(leaf, code & 31)

    def consume(states):
        for g, (leaf, quad) in enumerate(states):
            part = sums[leaf]
            for u in range(4):
                code = plan[4 * quad + u + 1, leaf]
                squared = separations(code >> 5, ready[4 * g + u])
                terms = spread[code >> 5] * lax.rsqrt(squared)
                part = part + jnp.sum(terms.reshape(16, 8, 128), axis=0)
            sums[leaf] = part

    def following(state, number):
        made = []
        for _ in range(number):
            state = advance(state)
            made.append(state)
        return tuple(made)

    first = (jnp.int32(0), jnp.int32(0))
    states = (first,) + following(first, GROUP // 4 - 1)
    produce(states)

    def one_group(step, states):
        after = following(states[-1], GROUP // 4)
        consume(states)
        produce(after)
        return after

    quads = GROUP // 4
    lax.fori_loop(0, (plan[39, 0] + quads - 1) // quads, one_group, states)
    out_ref[...] = jnp.sum(sums[...], axis=1)


def count_rows(code, low, rows):
    wide = lax.broadcasted_iota(jnp.int32, (rows, 256), 0) == code
    narrow = lax.broadcasted_iota(jnp.int32, (128, 256), 0) == low
    return nt(
        jnp.where(wide, 1.0, 0.0).astype(BF16), jnp.where(narrow, 1.0, 0.0).astype(BF16)
    ).astype(BF16)


def counts_kernel(leaf_ref, leaf_class_ref, parent_ref, parent_class_ref, s_ref, sp_ref,
                  code_scr, low_scr, turned):
    step = pl.program_id(0)

    def encode(slots, classes, cells, capacity):
        ghost = jnp.maximum(slots - cells, 0)
        own = slots < cells
        code = jnp.where(own, 0, 1 + lax.rem(ghost, capacity)) * 16 + classes
        return jnp.where(slots < 0, -1, code), jnp.where(own, slots, lax.div(ghost, capacity))

    def tables(first, capacity, out_ref):
        blocks = capacity + 1
        for t in range(16):
            rows = pl.ds(first + t, 1)
            table = count_rows(code_scr[rows, :], low_scr[rows, :], 16 * blocks)
            for b in range(blocks):
                out_ref[16 * t : 16 * t + 16, 128 * b : 128 * b + 128] = table[16 * b : 16 * b + 16]

    @pl.when(step == 0)
    def _():
        width = leaf_ref.shape[0]
        code_scr[...] = jnp.full_like(code_scr, -1)
        low_scr[...] = jnp.full_like(low_scr, -1)
        for part, scratch in zip(
            encode(leaf_ref[...], leaf_class_ref[...], LEAF, CAP_L), (code_scr, low_scr)
        ):
            turned[...] = jnp.full_like(turned, -1.0)
            turned[:width, :] = part.astype(F32)
            scratch[0:128, 0:128] = turned[0:128, :].T.astype(jnp.int32)
            scratch[0:128, 128:256] = turned[128:256, :].T.astype(jnp.int32)
        for part, scratch in zip(
            encode(parent_ref[...], parent_class_ref[...], 16, CAP_P), (code_scr, low_scr)
        ):
            scratch[128:144, :width] = part
        tables(128, CAP_P, sp_ref)

    tables(pl.multiple_of(16 * step, 16), CAP_L, s_ref)


def far_kernel(dev_ref, lists_ref, class_ref, s_ref, sp_ref, lt_ref, pt_ref, arrived_ref, pos_ref,
               near_ref, down_hbm, far_hbm, out_ref,
               src, src_parent, grouped, locals_rows, wide, loc, result, down_ref, down_tail, far_ref, far_tail, sems):
    step = pl.program_id(0)
    far_copies = fetches(far_hbm, far_ref, far_tail, sems, 0)
    down_copies = fetches(down_hbm, down_ref, down_tail, sems, 3)
    lane = lax.broadcasted_iota(jnp.int32, (128, 128), 1)

    def place(ref, row, parts):
        count = parts[0].shape[0]
        (h0, l0), (h1, l1) = split(parts[0]), split(parts[1])
        tail = parts[2]
        high = tail.astype(BF16).astype(F32)
        low = pltpu.roll(tail - high, 32, 1)
        ref[row : row + count, 0:128] = h0
        ref[row : row + count, 128:256] = h1
        ref[row : row + count, 256:384] = l0
        ref[row : row + count, 384:512] = l1
        ref[row : row + count, 512:640] = (high + low).astype(BF16)

    def collect(product, row, count):
        grouped[0, pl.ds(row, count), :] = product[:, 0:128] + product[:, 256:384]
        grouped[1, pl.ds(row, count), :] = product[:, 128:256] + product[:, 384:512]
        tail = product[:, 512:640]
        grouped[2, pl.ds(row, count), :] = tail + pltpu.roll(tail, 96, 1)

    def arrived_tail(row, p):
        part = arrived_ref[pl.ds(row, 128, stride=ROWS), :]
        part = pltpu.roll(part, 128 - 32 * p, 1) if p else part
        return jnp.where(lane < 32, part, 0.0)

    @pl.when(step == 0)
    def _():
        for copy in far_copies + down_copies:
            copy.start()
        place(src, 0, [lt_ref[h] for h in range(3)])
        for c in range(CAP_L):
            place(
                src,
                128 * (c + 1),
                [arrived_ref[pl.ds(2 * c, 128, stride=ROWS), :], arrived_ref[pl.ds(2 * c + 1, 128, stride=ROWS), :], arrived_tail(40 + c // 4, c % 4)],
            )
        own = [jnp.concatenate([pt_ref[h], jnp.zeros((112, 128), F32)], axis=0) for h in range(3)]
        place(src_parent, 0, own)
        for c in range(CAP_P):
            place(
                src_parent,
                128 * (c + 1),
                [arrived_ref[pl.ds(32 + 2 * c, 128, stride=ROWS), :], arrived_ref[pl.ds(33 + 2 * c, 128, stride=ROWS), :], arrived_tail(44, c)],
            )
        collect(nn(sp_ref[...], src_parent[...]), 2048, 256)
        mine = dev_ref[0] // 4
        operator = lax.broadcasted_iota(jnp.int32, (16, 128), 0)
        cell = lax.broadcasted_iota(jnp.int32, (16, 128), 1) // 4
        chosen = jnp.zeros((16, 128), F32)
        for k in range(7):
            hit = (operator == class_ref[mine * 7 + k]) & (cell == lists_ref[mine * 7 + k])
            chosen = chosen + jnp.where(hit, 1.0, 0.0)
        chosen = chosen.astype(BF16)
        for h in range(3):
            high, low = split(arrived_ref[pl.ds(45 + h, 128, stride=ROWS), :])
            grouped[h, 2304:2320, :] = nn(chosen, high) + nn(chosen, low)
            grouped[h, 2320:2560, :] = jnp.zeros((240, 128), F32)

    collect(nn(s_ref[...], src[...]), pl.multiple_of(step * 256, 256), 256)

    @pl.when(step == 7)
    def _():
        arrive(far_copies, far_ref, far_tail)
        total = jnp.zeros((TARGETS, COEF), F32)
        for o in range(16):
            total = total + apply_operator(
                joined(grouped, pl.ds(o, TARGETS, stride=16)), operator_at(far_ref, o, 16)
            )
        wide[...] = jnp.zeros_like(wide)
        wide[:, :COEF] = total
        for h in range(3):
            locals_rows[h] = wide[0:128, 128 * h : 128 * h + 128]
        arrive(down_copies, down_ref, down_tail)
        first = lax.rem(2 * dev_ref[0], 8)
        coarse = wide[144:145, :COEF]
        grand = jnp.concatenate(
            [apply_operator(coarse, operator_at(down_ref, first, 8)), apply_operator(coarse, operator_at(down_ref, first + 1, 8))],
            axis=0,
        )
        for c in range(8):
            rows = apply_operator(grand, operator_at(down_ref, c, 8))
            wide[128 + c : 129 + c, :COEF] = wide[128 + c : 129 + c, :COEF] + rows[0:1]
            wide[136 + c : 137 + c, :COEF] = wide[136 + c : 137 + c, :COEF] + rows[1:2]
        parents = wide[128:144, :COEF]
        for c in range(8):
            wide[0:16, :COEF] = apply_operator(parents, operator_at(down_ref, c, 8))
            for h in range(3):
                rows = pl.ds(c, 16, stride=8)
                locals_rows[h, rows, :] = (
                    locals_rows[h, rows, :] + wide[0:16, 128 * h : 128 * h + 128]
                )
        for h in range(3):
            loc[128 * h : 128 * h + 128, :] = locals_rows[h].T
        x_all, y_all, z_all = [2.0 * pos_ref[d].T for d in range(3)]
        for part in range(2):
            piece = slice(64 * part, 64 * part + 64)
            x, y, z = x_all[piece], y_all[piece], z_all[piece]
            over_i = None
            for i in range(ORDER, -1, -1):
                over_j = None
                for j in range(ORDER - i, -1, -1):
                    over_k = None
                    for k in range(ORDER - i - j, -1, -1):
                        a = INDEX[(i, j, k)]
                        value = loc[a : a + 1, :]
                        over_k = value if over_k is None else over_k * z + value
                    over_j = over_k if over_j is None else over_j * y + over_k
                over_i = over_j if over_i is None else over_i * x + over_j
            result[piece, :] = over_i
        out_ref[...] = near_ref[...] + result[...].T


def cost(flops, moved):
    return pl.CostEstimate(flops=flops, bytes_accessed=moved, transcendentals=0)


def shape(*dims, dtype=F32):
    return jax.ShapeDtypeStruct(dims, dtype)


def limits(mib):
    return pltpu.CompilerParams(vmem_limit_bytes=mib * 1024 * 1024)


def upward_call(dev, pos, chg, up_shift):
    return pl.pallas_call(
        upward_kernel,
        out_shape=(shape(3, 128, 128), shape(3, 16, 128), shape(3, 128)),
        in_specs=[SMEM, VMEM, VMEM, pl.BlockSpec(memory_space=pl.ANY)],
        out_specs=(VMEM, VMEM, VMEM),
        scratch_shapes=[
            pltpu.VMEM((384, 128), F32),
            pltpu.VMEM((16, 384), F32),
            pltpu.VMEM((3, 8 * COEF, 128), F32),
            pltpu.VMEM((8 * COEF, COEF - 256), F32),
            pltpu.SemaphoreType.DMA((3,)),
        ],
        compiler_params=limits(40),
        cost_estimate=cost(10**9, 3 * 10**6),
        name="upward",
    )(dev, pos, chg, up_shift)


def pack_call(asked, lt, pt, lift):
    return pl.pallas_call(
        pack_kernel,
        out_shape=shape(128 * ROWS, 128),
        in_specs=[VMEM] * 4,
        out_specs=VMEM,
        compiler_params=limits(40),
        cost_estimate=cost(10**9, 4 * 10**6),
        name="pack",
    )(asked, lt, pt, lift)


def near_call(dev, near_leaves, near_offsets, pos, chg, before, after):
    return pl.pallas_call(
        near_kernel,
        out_shape=shape(128, 128),
        in_specs=[SMEM] + [VMEM] * 6,
        out_specs=VMEM,
        scratch_shapes=[
            pltpu.VMEM((LEAF + 2 * RIM, 8, 128), F32),
            pltpu.VMEM((LEAF + 2 * RIM, 128), F32),
            pltpu.VMEM((27, 8, 128), F32),
            pltpu.VMEM((NOBODY + 1, 128, 128), BF16),
            pltpu.VMEM((NOBODY + 1, 128, 128), F32),
            pltpu.VMEM((LEAF, 8, 128), F32),
            pltpu.VMEM((GROUP, 48, 128), BF16),
            pltpu.VMEM((40, 128), jnp.int32),
            pltpu.SMEM((40, 128), jnp.int32),
            pltpu.SemaphoreType.DMA(()),
        ],
        compiler_params=limits(40),
        cost_estimate=cost(30 * 10**9, 10**6),
        name="near",
    )(dev, near_leaves, near_offsets, pos, chg, before, after)


def counts_call(far_leaves, far_leaf_class, far_parents, far_parent_class):
    width = far_leaves.shape[0]
    blocks = lambda i: (i, 0)
    whole = lambda i: (0, 0)
    return pl.pallas_call(
        counts_kernel,
        grid=(8,),
        out_shape=(shape(2048, 2176, dtype=BF16), shape(256, 640, dtype=BF16)),
        in_specs=[
            pl.BlockSpec((width, 128), whole),
            pl.BlockSpec((width, 128), whole),
            pl.BlockSpec((16, width), whole),
            pl.BlockSpec((16, width), whole),
        ],
        out_specs=(pl.BlockSpec((256, 2176), blocks), pl.BlockSpec((256, 640), whole)),
        scratch_shapes=[
            pltpu.VMEM((144, 256), jnp.int32),
            pltpu.VMEM((144, 256), jnp.int32),
            pltpu.VMEM((256, 128), F32),
        ],
        compiler_params=limits(40),
        cost_estimate=cost(10 * 10**9, 9 * 10**6),
        name="counts",
    )(far_leaves, far_leaf_class, far_parents, far_parent_class)


def far_call(dev, lists, classes, s, sp, lt, pt, arrived, pos, near, down_shift, far_shift):
    def whole(*dims):
        return pl.BlockSpec(dims, lambda i: (0,) * len(dims))

    hbm = pl.BlockSpec(memory_space=pl.ANY)
    return pl.pallas_call(
        far_kernel,
        grid=(8,),
        out_shape=shape(128, 128),
        in_specs=[
            SMEM, SMEM, SMEM,
            pl.BlockSpec((256, 2176), lambda i: (i, 0)),
            whole(256, 640), whole(3, 128, 128), whole(3, 16, 128), whole(128 * ROWS, 128),
            whole(3, 128, 128), whole(128, 128), hbm, hbm,
        ],
        out_specs=whole(128, 128),
        scratch_shapes=[
            pltpu.VMEM((2176, 640), BF16),
            pltpu.VMEM((640, 640), BF16),
            pltpu.VMEM((3, 16 * TARGETS, 128), F32),
            pltpu.VMEM((3, 128, 128), F32),
            pltpu.VMEM((TARGETS, 384), F32),
            pltpu.VMEM((384, 128), F32),
            pltpu.VMEM((128, 128), F32),
            pltpu.VMEM((3, 8 * COEF, 128), F32),
            pltpu.VMEM((8 * COEF, COEF - 256), F32),
            pltpu.VMEM((3, 16 * COEF, 128), F32),
            pltpu.VMEM((16 * COEF, COEF - 256), F32),
            pltpu.SemaphoreType.DMA((6,)),
        ],
        compiler_params=limits(48),
        cost_estimate=cost(10 * 10**9, 20 * 10**6),
        name="far",
    )(dev, lists, classes, s, sp, lt, pt, arrived, pos, near, down_shift, far_shift)


def by_rows(operators):
    return jnp.swapaxes(operators, 0, 1).reshape(-1, operators.shape[2])


def per_device(
    positions,
    charges,
    near_leaves,
    near_offsets,
    far_leaves,
    far_leaf_class,
    leaf_plan,
    far_parents,
    far_parent_class,
    parent_plan,
    coarse_lists,
    coarse_class,
    up_shift,
    down_shift,
    far_shift,
):
    device = lax.axis_index(AXES)
    dev = device.reshape(1).astype(jnp.int32)
    plans = jnp.concatenate([leaf_plan[0], parent_plan[0]], 1)
    asked = lax.all_to_all(plans, AXES, split_axis=0, concat_axis=0, tiled=True)
    pos = positions.reshape(3, LEAF, 128)
    chg = charges.reshape(LEAF, 128)
    own = jnp.concatenate([pos, chg[None]], 0)
    size = lax.axis_size(AXES)
    up = [(i, i + 1) for i in range(size - 1)]
    down = [(j, i) for i, j in up]
    before = lax.ppermute(own[:, LEAF - RIM :], AXES, up)
    after = lax.ppermute(own[:, :RIM], AXES, down)
    lt, pt, lift = upward_call(dev, pos, chg, by_rows(up_shift))
    outgoing = pack_call(asked, lt, pt, lift).reshape(LEAF, ROWS, 128)
    arrived = lax.all_to_all(outgoing, AXES, split_axis=0, concat_axis=0, tiled=True)
    arrived = arrived.reshape(LEAF * ROWS, 128)
    near = near_call(dev, near_leaves.T, near_offsets.T, pos, chg, before, after)
    s, sp = counts_call(far_leaves.T, far_leaf_class.T, far_parents, far_parent_class)
    potential = far_call(
        dev, coarse_lists.reshape(-1), coarse_class.reshape(-1), s, sp, lt, pt, arrived, pos, near,
        by_rows(down_shift), by_rows(far_shift),
    )
    return potential.reshape(-1)


def solution(mesh):
    row = P(AXES, None)
    placed = (
        P(None, AXES), P(AXES), row, row, row, row, P(AXES, None, None), row, row,
        P(AXES, None, None), P(), P(), P(), P(), P(),
    )
    return jax.shard_map(
        per_device, mesh=mesh, in_specs=placed, out_specs=P(AXES), check_vma=False
    )
```

```python
import jax
import jax.numpy as jnp
import numpy as np
from jax import lax
from jax.experimental import pallas as pl
from jax.experimental.pallas import tpu as pltpu
from jax.sharding import PartitionSpec as P

ORDER = 10
COEF = 286
RIM = 32
LEAF = 128
K_NEAR = 27
CAP_L = 16
CAP_P = 4
ROWS = 48
PLAN = 24
TARGETS = 160
GROUP = 64
NOBODY = LEAF + 2 * RIM
SOFT = 0.05 * 0.05
AXES = ("gx", "gy")
F32 = jnp.float32
BF16 = jnp.bfloat16
VMEM = pl.BlockSpec(memory_space=pltpu.VMEM)
SMEM = pl.BlockSpec(memory_space=pltpu.SMEM)


def exponents(order):
    entries = []
    for degree in range(order + 1):
        for first_power in range(degree, -1, -1):
            for second_power in range(degree - first_power, -1, -1):
                entries.append((first_power, second_power, degree - first_power - second_power))
    return entries


INDEX = {powers: number for number, powers in enumerate(exponents(ORDER))}


def split(x):
    high = x.astype(BF16)
    return high, (x - high.astype(F32)).astype(BF16)


def nt(a, b):
    return lax.dot_general(a, b, (((1,), (1,)), ((), ())), preferred_element_type=F32)


def nn(a, b):
    return jnp.dot(a, b, preferred_element_type=F32)


def turn(x, left):
    return pltpu.roll(x, 128 - left, 1)


def apply_parts(operator, high, low):
    operator_high, operator_low = split(operator)
    both = nn(operator_high, jnp.concatenate([high, low], axis=1))
    return both[:, 0:128] + (both[:, 128:256] + nn(operator_low, high))


def apply_operator(operator, columns):
    return apply_parts(operator, *split(columns))


def cut(source, chunks):
    chunks[0] = source[:, 0:128]
    chunks[1] = source[:, 128:256]
    chunks[2] = jnp.zeros(chunks.shape[1:], F32)
    chunks[2, :, 0 : COEF - 256] = source[:, 256:COEF]


def operator_at(chunks, number, count):
    rows = pl.ds(number, COEF, stride=count)
    return jnp.concatenate([chunks[h, rows, :] for h in range(3)], axis=1)


def upward_kernel(dev_ref, pos_ref, chg_ref, stored_up, lt_ref, pt_ref, lift_ref, moments, column,
                  up_ref):
    x, y, z = [2.0 * pos_ref[d].T for d in range(3)]
    with_x = chg_ref[...].T
    z_powers = [None, z]
    for k in range(ORDER - 1):
        z_powers.append(z_powers[-1] * z)
    moments[COEF - 6 : 384, :] = jnp.zeros((384 - COEF + 6, LEAF), F32)
    for i in range(ORDER + 1):
        if i:
            with_x = with_x * x
        with_xy = with_x
        for j in range(ORDER + 1 - i):
            if j:
                with_xy = with_xy * y
            for k in range(ORDER + 1 - i - j):
                term = with_xy * z_powers[k] if k else with_xy
                a = INDEX[(i, j, k)]
                moments[a : a + 1, :] = jnp.sum(term, axis=0, keepdims=True)
    for h in range(3):
        lt_ref[h] = moments[128 * h : 128 * h + 128, :].T
    column[...] = jnp.zeros_like(column)
    cut(stored_up, up_ref)
    lane = lax.broadcasted_iota(jnp.int32, (384, 128), 1)
    leaves = moments[...]
    total = jnp.zeros((COEF, 128), F32)
    for c in range(8):
        total = total + apply_operator(
            operator_at(up_ref, c, 8), jnp.where(lane % 8 == c, leaves, 0.0)
        )
    for left in (4, 2, 1):
        total = total + turn(total, left)
    column[0:COEF, :] = total
    parents = column[...]
    total = jnp.zeros((COEF, 128), F32)
    for c in range(8):
        total = total + apply_operator(
            operator_at(up_ref, c, 8), jnp.where(lane % 64 == 8 * c, parents, 0.0)
        )
    for h in range(3):
        moments[0:128, :] = column[128 * h : 128 * h + 128, :].T
        pt_ref[h] = moments[pl.ds(0, 16, stride=8), :]
    for left in (8, 16, 32):
        total = total + turn(total, left)
    column[0:COEF, :] = total
    grand = column[...]
    first = lax.rem(2 * dev_ref[0], 8)
    total = apply_operator(operator_at(up_ref, first, 8), jnp.where(lane == 0, grand, 0.0))
    total = total + apply_operator(
        operator_at(up_ref, first + 1, 8), jnp.where(lane == 64, grand, 0.0)
    )
    column[0:COEF, :] = total + turn(total, 64)
    for h in range(3):
        lift_ref[h : h + 1, :] = column[128 * h : 128 * h + 128, :].T[0:1, :]


def pack_kernel(dev_ref, asked_ref, lt_ref, pt_ref, lift_ref, out_ref):
    lane = lax.broadcasted_iota(jnp.int32, (128, 128), 1)
    leaf_rows = jnp.concatenate([lt_ref[h] for h in range(3)], axis=1)
    parent_rows = jnp.concatenate([pt_ref[h] for h in range(3)], axis=1)
    parent_rows = jnp.concatenate([parent_rows, jnp.zeros((112, 384), F32)], axis=0)
    leaf_rows = jnp.concatenate(split(leaf_rows), axis=0)
    parent_rows = jnp.concatenate(split(parent_rows), axis=0)
    for q in range(5):
        tail = jnp.zeros((128, 128), F32)
        for p in range(4):
            j = 4 * q + p
            asked = asked_ref[pl.ds(j, 128, stride=PLAN), :]
            asked = jnp.where(lane == dev_ref[0], asked.astype(F32), 0.0)
            asked = jnp.sum(asked, axis=1, keepdims=True)
            chosen = jnp.where(asked == lane.astype(F32), 1.0, 0.0).astype(BF16)
            chosen = jnp.concatenate([chosen, chosen], axis=1)
            rows = nn(chosen, leaf_rows if q < 4 else parent_rows)
            out_ref[pl.ds(2 * j, 128, stride=ROWS), :] = rows[:, 0:128]
            out_ref[pl.ds(2 * j + 1, 128, stride=ROWS), :] = rows[:, 128:256]
            part = rows[:, 256:384]
            tail = tail + (pltpu.roll(part, 32 * p, 1) if p else part)
        out_ref[pl.ds(40 + q, 128, stride=ROWS), :] = tail
    for h in range(3):
        out_ref[pl.ds(45 + h, 128, stride=ROWS), :] = jnp.broadcast_to(lift_ref[h : h + 1, :], (128, 128))


def near_kernel(dev_ref, leaves_ref, offsets_ref, pos_ref, chg_ref, before_ref, after_ref, out_ref,
                eight, charge, offsets, features, spread, sums, ready, lists, plan, sem):
    sub = lax.broadcasted_iota(jnp.int32, (8, 128), 0)
    named = leaves_ref[...]
    first_leaf = dev_ref[0] * LEAF
    present = named >= 0
    own_id = first_leaf + lax.broadcasted_iota(jnp.int32, (K_NEAR, LEAF), 1)
    itself = (named == own_id) & (offsets_ref[...] == 13)
    counted = present & jnp.logical_not(itself)
    code = jnp.where(counted, (named - first_leaf + RIM) * 32 + offsets_ref[...], NOBODY * 32 + 13)
    count = jnp.sum(jnp.where(present, 1.0, 0.0), axis=0, keepdims=True).astype(jnp.int32)
    quads = jnp.maximum((count + 2) // 4, 1)
    selves = jnp.sum(jnp.where(itself, 1.0, 0.0), axis=0, keepdims=True).astype(jnp.int32)
    total = jnp.sum(quads.astype(F32), axis=1, keepdims=True).astype(jnp.int32)
    lists[...] = jnp.full_like(lists, NOBODY * 32 + 13)
    lists[0:K_NEAR, :] = code
    lists[37:38, :] = quads
    lists[38:39, :] = selves
    lists[39:40, :] = jnp.broadcast_to(total, (1, 128))
    copy = pltpu.make_async_copy(lists, plan, sem)
    copy.start()
    eight[:, 3, :] = jnp.full((LEAF + 2 * RIM, 128), 1.0, F32)
    eight[:, 7, :] = jnp.full((LEAF + 2 * RIM, 128), SOFT, F32)
    eight3 = ((0, 4), (1, 5), (2, 6))
    for d in range(3):
        for row in eight3[d]:
            eight[0:RIM, row, :] = before_ref[d]
            eight[RIM : RIM + LEAF, row, :] = pos_ref[d]
            eight[RIM + LEAF : 2 * RIM + LEAF, row, :] = after_ref[d]
    charge[0:RIM, :] = before_ref[3]
    charge[RIM : RIM + LEAF, :] = chg_ref[...]
    charge[RIM + LEAF : 2 * RIM + LEAF, :] = after_ref[3]
    lane = lax.broadcasted_iota(jnp.int32, (128, 128), 1)
    features[NOBODY] = jnp.where(lane == 7, 1.0, 0.0).astype(BF16)
    spread[NOBODY] = jnp.zeros((128, 128), F32)
    for o in range(27):
        shift = (o // 9 - 1, o // 3 % 3 - 1, o % 3 - 1)
        table = jnp.zeros((8, 128), F32)
        for d in range(3):
            table = jnp.where((sub == d) | (sub == d + 4), -float(shift[d]), table)
        offsets[o] = table
    squares = (sub >= 4) & (sub < 7)

    def thirds(v):
        high = v.astype(BF16).astype(F32)
        rest = v - high
        middle = rest.astype(BF16).astype(F32)
        return high, middle, rest - middle

    def target(leaf, offset):
        v = eight[RIM + leaf] + offsets[offset]
        v = jnp.where(squares, v * v, v)
        high, middle, low = thirds(v)
        return jnp.concatenate([high, high, high, middle, middle, low], axis=0).astype(BF16)

    def separations(leaf, rows):
        padded = jnp.concatenate([rows, jnp.zeros((80, 128), BF16)], axis=0)
        return nn(features[leaf], padded)

    row = lax.broadcasted_iota(jnp.int32, (128, 128), 0)
    three = jnp.where((row >= 48) & (row < 51), 1.0, 0.0).astype(BF16)
    diagonal = row == lane
    identity = jnp.where(diagonal, 1.0, 0.0).astype(BF16)

    def source(leaf):
        v = eight[leaf]
        norm = jnp.sum(jnp.where(sub < 3, v * v, 0.0), axis=0, keepdims=True)
        v = jnp.where(sub < 3, -2.0 * v, jnp.where(sub == 3, norm, 1.0))
        high, middle, low = thirds(v)
        first, second, third = thirds(charge[pl.ds(leaf, 1), :])
        parts = jnp.where(sub == 0, first, jnp.where(sub == 1, second, jnp.where(sub == 2, third, 0.0)))
        rows = jnp.concatenate([high, middle, low, high, middle, high, parts], axis=0)
        rows = jnp.concatenate([rows, jnp.zeros((72, 128), F32)], axis=0)
        rows = rows.T.astype(BF16)
        features[leaf] = rows
        spread[leaf] = nn(rows, three)

    def prepare(step, carry):
        for u in range(16):
            source(16 * step + u)
        return carry

    lax.fori_loop(0, (LEAF + 2 * RIM) // 16, prepare, 0)
    copy.wait()

    def own_leaf(step, carry):
        for u in range(16):
            leaf = 16 * step + u
            squared = separations(RIM + leaf, target(leaf, 13))
            terms = jnp.where(diagonal, 0.0, spread[RIM + leaf] * lax.rsqrt(squared))
            sums[leaf] = jnp.sum(terms.reshape(16, 8, 128), axis=0) * plan[38, leaf].astype(F32)
        return carry

    lax.fori_loop(0, LEAF // 16, own_leaf, 0)

    def advance(state):
        leaf, quad = state
        last = quad + 1 >= plan[37, leaf]
        return (
            jnp.where(last, jnp.minimum(leaf + 1, LEAF - 1), leaf),
            jnp.where(last, jnp.where(leaf == LEAF - 1, 7, 0), quad + 1),
        )

    def produce(states):
        for g, (leaf, quad) in enumerate(states):
            for u in range(4):
                code = plan[4 * quad + u + 1, leaf]
                ready[4 * g + u] = target(leaf, code & 31)

    def consume(states):
        for g, (leaf, quad) in enumerate(states):
            part = sums[leaf]
            for u in range(4):
                code = plan[4 * quad + u + 1, leaf]
                squared = separations(code >> 5, ready[4 * g + u])
                terms = spread[code >> 5] * lax.rsqrt(squared)
                part = part + jnp.sum(terms.reshape(16, 8, 128), axis=0)
            sums[leaf] = part

    def following(state, number):
        made = []
        for _ in range(number):
            state = advance(state)
            made.append(state)
        return tuple(made)

    first = (jnp.int32(0), jnp.int32(0))
    states = (first,) + following(first, GROUP // 4 - 1)
    produce(states)

    def one_group(step, states):
        after = following(states[-1], GROUP // 4)
        consume(states)
        produce(after)
        return after

    quads = GROUP // 4
    lax.fori_loop(0, (plan[39, 0] + quads - 1) // quads, one_group, states)
    out_ref[...] = jnp.sum(sums[...], axis=1)


def count_rows(code, low, rows):
    wide = lax.broadcasted_iota(jnp.int32, (rows, 256), 0) == code
    narrow = lax.broadcasted_iota(jnp.int32, (128, 256), 0) == low
    return nt(
        jnp.where(wide, 1.0, 0.0).astype(BF16), jnp.where(narrow, 1.0, 0.0).astype(BF16)
    ).astype(BF16)


def encode(slots, classes, cells, capacity):
    ghost = jnp.maximum(slots - cells, 0)
    own = slots < cells
    code = jnp.where(own, 0, 1 + lax.rem(ghost, capacity)) * 16 + classes
    return jnp.where(slots < 0, -1, code), jnp.where(own, slots, lax.div(ghost, capacity))


def far_kernel(dev_ref, lists_ref, class_ref, leaf_ref, leaf_class_ref, parent_ref, parent_class_ref,
               lt_ref, pt_ref, arrived_ref, pos_ref, near_ref, stored_down, stored_far, out_ref,
               src, src_parent, even, odd, even_parent, grouped, code_scr, low_scr, turned, column, loc,
               result, down_ref, far_ref):
    lane = lax.broadcasted_iota(jnp.int32, (128, 128), 1)

    def count(first, capacity, table_ref):
        blocks = capacity + 1
        for t in range(16):
            rows = pl.ds(first + t, 1)
            table = count_rows(code_scr[rows, :], low_scr[rows, :], 16 * blocks)
            for b in range(blocks):
                table_ref[16 * t : 16 * t + 16, 128 * b : 128 * b + 128] = table[
                    16 * b : 16 * b + 16
                ]

    def place(ref, row, parts):
        count = parts[0].shape[0]
        (h0, l0), (h1, l1) = split(parts[0]), split(parts[1])
        tail = parts[2]
        high = tail.astype(BF16).astype(F32)
        low = pltpu.roll(tail - high, 32, 1)
        ref[row : row + count, 0:128] = h0
        ref[row : row + count, 128:256] = h1
        ref[row : row + count, 256:384] = l0
        ref[row : row + count, 384:512] = l1
        ref[row : row + count, 512:640] = (high + low).astype(BF16)

    def collect(product, row, count):
        grouped[0, pl.ds(row, count), :] = product[:, 0:128] + product[:, 256:384]
        grouped[1, pl.ds(row, count), :] = product[:, 128:256] + product[:, 384:512]
        tail = product[:, 512:640]
        grouped[2, pl.ds(row, count), :] = tail + pltpu.roll(tail, 96, 1)

    def arrived_tail(row, p):
        part = arrived_ref[pl.ds(row, 128, stride=ROWS), :]
        part = pltpu.roll(part, 128 - 32 * p, 1) if p else part
        return jnp.where(lane < 32, part, 0.0)

    width = leaf_ref.shape[0]
    code_scr[...] = jnp.full_like(code_scr, -1)
    low_scr[...] = jnp.full_like(low_scr, -1)
    for part, scratch in zip(
        encode(leaf_ref[...], leaf_class_ref[...], LEAF, CAP_L), (code_scr, low_scr)
    ):
        turned[...] = jnp.full_like(turned, -1.0)
        turned[:width, :] = part.astype(F32)
        scratch[0:128, 0:128] = turned[0:128, :].T.astype(jnp.int32)
        scratch[0:128, 128:256] = turned[128:256, :].T.astype(jnp.int32)
    for part, scratch in zip(
        encode(parent_ref[...], parent_class_ref[...], 16, CAP_P), (code_scr, low_scr)
    ):
        scratch[128:144, :width] = part
    count(128, CAP_P, even_parent)
    count(0, CAP_L, even)
    place(src, 0, [lt_ref[h] for h in range(3)])
    for c in range(CAP_L):
        place(
            src,
            128 * (c + 1),
            [arrived_ref[pl.ds(2 * c, 128, stride=ROWS), :], arrived_ref[pl.ds(2 * c + 1, 128, stride=ROWS), :], arrived_tail(40 + c // 4, c % 4)],
        )
    own = [jnp.concatenate([pt_ref[h], jnp.zeros((112, 128), F32)], axis=0) for h in range(3)]
    place(src_parent, 0, own)
    for c in range(CAP_P):
        place(
            src_parent,
            128 * (c + 1),
            [arrived_ref[pl.ds(32 + 2 * c, 128, stride=ROWS), :], arrived_ref[pl.ds(33 + 2 * c, 128, stride=ROWS), :], arrived_tail(44, c)],
        )
    collect(nn(even_parent[...], src_parent[...]), 2048, 256)
    mine = dev_ref[0] // 4
    operator = lax.broadcasted_iota(jnp.int32, (16, 128), 0)
    cell = lax.broadcasted_iota(jnp.int32, (16, 128), 1) // 4
    chosen = jnp.zeros((16, 128), F32)
    for k in range(7):
        hit = (operator == class_ref[mine * 7 + k]) & (cell == lists_ref[mine * 7 + k])
        chosen = chosen + jnp.where(hit, 1.0, 0.0)
    chosen = chosen.astype(BF16)
    for h in range(3):
        high, low = split(arrived_ref[pl.ds(45 + h, 128, stride=ROWS), :])
        grouped[h, 2304:2320, :] = nn(chosen, high) + nn(chosen, low)
        grouped[h, 2320:2560, :] = jnp.zeros((240, 128), F32)

    def two_blocks(step, carry):
        row = pl.multiple_of(step * 512, 512)
        count(32 * step + 16, CAP_L, odd)
        collect(nn(even[...], src[...]), row, 256)
        count(jnp.minimum(32 * step + 32, 112), CAP_L, even)
        collect(nn(odd[...], src[...]), row + 256, 256)
        return carry

    lax.fori_loop(0, 4, two_blocks, 0)

    cut(stored_far, far_ref)
    column[...] = jnp.zeros_like(column)
    loc[...] = jnp.zeros_like(loc)
    tall = lax.broadcasted_iota(jnp.int32, (384, 128), 1)
    leaf_total = jnp.zeros((COEF, 128), F32)
    upper_total = jnp.zeros((COEF, 128), F32)
    for q in range(4):
        upper = jnp.concatenate(
            [
                jnp.concatenate(
                    [grouped[h, pl.ds(2048 + 4 * q + p, 32, stride=16), :] for p in range(4)],
                    axis=0,
                ).T
                for h in range(3)
            ],
            axis=0,
        )
        for p in range(4):
            o = 4 * q + p
            leaf = jnp.concatenate(
                [grouped[h, pl.ds(o, 128, stride=16), :].T for h in range(3)], axis=0
            )
            operator_high, operator_low = split(operator_at(far_ref, o, 16))
            leaf_high, leaf_low = split(leaf)
            upper_high, upper_low = split(jnp.where(tall // 32 == p, upper, 0.0))
            first = nn(operator_high, jnp.concatenate([leaf_high, leaf_low], axis=1))
            second = nn(operator_high, jnp.concatenate([upper_high, upper_low], axis=1))
            third = nn(operator_low, jnp.concatenate([leaf_high, upper_high], axis=1))
            leaf_total = leaf_total + (first[:, 0:128] + (first[:, 128:256] + third[:, 0:128]))
            upper_total = upper_total + (
                second[:, 0:128] + (second[:, 128:256] + third[:, 128:256])
            )
    upper_total = upper_total + turn(upper_total, 32)
    upper_total = upper_total + turn(upper_total, 64)
    cut(stored_down, down_ref)
    column[0:COEF, :] = upper_total
    coarse = jnp.broadcast_to(column[:, 16:17], (384, 128))
    first = lax.rem(2 * dev_ref[0], 8)
    grand = apply_operator(operator_at(down_ref, first, 8), jnp.where(tall < 8, coarse, 0.0))
    grand = grand + apply_operator(
        operator_at(down_ref, first + 1, 8), jnp.where((tall >= 8) & (tall < 16), coarse, 0.0)
    )
    loc[0:COEF, :] = grand
    grand = loc[...]
    for c in range(8):
        upper_total = upper_total + apply_operator(
            operator_at(down_ref, c, 8), jnp.where((tall % 8 == c) & (tall < 16), grand, 0.0)
        )
    column[0:COEF, :] = upper_total
    parents = split(jnp.where(tall < 16, column[...], 0.0))
    repeat = lax.broadcasted_iota(jnp.int32, (128, 128), 0) == lane // 8
    repeat = jnp.where(repeat, 1.0, 0.0).astype(BF16)
    parents = [nn(part, repeat) for part in parents]
    for c in range(8):
        high, low = [jnp.where(tall % 8 == c, part, 0.0).astype(BF16) for part in parents]
        leaf_total = leaf_total + apply_parts(operator_at(down_ref, c, 8), high, low)
    loc[0:COEF, :] = leaf_total
    x_all, y_all, z_all = [2.0 * pos_ref[d].T for d in range(3)]
    for part in range(2):
        piece = slice(64 * part, 64 * part + 64)
        x, y, z = x_all[piece], y_all[piece], z_all[piece]
        over_i = None
        for i in range(ORDER, -1, -1):
            over_j = None
            for j in range(ORDER - i, -1, -1):
                over_k = None
                for k in range(ORDER - i - j, -1, -1):
                    a = INDEX[(i, j, k)]
                    value = loc[a : a + 1, :]
                    over_k = value if over_k is None else over_k * z + value
                over_j = over_k if over_j is None else over_j * y + over_k
            over_i = over_j if over_i is None else over_i * x + over_j
        result[piece, :] = over_i
    out_ref[...] = near_ref[...] + result[...].T


def cost(flops, moved):
    return pl.CostEstimate(flops=flops, bytes_accessed=moved, transcendentals=0)


def shape(*dims, dtype=F32):
    return jax.ShapeDtypeStruct(dims, dtype)


def limits(mib):
    return pltpu.CompilerParams(vmem_limit_bytes=mib * 1024 * 1024)


def upward_call(dev, pos, chg, up_shift):
    return pl.pallas_call(
        upward_kernel,
        out_shape=(shape(3, 128, 128), shape(3, 16, 128), shape(3, 128)),
        in_specs=[SMEM] + [VMEM] * 3,
        out_specs=(VMEM, VMEM, VMEM),
        scratch_shapes=[
            pltpu.VMEM((384, 128), F32),
            pltpu.VMEM((384, 128), F32),
            pltpu.VMEM((3, 8 * COEF, 128), F32),
        ],
        compiler_params=limits(16),
        cost_estimate=cost(8 * 10**9, 3 * 10**6),
        name="upward",
    )(dev, pos, chg, up_shift)


def pack_call(dev, asked, lt, pt, lift):
    return pl.pallas_call(
        pack_kernel,
        out_shape=shape(128 * ROWS, 128),
        in_specs=[SMEM] + [VMEM] * 4,
        out_specs=VMEM,
        compiler_params=limits(24),
        cost_estimate=cost(10**9, 4 * 10**6),
        name="pack",
    )(dev, asked, lt, pt, lift)


def near_call(dev, near_leaves, near_offsets, pos, chg, before, after):
    return pl.pallas_call(
        near_kernel,
        out_shape=shape(128, 128),
        in_specs=[SMEM] + [VMEM] * 6,
        out_specs=VMEM,
        scratch_shapes=[
            pltpu.VMEM((LEAF + 2 * RIM, 8, 128), F32),
            pltpu.VMEM((LEAF + 2 * RIM, 128), F32),
            pltpu.VMEM((27, 8, 128), F32),
            pltpu.VMEM((NOBODY + 1, 128, 128), BF16),
            pltpu.VMEM((NOBODY + 1, 128, 128), F32),
            pltpu.VMEM((LEAF, 8, 128), F32),
            pltpu.VMEM((GROUP, 48, 128), BF16),
            pltpu.VMEM((40, 128), jnp.int32),
            pltpu.SMEM((40, 128), jnp.int32),
            pltpu.SemaphoreType.DMA(()),
        ],
        compiler_params=limits(24),
        cost_estimate=cost(30 * 10**9, 10**6),
        name="near",
    )(dev, near_leaves, near_offsets, pos, chg, before, after)


def far_call(dev, lists, classes, leaves, leaf_class, parents, parent_class, lt, pt, arrived, pos, near,
             down_shift, far_shift):
    return pl.pallas_call(
        far_kernel,
        out_shape=shape(128, 128),
        in_specs=[SMEM] * 3 + [VMEM] * 11,
        out_specs=VMEM,
        scratch_shapes=[
            pltpu.VMEM((2176, 640), BF16),
            pltpu.VMEM((640, 640), BF16),
            pltpu.VMEM((256, 2176), BF16),
            pltpu.VMEM((256, 2176), BF16),
            pltpu.VMEM((256, 640), BF16),
            pltpu.VMEM((3, 16 * TARGETS, 128), F32),
            pltpu.VMEM((144, 256), jnp.int32),
            pltpu.VMEM((144, 256), jnp.int32),
            pltpu.VMEM((256, 128), F32),
            pltpu.VMEM((384, 128), F32),
            pltpu.VMEM((384, 128), F32),
            pltpu.VMEM((128, 128), F32),
            pltpu.VMEM((3, 8 * COEF, 128), F32),
            pltpu.VMEM((3, 16 * COEF, 128), F32),
        ],
        compiler_params=limits(40),
        cost_estimate=cost(20 * 10**9, 20 * 10**6),
        name="far",
    )(dev, lists, classes, leaves, leaf_class, parents, parent_class, lt, pt, arrived, pos, near,
      down_shift, far_shift)


def by_rows(operators):
    return jnp.swapaxes(operators, 0, 1).reshape(-1, operators.shape[2])


def per_device(
    positions,
    charges,
    near_leaves,
    near_offsets,
    far_leaves,
    far_leaf_class,
    leaf_plan,
    far_parents,
    far_parent_class,
    parent_plan,
    coarse_lists,
    coarse_class,
    up_shift,
    down_shift,
    far_shift,
):
    device = lax.axis_index(AXES)
    dev = device.reshape(1).astype(jnp.int32)
    filler = jnp.full((PLAN - CAP_L - CAP_P, 128), -1, jnp.int32)
    plans = jnp.concatenate([leaf_plan[0].T, parent_plan[0].T, filler], 0)
    asked = lax.all_gather(plans, AXES, axis=0, tiled=True)
    pos = positions.reshape(3, LEAF, 128)
    chg = charges.reshape(LEAF, 128)
    own = jnp.concatenate([pos, chg[None]], 0)
    size = lax.axis_size(AXES)
    up = [(i, i + 1) for i in range(size - 1)]
    down = [(j, i) for i, j in up]
    before = lax.ppermute(own[:, LEAF - RIM :], AXES, up)
    after = lax.ppermute(own[:, :RIM], AXES, down)
    lt, pt, lift = upward_call(dev, pos, chg, by_rows(up_shift))
    outgoing = pack_call(dev, asked, lt, pt, lift).reshape(LEAF, ROWS, 128)
    near_leaves, outgoing = lax.optimization_barrier((near_leaves, outgoing))
    arrived = lax.all_to_all(outgoing, AXES, split_axis=0, concat_axis=0, tiled=True)
    arrived = arrived.reshape(LEAF * ROWS, 128)
    near = near_call(dev, near_leaves.T, near_offsets.T, pos, chg, before, after)
    potential = far_call(
        dev, coarse_lists.reshape(-1), coarse_class.reshape(-1), far_leaves.T, far_leaf_class.T,
        far_parents, far_parent_class, lt, pt, arrived, pos, near,
        by_rows(down_shift), by_rows(far_shift),
    )
    return potential.reshape(-1)


def solution(mesh):
    row = P(AXES, None)
    placed = (
        P(None, AXES), P(AXES), row, row, row, row, P(AXES, None, None), row, row,
        P(AXES, None, None), P(), P(), P(), P(), P(),
    )
    return jax.shard_map(
        per_device, mesh=mesh, in_specs=placed, out_specs=P(AXES), check_vma=False
    )
```

```python
import jax
import jax.numpy as jnp
import numpy as np
from jax import lax
from jax.experimental import pallas as pl
from jax.experimental.pallas import tpu as pltpu
from jax.sharding import PartitionSpec as P

ORDER = 10
COEF = 286
RIM = 32
LEAF = 128
K_NEAR = 27
CAP_L = 16
CAP_P = 4
ROWS = 48
TARGETS = 160
GROUP = 64
NOBODY = LEAF + 2 * RIM
SOFT = 0.05 * 0.05
AXES = ("gx", "gy")
F32 = jnp.float32
BF16 = jnp.bfloat16
VMEM = pl.BlockSpec(memory_space=pltpu.VMEM)
SMEM = pl.BlockSpec(memory_space=pltpu.SMEM)
HBM = pl.BlockSpec(memory_space=pl.ANY)


def exponents(order):
    entries = []
    for degree in range(order + 1):
        for first_power in range(degree, -1, -1):
            for second_power in range(degree - first_power, -1, -1):
                entries.append((first_power, second_power, degree - first_power - second_power))
    return entries


INDEX = {powers: number for number, powers in enumerate(exponents(ORDER))}


def split(x):
    high = x.astype(BF16)
    return high, (x - high.astype(F32)).astype(BF16)


def nt(a, b):
    return lax.dot_general(a, b, (((1,), (1,)), ((), ())), preferred_element_type=F32)


def nn(a, b):
    return jnp.dot(a, b, preferred_element_type=F32)


def turn(x, left):
    return pltpu.roll(x, 128 - left, 1)


def apply_parts(operator, high, low):
    operator_high, operator_low = split(operator)
    both = nn(operator_high, jnp.concatenate([high, low], axis=1))
    return both[:, 0:128] + (both[:, 128:256] + nn(operator_low, high))


def apply_operator(operator, columns):
    return apply_parts(operator, *split(columns))


def fetches(source, chunks, tail, sems, first):
    return [
        pltpu.make_async_copy(source.at[:, 0:128], chunks.at[0], sems.at[first]),
        pltpu.make_async_copy(source.at[:, 128:256], chunks.at[1], sems.at[first + 1]),
        pltpu.make_async_copy(source.at[:, 256:COEF], tail, sems.at[first + 2]),
    ]


def arrive(copies, chunks, tail):
    chunks[2] = jnp.zeros(chunks.shape[1:], F32)
    for copy in copies:
        copy.wait()
    chunks[2, :, 0 : COEF - 256] = tail[...]


def operator_at(chunks, number, count):
    rows = pl.ds(number, COEF, stride=count)
    return jnp.concatenate([chunks[h, rows, :] for h in range(3)], axis=1)


def upward_kernel(dev_ref, asked_ref, pos_ref, chg_ref, up_hbm, lt_ref, pt_ref, out_ref, moments,
                  column, up_ref, up_tail, sems):
    copies = fetches(up_hbm, up_ref, up_tail, sems, 0)
    for copy in copies:
        copy.start()
    x, y, z = [2.0 * pos_ref[d].T for d in range(3)]
    with_x = chg_ref[...].T
    z_powers = [None, z]
    for k in range(ORDER - 1):
        z_powers.append(z_powers[-1] * z)
    moments[COEF - 6 : 384, :] = jnp.zeros((384 - COEF + 6, LEAF), F32)
    for i in range(ORDER + 1):
        if i:
            with_x = with_x * x
        with_xy = with_x
        for j in range(ORDER + 1 - i):
            if j:
                with_xy = with_xy * y
            for k in range(ORDER + 1 - i - j):
                term = with_xy * z_powers[k] if k else with_xy
                a = INDEX[(i, j, k)]
                moments[a : a + 1, :] = jnp.sum(term, axis=0, keepdims=True)
    for h in range(3):
        lt_ref[h] = moments[128 * h : 128 * h + 128, :].T
    column[...] = jnp.zeros_like(column)
    arrive(copies, up_ref, up_tail)
    lane = lax.broadcasted_iota(jnp.int32, (384, 128), 1)
    leaves = moments[...]
    total = jnp.zeros((COEF, 128), F32)
    for c in range(8):
        total = total + apply_operator(
            operator_at(up_ref, c, 8), jnp.where(lane % 8 == c, leaves, 0.0)
        )
    for left in (4, 2, 1):
        total = total + turn(total, left)
    column[0:COEF, :] = total
    parents = column[...]
    total = jnp.zeros((COEF, 128), F32)
    for c in range(8):
        total = total + apply_operator(
            operator_at(up_ref, c, 8), jnp.where(lane % 64 == 8 * c, parents, 0.0)
        )
    for h in range(3):
        moments[0:128, :] = column[128 * h : 128 * h + 128, :].T
        pt_ref[h] = moments[pl.ds(0, 16, stride=8), :]
    for left in (8, 16, 32):
        total = total + turn(total, left)
    column[0:COEF, :] = total
    grand = column[...]
    first = lax.rem(2 * dev_ref[0], 8)
    total = apply_operator(operator_at(up_ref, first, 8), jnp.where(lane == 0, grand, 0.0))
    total = total + apply_operator(
        operator_at(up_ref, first + 1, 8), jnp.where(lane == 64, grand, 0.0)
    )
    column[0:COEF, :] = total + turn(total, 64)
    for h in range(3):
        lift = column[128 * h : 128 * h + 128, :].T[0:1, :]
        out_ref[pl.ds(45 + h, 128, stride=ROWS), :] = jnp.broadcast_to(lift, (128, 128))
    lane = lax.broadcasted_iota(jnp.int32, (128, 128), 1)
    leaf_rows = jnp.concatenate([lt_ref[h] for h in range(3)], axis=1)
    parent_rows = jnp.concatenate([pt_ref[h] for h in range(3)], axis=1)
    parent_rows = jnp.concatenate([parent_rows, jnp.zeros((112, 384), F32)], axis=0)
    leaf_rows = jnp.concatenate(split(leaf_rows), axis=0)
    parent_rows = jnp.concatenate(split(parent_rows), axis=0)
    for q in range(5):
        tail = jnp.zeros((128, 128), F32)
        for p in range(4):
            j = 4 * q + p
            chosen = jnp.where(asked_ref[:, j : j + 1] == lane, 1.0, 0.0).astype(BF16)
            chosen = jnp.concatenate([chosen, chosen], axis=1)
            rows = nn(chosen, leaf_rows if q < 4 else parent_rows)
            out_ref[pl.ds(2 * j, 128, stride=ROWS), :] = rows[:, 0:128]
            out_ref[pl.ds(2 * j + 1, 128, stride=ROWS), :] = rows[:, 128:256]
            part = rows[:, 256:384]
            tail = tail + (pltpu.roll(part, 32 * p, 1) if p else part)
        out_ref[pl.ds(40 + q, 128, stride=ROWS), :] = tail


def near_kernel(dev_ref, leaves_ref, offsets_ref, pos_ref, chg_ref, before_ref, after_ref, out_ref,
                eight, charge, offsets, features, spread, sums, ready, lists, plan, sem):
    sub = lax.broadcasted_iota(jnp.int32, (8, 128), 0)
    named = leaves_ref[...]
    first_leaf = dev_ref[0] * LEAF
    present = named >= 0
    own_id = first_leaf + lax.broadcasted_iota(jnp.int32, (K_NEAR, LEAF), 1)
    itself = (named == own_id) & (offsets_ref[...] == 13)
    counted = present & jnp.logical_not(itself)
    code = jnp.where(counted, (named - first_leaf + RIM) * 32 + offsets_ref[...], NOBODY * 32 + 13)
    count = jnp.sum(jnp.where(present, 1.0, 0.0), axis=0, keepdims=True).astype(jnp.int32)
    quads = jnp.maximum((count + 2) // 4, 1)
    selves = jnp.sum(jnp.where(itself, 1.0, 0.0), axis=0, keepdims=True).astype(jnp.int32)
    total = jnp.sum(quads.astype(F32), axis=1, keepdims=True).astype(jnp.int32)
    lists[...] = jnp.full_like(lists, NOBODY * 32 + 13)
    lists[0:K_NEAR, :] = code
    lists[37:38, :] = quads
    lists[38:39, :] = selves
    lists[39:40, :] = jnp.broadcast_to(total, (1, 128))
    copy = pltpu.make_async_copy(lists, plan, sem)
    copy.start()
    eight[:, 3, :] = jnp.full((LEAF + 2 * RIM, 128), 1.0, F32)
    eight[:, 7, :] = jnp.full((LEAF + 2 * RIM, 128), SOFT, F32)
    eight3 = ((0, 4), (1, 5), (2, 6))
    for d in range(3):
        for row in eight3[d]:
            eight[0:RIM, row, :] = before_ref[d]
            eight[RIM : RIM + LEAF, row, :] = pos_ref[d]
            eight[RIM + LEAF : 2 * RIM + LEAF, row, :] = after_ref[d]
    charge[0:RIM, :] = before_ref[3]
    charge[RIM : RIM + LEAF, :] = chg_ref[...]
    charge[RIM + LEAF : 2 * RIM + LEAF, :] = after_ref[3]
    lane = lax.broadcasted_iota(jnp.int32, (128, 128), 1)
    features[NOBODY] = jnp.where(lane == 7, 1.0, 0.0).astype(BF16)
    spread[NOBODY] = jnp.zeros((128, 128), F32)
    for o in range(27):
        shift = (o // 9 - 1, o // 3 % 3 - 1, o % 3 - 1)
        table = jnp.zeros((8, 128), F32)
        for d in range(3):
            table = jnp.where((sub == d) | (sub == d + 4), -float(shift[d]), table)
        offsets[o] = table
    squares = (sub >= 4) & (sub < 7)

    def thirds(v):
        high = v.astype(BF16).astype(F32)
        rest = v - high
        middle = rest.astype(BF16).astype(F32)
        return high, middle, rest - middle

    def target(leaf, offset):
        v = eight[RIM + leaf] + offsets[offset]
        v = jnp.where(squares, v * v, v)
        high, middle, low = thirds(v)
        return jnp.concatenate([high, high, high, middle, middle, low], axis=0).astype(BF16)

    def separations(leaf, rows):
        padded = jnp.concatenate([rows, jnp.zeros((80, 128), BF16)], axis=0)
        return nn(features[leaf], padded)

    row = lax.broadcasted_iota(jnp.int32, (128, 128), 0)
    three = jnp.where((row >= 48) & (row < 51), 1.0, 0.0).astype(BF16)
    diagonal = row == lane
    identity = jnp.where(diagonal, 1.0, 0.0).astype(BF16)

    def source(leaf):
        v = eight[leaf]
        norm = jnp.sum(jnp.where(sub < 3, v * v, 0.0), axis=0, keepdims=True)
        v = jnp.where(sub < 3, -2.0 * v, jnp.where(sub == 3, norm, 1.0))
        high, middle, low = thirds(v)
        first, second, third = thirds(charge[pl.ds(leaf, 1), :])
        parts = jnp.where(sub == 0, first, jnp.where(sub == 1, second, jnp.where(sub == 2, third, 0.0)))
        rows = jnp.concatenate([high, middle, low, high, middle, high, parts], axis=0)
        rows = jnp.concatenate([rows, jnp.zeros((72, 128), F32)], axis=0)
        rows = rows.T.astype(BF16)
        features[leaf] = rows
        spread[leaf] = nn(rows, three)

    def prepare(step, carry):
        for u in range(16):
            source(16 * step + u)
        return carry

    lax.fori_loop(0, (LEAF + 2 * RIM) // 16, prepare, 0)
    copy.wait()

    def own_leaf(step, carry):
        for u in range(16):
            leaf = 16 * step + u
            squared = separations(RIM + leaf, target(leaf, 13))
            terms = jnp.where(diagonal, 0.0, spread[RIM + leaf] * lax.rsqrt(squared))
            sums[leaf] = jnp.sum(terms.reshape(16, 8, 128), axis=0) * plan[38, leaf].astype(F32)
        return carry

    lax.fori_loop(0, LEAF // 16, own_leaf, 0)

    def advance(state):
        leaf, quad = state
        last = quad + 1 >= plan[37, leaf]
        return (
            jnp.where(last, jnp.minimum(leaf + 1, LEAF - 1), leaf),
            jnp.where(last, jnp.where(leaf == LEAF - 1, 7, 0), quad + 1),
        )

    def produce(states):
        for g, (leaf, quad) in enumerate(states):
            for u in range(4):
                code = plan[4 * quad + u + 1, leaf]
                ready[4 * g + u] = target(leaf, code & 31)

    def consume(states):
        for g, (leaf, quad) in enumerate(states):
            part = sums[leaf]
            for u in range(4):
                code = plan[4 * quad + u + 1, leaf]
                squared = separations(code >> 5, ready[4 * g + u])
                terms = spread[code >> 5] * lax.rsqrt(squared)
                part = part + jnp.sum(terms.reshape(16, 8, 128), axis=0)
            sums[leaf] = part

    def following(state, number):
        made = []
        for _ in range(number):
            state = advance(state)
            made.append(state)
        return tuple(made)

    first = (jnp.int32(0), jnp.int32(0))
    states = (first,) + following(first, GROUP // 4 - 1)
    produce(states)

    def one_group(step, states):
        after = following(states[-1], GROUP // 4)
        consume(states)
        produce(after)
        return after

    quads = GROUP // 4
    lax.fori_loop(0, (plan[39, 0] + quads - 1) // quads, one_group, states)
    out_ref[...] = jnp.sum(sums[...], axis=1)


def count_rows(code, low, rows):
    wide = lax.broadcasted_iota(jnp.int32, (rows, 256), 0) == code
    narrow = lax.broadcasted_iota(jnp.int32, (128, 256), 0) == low
    return nt(
        jnp.where(wide, 1.0, 0.0).astype(BF16), jnp.where(narrow, 1.0, 0.0).astype(BF16)
    ).astype(BF16)


def encode(slots, classes, cells, capacity):
    ghost = jnp.maximum(slots - cells, 0)
    own = slots < cells
    code = jnp.where(own, 0, 1 + lax.rem(ghost, capacity)) * 16 + classes
    return jnp.where(slots < 0, -1, code), jnp.where(own, slots, lax.div(ghost, capacity))


def far_kernel(dev_ref, lists_ref, class_ref, leaf_ref, leaf_class_ref, parent_ref, parent_class_ref,
               lt_ref, pt_ref, pos_ref, near_ref, arrived_hbm, down_hbm, far_hbm, out_ref,
               src, src_parent, even, odd, even_parent, grouped, code_scr, low_scr, turned, column, loc,
               result, arrived_ref, down_ref, down_tail, far_ref, far_tail, sems):
    arrival = pltpu.make_async_copy(arrived_hbm, arrived_ref, sems.at[6])
    arrival.start()
    far_copies = fetches(far_hbm, far_ref, far_tail, sems, 0)
    down_copies = fetches(down_hbm, down_ref, down_tail, sems, 3)
    for copy in far_copies + down_copies:
        copy.start()
    lane = lax.broadcasted_iota(jnp.int32, (128, 128), 1)

    def count(first, capacity, table_ref):
        blocks = capacity + 1
        for t in range(16):
            rows = pl.ds(first + t, 1)
            table = count_rows(code_scr[rows, :], low_scr[rows, :], 16 * blocks)
            for b in range(blocks):
                table_ref[16 * t : 16 * t + 16, 128 * b : 128 * b + 128] = table[
                    16 * b : 16 * b + 16
                ]

    def place(ref, row, parts):
        count = parts[0].shape[0]
        (h0, l0), (h1, l1) = split(parts[0]), split(parts[1])
        tail = parts[2]
        high = tail.astype(BF16).astype(F32)
        low = pltpu.roll(tail - high, 32, 1)
        ref[row : row + count, 0:128] = h0
        ref[row : row + count, 128:256] = h1
        ref[row : row + count, 256:384] = l0
        ref[row : row + count, 384:512] = l1
        ref[row : row + count, 512:640] = (high + low).astype(BF16)

    def collect(product, row, count):
        grouped[0, pl.ds(row, count), :] = product[:, 0:128] + product[:, 256:384]
        grouped[1, pl.ds(row, count), :] = product[:, 128:256] + product[:, 384:512]
        tail = product[:, 512:640]
        grouped[2, pl.ds(row, count), :] = tail + pltpu.roll(tail, 96, 1)

    def arrived_tail(row, p):
        part = arrived_ref[pl.ds(row, 128, stride=ROWS), :]
        part = pltpu.roll(part, 128 - 32 * p, 1) if p else part
        return jnp.where(lane < 32, part, 0.0)

    width = leaf_ref.shape[0]
    code_scr[...] = jnp.full_like(code_scr, -1)
    low_scr[...] = jnp.full_like(low_scr, -1)
    for part, scratch in zip(
        encode(leaf_ref[...], leaf_class_ref[...], LEAF, CAP_L), (code_scr, low_scr)
    ):
        turned[...] = jnp.full_like(turned, -1.0)
        turned[:width, :] = part.astype(F32)
        scratch[0:128, 0:128] = turned[0:128, :].T.astype(jnp.int32)
        scratch[0:128, 128:256] = turned[128:256, :].T.astype(jnp.int32)
    for part, scratch in zip(
        encode(parent_ref[...], parent_class_ref[...], 16, CAP_P), (code_scr, low_scr)
    ):
        scratch[128:144, :width] = part
    count(128, CAP_P, even_parent)
    count(0, CAP_L, even)
    place(src, 0, [lt_ref[h] for h in range(3)])
    arrival.wait()
    for c in range(CAP_L):
        place(
            src,
            128 * (c + 1),
            [arrived_ref[pl.ds(2 * c, 128, stride=ROWS), :], arrived_ref[pl.ds(2 * c + 1, 128, stride=ROWS), :], arrived_tail(40 + c // 4, c % 4)],
        )
    own = [jnp.concatenate([pt_ref[h], jnp.zeros((112, 128), F32)], axis=0) for h in range(3)]
    place(src_parent, 0, own)
    for c in range(CAP_P):
        place(
            src_parent,
            128 * (c + 1),
            [arrived_ref[pl.ds(32 + 2 * c, 128, stride=ROWS), :], arrived_ref[pl.ds(33 + 2 * c, 128, stride=ROWS), :], arrived_tail(44, c)],
        )
    collect(nn(even_parent[...], src_parent[...]), 2048, 256)
    mine = dev_ref[0] // 4
    operator = lax.broadcasted_iota(jnp.int32, (16, 128), 0)
    cell = lax.broadcasted_iota(jnp.int32, (16, 128), 1) // 4
    chosen = jnp.zeros((16, 128), F32)
    for k in range(7):
        hit = (operator == class_ref[mine * 7 + k]) & (cell == lists_ref[mine * 7 + k])
        chosen = chosen + jnp.where(hit, 1.0, 0.0)
    chosen = chosen.astype(BF16)
    for h in range(3):
        high, low = split(arrived_ref[pl.ds(45 + h, 128, stride=ROWS), :])
        grouped[h, 2304:2320, :] = nn(chosen, high) + nn(chosen, low)
        grouped[h, 2320:2560, :] = jnp.zeros((240, 128), F32)

    def two_blocks(step, carry):
        row = pl.multiple_of(step * 512, 512)
        count(32 * step + 16, CAP_L, odd)
        collect(nn(even[...], src[...]), row, 256)
        count(jnp.minimum(32 * step + 32, 112), CAP_L, even)
        collect(nn(odd[...], src[...]), row + 256, 256)
        return carry

    lax.fori_loop(0, 4, two_blocks, 0)

    arrive(far_copies, far_ref, far_tail)
    column[...] = jnp.zeros_like(column)
    loc[...] = jnp.zeros_like(loc)
    tall = lax.broadcasted_iota(jnp.int32, (384, 128), 1)
    leaf_total = jnp.zeros((COEF, 128), F32)
    upper_total = jnp.zeros((COEF, 128), F32)
    for q in range(4):
        upper = jnp.concatenate(
            [
                jnp.concatenate(
                    [grouped[h, pl.ds(2048 + 4 * q + p, 32, stride=16), :] for p in range(4)],
                    axis=0,
                ).T
                for h in range(3)
            ],
            axis=0,
        )
        for p in range(4):
            o = 4 * q + p
            leaf = jnp.concatenate(
                [grouped[h, pl.ds(o, 128, stride=16), :].T for h in range(3)], axis=0
            )
            operator_high, operator_low = split(operator_at(far_ref, o, 16))
            leaf_high, leaf_low = split(leaf)
            upper_high, upper_low = split(jnp.where(tall // 32 == p, upper, 0.0))
            first = nn(operator_high, jnp.concatenate([leaf_high, leaf_low], axis=1))
            second = nn(operator_high, jnp.concatenate([upper_high, upper_low], axis=1))
            third = nn(operator_low, jnp.concatenate([leaf_high, upper_high], axis=1))
            leaf_total = leaf_total + (first[:, 0:128] + (first[:, 128:256] + third[:, 0:128]))
            upper_total = upper_total + (
                second[:, 0:128] + (second[:, 128:256] + third[:, 128:256])
            )
    upper_total = upper_total + turn(upper_total, 32)
    upper_total = upper_total + turn(upper_total, 64)
    arrive(down_copies, down_ref, down_tail)
    column[0:COEF, :] = upper_total
    coarse = jnp.broadcast_to(column[:, 16:17], (384, 128))
    first = lax.rem(2 * dev_ref[0], 8)
    grand = apply_operator(operator_at(down_ref, first, 8), jnp.where(tall < 8, coarse, 0.0))
    grand = grand + apply_operator(
        operator_at(down_ref, first + 1, 8), jnp.where((tall >= 8) & (tall < 16), coarse, 0.0)
    )
    loc[0:COEF, :] = grand
    grand = loc[...]
    for c in range(8):
        upper_total = upper_total + apply_operator(
            operator_at(down_ref, c, 8), jnp.where((tall % 8 == c) & (tall < 16), grand, 0.0)
        )
    column[0:COEF, :] = upper_total
    parents = split(jnp.where(tall < 16, column[...], 0.0))
    repeat = lax.broadcasted_iota(jnp.int32, (128, 128), 0) == lane // 8
    repeat = jnp.where(repeat, 1.0, 0.0).astype(BF16)
    parents = [nn(part, repeat) for part in parents]
    for c in range(8):
        high, low = [jnp.where(tall % 8 == c, part, 0.0).astype(BF16) for part in parents]
        leaf_total = leaf_total + apply_parts(operator_at(down_ref, c, 8), high, low)
    loc[0:COEF, :] = leaf_total
    x_all, y_all, z_all = [2.0 * pos_ref[d].T for d in range(3)]
    for part in range(2):
        piece = slice(64 * part, 64 * part + 64)
        x, y, z = x_all[piece], y_all[piece], z_all[piece]
        over_i = None
        for i in range(ORDER, -1, -1):
            over_j = None
            for j in range(ORDER - i, -1, -1):
                over_k = None
                for k in range(ORDER - i - j, -1, -1):
                    a = INDEX[(i, j, k)]
                    value = loc[a : a + 1, :]
                    over_k = value if over_k is None else over_k * z + value
                over_j = over_k if over_j is None else over_j * y + over_k
            over_i = over_j if over_i is None else over_i * x + over_j
        result[piece, :] = over_i
    out_ref[...] = near_ref[...] + result[...].T


def cost(flops, moved):
    return pl.CostEstimate(flops=flops, bytes_accessed=moved, transcendentals=0)


def shape(*dims, dtype=F32):
    return jax.ShapeDtypeStruct(dims, dtype)


def limits(mib):
    return pltpu.CompilerParams(vmem_limit_bytes=mib * 1024 * 1024)


def upward_call(dev, asked, pos, chg, up_shift):
    return pl.pallas_call(
        upward_kernel,
        out_shape=(shape(3, 128, 128), shape(3, 16, 128), shape(128 * ROWS, 128)),
        in_specs=[SMEM] + [VMEM] * 3 + [HBM],
        out_specs=(VMEM, VMEM, VMEM),
        scratch_shapes=[
            pltpu.VMEM((384, 128), F32),
            pltpu.VMEM((384, 128), F32),
            pltpu.VMEM((3, 8 * COEF, 128), F32),
            pltpu.VMEM((8 * COEF, COEF - 256), F32),
            pltpu.SemaphoreType.DMA((3,)),
        ],
        compiler_params=limits(60),
        cost_estimate=cost(8 * 10**9, 3 * 10**6),
        name="upward",
    )(dev, asked, pos, chg, up_shift)


def near_call(dev, near_leaves, near_offsets, pos, chg, before, after):
    return pl.pallas_call(
        near_kernel,
        out_shape=shape(128, 128),
        in_specs=[SMEM] + [VMEM] * 6,
        out_specs=VMEM,
        scratch_shapes=[
            pltpu.VMEM((LEAF + 2 * RIM, 8, 128), F32),
            pltpu.VMEM((LEAF + 2 * RIM, 128), F32),
            pltpu.VMEM((27, 8, 128), F32),
            pltpu.VMEM((NOBODY + 1, 128, 128), BF16),
            pltpu.VMEM((NOBODY + 1, 128, 128), F32),
            pltpu.VMEM((LEAF, 8, 128), F32),
            pltpu.VMEM((GROUP, 48, 128), BF16),
            pltpu.VMEM((40, 128), jnp.int32),
            pltpu.SMEM((40, 128), jnp.int32),
            pltpu.SemaphoreType.DMA(()),
        ],
        compiler_params=limits(60),
        cost_estimate=cost(30 * 10**9, 10**6),
        name="near",
    )(dev, near_leaves, near_offsets, pos, chg, before, after)


def far_call(dev, lists, classes, leaves, leaf_class, parents, parent_class, lt, pt, pos, near, arrived,
             down_shift, far_shift):
    return pl.pallas_call(
        far_kernel,
        out_shape=shape(128, 128),
        in_specs=[SMEM] * 3 + [VMEM] * 8 + [HBM] * 3,
        out_specs=VMEM,
        scratch_shapes=[
            pltpu.VMEM((2176, 640), BF16),
            pltpu.VMEM((640, 640), BF16),
            pltpu.VMEM((256, 2176), BF16),
            pltpu.VMEM((256, 2176), BF16),
            pltpu.VMEM((256, 640), BF16),
            pltpu.VMEM((3, 16 * TARGETS, 128), F32),
            pltpu.VMEM((144, 256), jnp.int32),
            pltpu.VMEM((144, 256), jnp.int32),
            pltpu.VMEM((256, 128), F32),
            pltpu.VMEM((384, 128), F32),
            pltpu.VMEM((384, 128), F32),
            pltpu.VMEM((128, 128), F32),
            pltpu.VMEM((128 * ROWS, 128), F32),
            pltpu.VMEM((3, 8 * COEF, 128), F32),
            pltpu.VMEM((8 * COEF, COEF - 256), F32),
            pltpu.VMEM((3, 16 * COEF, 128), F32),
            pltpu.VMEM((16 * COEF, COEF - 256), F32),
            pltpu.SemaphoreType.DMA((7,)),
        ],
        compiler_params=limits(60),
        cost_estimate=cost(20 * 10**9, 20 * 10**6),
        name="far",
    )(dev, lists, classes, leaves, leaf_class, parents, parent_class, lt, pt, pos, near, arrived,
      down_shift, far_shift)


def by_rows(operators):
    return jnp.swapaxes(operators, 0, 1).reshape(-1, operators.shape[2])


def per_device(
    positions,
    charges,
    near_leaves,
    near_offsets,
    far_leaves,
    far_leaf_class,
    leaf_plan,
    far_parents,
    far_parent_class,
    parent_plan,
    coarse_lists,
    coarse_class,
    up_shift,
    down_shift,
    far_shift,
):
    device = lax.axis_index(AXES)
    dev = device.reshape(1).astype(jnp.int32)
    plans = jnp.concatenate([leaf_plan[0], parent_plan[0]], 1)
    asked = lax.all_to_all(plans, AXES, split_axis=0, concat_axis=0, tiled=True)
    pos = positions.reshape(3, LEAF, 128)
    chg = charges.reshape(LEAF, 128)
    rims = [
        jnp.concatenate([pos[:, rows], chg[None, rows]], 0)
        for rows in (slice(LEAF - RIM, LEAF), slice(0, RIM))
    ]
    size = lax.axis_size(AXES)
    up = [(i, i + 1) for i in range(size - 1)]
    down = [(j, i) for i, j in up]
    before = lax.ppermute(rims[0], AXES, up)
    after = lax.ppermute(rims[1], AXES, down)
    before, after, asked = lax.optimization_barrier((before, after, asked))
    lt, pt, outgoing = upward_call(dev, asked, pos, chg, by_rows(up_shift))
    outgoing = outgoing.reshape(LEAF, ROWS, 128)
    near_leaves, outgoing = lax.optimization_barrier((near_leaves, outgoing))
    arrived = lax.all_to_all(outgoing, AXES, split_axis=0, concat_axis=0, tiled=True)
    arrived = arrived.reshape(LEAF * ROWS, 128)
    near = near_call(dev, near_leaves.T, near_offsets.T, pos, chg, before, after)
    potential = far_call(
        dev, coarse_lists.reshape(-1), coarse_class.reshape(-1), far_leaves.T, far_leaf_class.T,
        far_parents, far_parent_class, lt, pt, pos, near, arrived,
        by_rows(down_shift), by_rows(far_shift),
    )
    return potential.reshape(-1)


def solution(mesh):
    row = P(AXES, None)
    placed = (
        P(None, AXES), P(AXES), row, row, row, row, P(AXES, None, None), row, row,
        P(AXES, None, None), P(), P(), P(), P(), P(),
    )
    return jax.shard_map(
        per_device, mesh=mesh, in_specs=placed, out_specs=P(AXES), check_vma=False
    )
```

```python
import jax
import jax.numpy as jnp
import numpy as np
from jax import lax
from jax.experimental import pallas as pl
from jax.experimental.pallas import tpu as pltpu
from jax.sharding import PartitionSpec as P

ORDER = 10
COEF = 286
RIM = 32
LEAF = 128
K_NEAR = 27
CAP_L = 16
CAP_P = 4
ROWS = 48
PACK_MIB = 60
TARGETS = 160
GROUP = 128
NOBODY = LEAF + 2 * RIM
SOFT = 0.05 * 0.05
AXES = ("gx", "gy")
F32 = jnp.float32
BF16 = jnp.bfloat16
VMEM = pl.BlockSpec(memory_space=pltpu.VMEM)
SMEM = pl.BlockSpec(memory_space=pltpu.SMEM)
HBM = pl.BlockSpec(memory_space=pl.ANY)


def exponents(order):
    entries = []
    for degree in range(order + 1):
        for first_power in range(degree, -1, -1):
            for second_power in range(degree - first_power, -1, -1):
                entries.append((first_power, second_power, degree - first_power - second_power))
    return entries


INDEX = {powers: number for number, powers in enumerate(exponents(ORDER))}


def split(x):
    high = x.astype(BF16)
    return high, (x - high.astype(F32)).astype(BF16)


def nt(a, b):
    return lax.dot_general(a, b, (((1,), (1,)), ((), ())), preferred_element_type=F32)


def nn(a, b):
    return jnp.dot(a, b, preferred_element_type=F32)


def turn(x, left):
    return pltpu.roll(x, 128 - left, 1)


def apply_parts(operator, high, low):
    operator_high, operator_low = split(operator)
    both = nn(operator_high, jnp.concatenate([high, low], axis=1))
    return both[:, 0:128] + (both[:, 128:256] + nn(operator_low, high))


def apply_operator(operator, columns):
    return apply_parts(operator, *split(columns))


def cut(source, chunks):
    chunks[0] = source[:, 0:128]
    chunks[1] = source[:, 128:256]
    chunks[2] = jnp.zeros(chunks.shape[1:], F32)
    chunks[2, :, 0 : COEF - 256] = source[:, 256:COEF]


def chunk_at(chunks, h, number, count):
    return chunks[h, pl.ds(number, COEF, stride=count), :]


def operator_at(chunks, number, count):
    return jnp.concatenate([chunk_at(chunks, h, number, count) for h in range(3)], axis=1)


def eight_operators(chunks, numbers, count):
    parts = [
        jnp.concatenate([chunk_at(chunks, h, number, count) for h in range(2)], axis=1)
        for number in numbers
    ]
    halves = []
    for g in range(2):
        half = chunk_at(chunks, 2, numbers[4 * g], count)
        for p in range(1, 4):
            half = half + pltpu.roll(chunk_at(chunks, 2, numbers[4 * g + p], count), 32 * p, 1)
        halves.append(half)
    return parts + [jnp.concatenate(halves, axis=1)]


def eight_columns(columns):
    return [c[0:256] for c in columns] + [jnp.concatenate([c[256:288] for c in columns], axis=0)]


def apply_eight(chunks, columns, total):
    operators = eight_operators(chunks, range(8), 8)
    for operator, part in zip(operators, eight_columns(columns)):
        total = total + apply_operator(operator, part)
    return total


def upward_kernel(dev_ref, pos_ref, chg_ref, up_hbm, lt_ref, pt_ref, lift_ref, moments, column, up_ref,
                  stored_up, sem):
    copy = pltpu.make_async_copy(up_hbm, stored_up, sem)
    copy.start()
    x, y, z = [2.0 * pos_ref[d].T for d in range(3)]
    with_x = chg_ref[...].T
    z_powers = [None, z]
    for k in range(ORDER - 1):
        z_powers.append(z_powers[-1] * z)
    moments[COEF - 6 : 384, :] = jnp.zeros((384 - COEF + 6, LEAF), F32)
    for i in range(ORDER + 1):
        if i:
            with_x = with_x * x
        with_xy = with_x
        for j in range(ORDER + 1 - i):
            if j:
                with_xy = with_xy * y
            for k in range(ORDER + 1 - i - j):
                term = with_xy * z_powers[k] if k else with_xy
                a = INDEX[(i, j, k)]
                moments[a : a + 1, :] = jnp.sum(term, axis=0, keepdims=True)
    for h in range(3):
        lt_ref[h] = moments[128 * h : 128 * h + 128, :].T
    column[...] = jnp.zeros_like(column)
    copy.wait()
    cut(stored_up, up_ref)
    lane = lax.broadcasted_iota(jnp.int32, (384, 128), 1)
    leaves = moments[...]
    total = jnp.zeros((COEF, 128), F32)
    total = apply_eight(up_ref, [jnp.where(lane % 8 == c, leaves, 0.0) for c in range(8)], total)
    for left in (4, 2, 1):
        total = total + turn(total, left)
    column[0:COEF, :] = total
    parents = column[...]
    total = jnp.zeros((COEF, 128), F32)
    total = apply_eight(
        up_ref, [jnp.where(lane % 64 == 8 * c, parents, 0.0) for c in range(8)], total
    )
    for h in range(3):
        moments[0:128, :] = column[128 * h : 128 * h + 128, :].T
        pt_ref[h] = moments[pl.ds(0, 16, stride=8), :]
    for left in (8, 16, 32):
        total = total + turn(total, left)
    column[0:COEF, :] = total
    grand = column[...]
    first = lax.rem(2 * dev_ref[0], 8)
    total = apply_operator(operator_at(up_ref, first, 8), jnp.where(lane == 0, grand, 0.0))
    total = total + apply_operator(
        operator_at(up_ref, first + 1, 8), jnp.where(lane == 64, grand, 0.0)
    )
    column[0:COEF, :] = total + turn(total, 64)
    for h in range(3):
        lift_ref[h : h + 1, :] = column[128 * h : 128 * h + 128, :].T[0:1, :]


def pack_kernel(asked_ref, lt_ref, pt_ref, lift_ref, out_ref):
    for h in range(3):
        out_ref[pl.ds(45 + h, 128, stride=ROWS), :] = jnp.broadcast_to(
            lift_ref[h : h + 1, :], (128, 128)
        )
    lane = lax.broadcasted_iota(jnp.int32, (128, 128), 1)
    leaf_rows = jnp.concatenate([lt_ref[h] for h in range(3)], axis=1)
    parent_rows = jnp.concatenate([pt_ref[h] for h in range(3)], axis=1)
    parent_rows = jnp.concatenate([parent_rows, jnp.zeros((112, 384), F32)], axis=0)
    leaf_rows = jnp.concatenate(split(leaf_rows), axis=0)
    parent_rows = jnp.concatenate(split(parent_rows), axis=0)
    for q in range(5):
        tail = jnp.zeros((128, 128), F32)
        for p in range(4):
            j = 4 * q + p
            chosen = jnp.where(asked_ref[:, j : j + 1] == lane, 1.0, 0.0).astype(BF16)
            chosen = jnp.concatenate([chosen, chosen], axis=1)
            rows = nn(chosen, leaf_rows if q < 4 else parent_rows)
            out_ref[pl.ds(2 * j, 128, stride=ROWS), :] = rows[:, 0:128]
            out_ref[pl.ds(2 * j + 1, 128, stride=ROWS), :] = rows[:, 128:256]
            part = rows[:, 256:384]
            tail = tail + (pltpu.roll(part, 32 * p, 1) if p else part)
        out_ref[pl.ds(40 + q, 128, stride=ROWS), :] = tail


def near_kernel(dev_ref, leaves_ref, offsets_ref, pos_ref, chg_ref, before_ref, after_ref, out_ref,
                eight, charge, offsets, features, spread, sums, ready, lists, plan, sem):
    sub = lax.broadcasted_iota(jnp.int32, (8, 128), 0)
    named = leaves_ref[...]
    first_leaf = dev_ref[0] * LEAF
    present = named >= 0
    own_id = first_leaf + lax.broadcasted_iota(jnp.int32, (K_NEAR, LEAF), 1)
    itself = (named == own_id) & (offsets_ref[...] == 13)
    counted = present & jnp.logical_not(itself)
    code = jnp.where(counted, (named - first_leaf + RIM) * 32 + offsets_ref[...], NOBODY * 32 + 13)
    count = jnp.sum(jnp.where(present, 1.0, 0.0), axis=0, keepdims=True).astype(jnp.int32)
    quads = jnp.maximum((count + 2) // 4, 1)
    selves = jnp.sum(jnp.where(itself, 1.0, 0.0), axis=0, keepdims=True).astype(jnp.int32)
    total = jnp.sum(quads.astype(F32), axis=1, keepdims=True).astype(jnp.int32)
    lists[...] = jnp.full_like(lists, NOBODY * 32 + 13)
    lists[0:K_NEAR, :] = code
    lists[37:38, :] = quads
    lists[38:39, :] = selves
    lists[39:40, :] = jnp.broadcast_to(total, (1, 128))
    copy = pltpu.make_async_copy(lists, plan, sem)
    copy.start()
    eight[:, 3, :] = jnp.full((LEAF + 2 * RIM, 128), 1.0, F32)
    eight[:, 7, :] = jnp.full((LEAF + 2 * RIM, 128), SOFT, F32)
    eight3 = ((0, 4), (1, 5), (2, 6))
    for d in range(3):
        for row in eight3[d]:
            eight[0:RIM, row, :] = before_ref[d]
            eight[RIM : RIM + LEAF, row, :] = pos_ref[d]
            eight[RIM + LEAF : 2 * RIM + LEAF, row, :] = after_ref[d]
    charge[0:RIM, :] = before_ref[3]
    charge[RIM : RIM + LEAF, :] = chg_ref[...]
    charge[RIM + LEAF : 2 * RIM + LEAF, :] = after_ref[3]
    lane = lax.broadcasted_iota(jnp.int32, (128, 128), 1)
    features[NOBODY] = jnp.where(lane == 7, 1.0, 0.0).astype(BF16)
    spread[NOBODY] = jnp.zeros((128, 128), F32)
    for o in range(27):
        shift = (o // 9 - 1, o // 3 % 3 - 1, o % 3 - 1)
        table = jnp.zeros((8, 128), F32)
        for d in range(3):
            table = jnp.where((sub == d) | (sub == d + 4), -float(shift[d]), table)
        offsets[o] = table
    squares = (sub >= 4) & (sub < 7)

    def thirds(v):
        high = v.astype(BF16).astype(F32)
        rest = v - high
        middle = rest.astype(BF16).astype(F32)
        return high, middle, rest - middle

    def target(leaf, offset):
        v = eight[RIM + leaf] + offsets[offset]
        v = jnp.where(squares, v * v, v)
        high, middle, low = thirds(v)
        return jnp.concatenate([high, high, high, middle, middle, low], axis=0).astype(BF16)

    def separations(leaf, rows):
        padded = jnp.concatenate([rows, jnp.zeros((80, 128), BF16)], axis=0)
        return nn(features[leaf], padded)

    row = lax.broadcasted_iota(jnp.int32, (128, 128), 0)
    three = jnp.where((row >= 48) & (row < 51), 1.0, 0.0).astype(BF16)
    diagonal = row == lane
    identity = jnp.where(diagonal, 1.0, 0.0).astype(BF16)

    def source(leaf):
        v = eight[leaf]
        norm = jnp.sum(jnp.where(sub < 3, v * v, 0.0), axis=0, keepdims=True)
        v = jnp.where(sub < 3, -2.0 * v, jnp.where(sub == 3, norm, 1.0))
        high, middle, low = thirds(v)
        first, second, third = thirds(charge[pl.ds(leaf, 1), :])
        parts = jnp.where(sub == 0, first, jnp.where(sub == 1, second, jnp.where(sub == 2, third, 0.0)))
        rows = jnp.concatenate([high, middle, low, high, middle, high, parts], axis=0)
        rows = jnp.concatenate([rows, jnp.zeros((72, 128), F32)], axis=0)
        rows = rows.T.astype(BF16)
        features[leaf] = rows
        spread[leaf] = nn(rows, three)

    def prepare(step, carry):
        for u in range(48):
            source(48 * step + u)
        return carry

    lax.fori_loop(0, (LEAF + 2 * RIM) // 48, prepare, 0)
    copy.wait()

    def own_leaf(step, carry):
        for u in range(32):
            leaf = 32 * step + u
            squared = separations(RIM + leaf, target(leaf, 13))
            terms = jnp.where(diagonal, 0.0, spread[RIM + leaf] * lax.rsqrt(squared))
            sums[leaf] = jnp.sum(terms.reshape(16, 8, 128), axis=0) * plan[38, leaf].astype(F32)
        return carry

    lax.fori_loop(0, LEAF // 32, own_leaf, 0)

    def advance(state):
        leaf, quad = state
        last = quad + 1 >= plan[37, leaf]
        return (
            jnp.where(last, jnp.minimum(leaf + 1, LEAF - 1), leaf),
            jnp.where(last, jnp.where(leaf == LEAF - 1, 7, 0), quad + 1),
        )

    def produce(states):
        for g, (leaf, quad) in enumerate(states):
            for u in range(4):
                code = plan[4 * quad + u + 1, leaf]
                ready[4 * g + u] = target(leaf, code & 31)

    def consume(states):
        for g, (leaf, quad) in enumerate(states):
            part = sums[leaf]
            for u in range(4):
                code = plan[4 * quad + u + 1, leaf]
                squared = separations(code >> 5, ready[4 * g + u])
                terms = spread[code >> 5] * lax.rsqrt(squared)
                part = part + jnp.sum(terms.reshape(16, 8, 128), axis=0)
            sums[leaf] = part

    def following(state, number):
        made = []
        for _ in range(number):
            state = advance(state)
            made.append(state)
        return tuple(made)

    first = (jnp.int32(0), jnp.int32(0))
    states = (first,) + following(first, GROUP // 4 - 1)
    produce(states)

    def one_group(step, states):
        after = following(states[-1], GROUP // 4)
        consume(states)
        produce(after)
        return after

    quads = GROUP // 4
    lax.fori_loop(0, (plan[39, 0] + quads - 1) // quads, one_group, states)
    out_ref[...] = jnp.sum(sums[...], axis=1)


def count_rows(code, low, rows):
    wide = lax.broadcasted_iota(jnp.int32, (rows, 256), 0) == code
    narrow = lax.broadcasted_iota(jnp.int32, (128, 256), 0) == low
    return nt(
        jnp.where(wide, 1.0, 0.0).astype(BF16), jnp.where(narrow, 1.0, 0.0).astype(BF16)
    ).astype(BF16)


def encode(slots, classes, cells, capacity):
    ghost = jnp.maximum(slots - cells, 0)
    own = slots < cells
    code = jnp.where(own, 0, 1 + lax.rem(ghost, capacity)) * 16 + classes
    return jnp.where(slots < 0, -1, code), jnp.where(own, slots, lax.div(ghost, capacity))


def far_kernel(dev_ref, lists_ref, class_ref, leaf_ref, leaf_class_ref, parent_ref, parent_class_ref,
               lt_ref, pt_ref, pos_ref, near_ref, arrived_hbm, down_hbm, far_hbm, out_ref,
               src, src_parent, even, odd, even_parent, grouped, code_scr, low_scr, turned, column, loc,
               result, arrived_ref, down_ref, stored_down, far_ref, stored_far, sems):
    arrival, far_copy, down_copy = [
        pltpu.make_async_copy(origin, scratch, sems.at[i])
        for i, (origin, scratch) in enumerate(
            ((arrived_hbm, arrived_ref), (far_hbm, stored_far), (down_hbm, stored_down))
        )
    ]
    arrival.start()
    far_copy.start()
    down_copy.start()
    lane = lax.broadcasted_iota(jnp.int32, (128, 128), 1)

    def count(first, capacity, table_ref):
        blocks = capacity + 1
        for t in range(16):
            rows = pl.ds(first + t, 1)
            table = count_rows(code_scr[rows, :], low_scr[rows, :], 16 * blocks)
            for b in range(blocks):
                table_ref[16 * t : 16 * t + 16, 128 * b : 128 * b + 128] = table[
                    16 * b : 16 * b + 16
                ]

    def place(ref, row, parts):
        count = parts[0].shape[0]
        (h0, l0), (h1, l1) = split(parts[0]), split(parts[1])
        tail = parts[2]
        high = tail.astype(BF16).astype(F32)
        low = pltpu.roll(tail - high, 32, 1)
        ref[row : row + count, 0:128] = h0
        ref[row : row + count, 128:256] = h1
        ref[row : row + count, 256:384] = l0
        ref[row : row + count, 384:512] = l1
        ref[row : row + count, 512:640] = (high + low).astype(BF16)

    def collect(product, row, count):
        grouped[0, pl.ds(row, count), :] = product[:, 0:128] + product[:, 256:384]
        grouped[1, pl.ds(row, count), :] = product[:, 128:256] + product[:, 384:512]
        tail = product[:, 512:640]
        grouped[2, pl.ds(row, count), :] = tail + pltpu.roll(tail, 96, 1)

    def arrived_tail(row, p):
        part = arrived_ref[pl.ds(row, 128, stride=ROWS), :]
        part = pltpu.roll(part, 128 - 32 * p, 1) if p else part
        return jnp.where(lane < 32, part, 0.0)

    width = leaf_ref.shape[0]
    code_scr[...] = jnp.full_like(code_scr, -1)
    low_scr[...] = jnp.full_like(low_scr, -1)
    for part, scratch in zip(
        encode(leaf_ref[...], leaf_class_ref[...], LEAF, CAP_L), (code_scr, low_scr)
    ):
        turned[...] = jnp.full_like(turned, -1.0)
        turned[:width, :] = part.astype(F32)
        scratch[0:128, 0:128] = turned[0:128, :].T.astype(jnp.int32)
        scratch[0:128, 128:256] = turned[128:256, :].T.astype(jnp.int32)
    for part, scratch in zip(
        encode(parent_ref[...], parent_class_ref[...], 16, CAP_P), (code_scr, low_scr)
    ):
        scratch[128:144, :width] = part
    count(128, CAP_P, even_parent)
    count(0, CAP_L, even)
    place(src, 0, [lt_ref[h] for h in range(3)])
    arrival.wait()
    for c in range(CAP_L):
        place(
            src,
            128 * (c + 1),
            [arrived_ref[pl.ds(2 * c, 128, stride=ROWS), :], arrived_ref[pl.ds(2 * c + 1, 128, stride=ROWS), :], arrived_tail(40 + c // 4, c % 4)],
        )
    own = [jnp.concatenate([pt_ref[h], jnp.zeros((112, 128), F32)], axis=0) for h in range(3)]
    place(src_parent, 0, own)
    for c in range(CAP_P):
        place(
            src_parent,
            128 * (c + 1),
            [arrived_ref[pl.ds(32 + 2 * c, 128, stride=ROWS), :], arrived_ref[pl.ds(33 + 2 * c, 128, stride=ROWS), :], arrived_tail(44, c)],
        )
    collect(nn(even_parent[...], src_parent[...]), 2048, 256)
    mine = dev_ref[0] // 4
    operator = lax.broadcasted_iota(jnp.int32, (16, 128), 0)
    cell = lax.broadcasted_iota(jnp.int32, (16, 128), 1) // 4
    chosen = jnp.zeros((16, 128), F32)
    for k in range(7):
        hit = (operator == class_ref[mine * 7 + k]) & (cell == lists_ref[mine * 7 + k])
        chosen = chosen + jnp.where(hit, 1.0, 0.0)
    chosen = chosen.astype(BF16)
    for h in range(3):
        high, low = split(arrived_ref[pl.ds(45 + h, 128, stride=ROWS), :])
        grouped[h, 2304:2320, :] = nn(chosen, high) + nn(chosen, low)
        grouped[h, 2320:2560, :] = jnp.zeros((240, 128), F32)

    def two_blocks(step, carry):
        row = pl.multiple_of(step * 512, 512)
        count(32 * step + 16, CAP_L, odd)
        collect(nn(even[...], src[...]), row, 256)
        count(jnp.minimum(32 * step + 32, 112), CAP_L, even)
        collect(nn(odd[...], src[...]), row + 256, 256)
        return carry

    lax.fori_loop(0, 4, two_blocks, 0)

    far_copy.wait()
    cut(stored_far, far_ref)
    column[...] = jnp.zeros_like(column)
    loc[...] = jnp.zeros_like(loc)
    tall = lax.broadcasted_iota(jnp.int32, (384, 128), 1)
    leaf_total = jnp.zeros((COEF, 128), F32)
    upper_total = jnp.zeros((COEF, 128), F32)
    for half in range(2):
        numbers = range(8 * half, 8 * half + 8)
        uppers = []
        for q in (2 * half, 2 * half + 1):
            upper = jnp.concatenate(
                [
                    jnp.concatenate(
                        [grouped[h, pl.ds(2048 + 4 * q + p, 32, stride=16), :] for p in range(4)],
                        axis=0,
                    ).T
                    for h in range(3)
                ],
                axis=0,
            )
            uppers += [jnp.where(tall // 32 == p, upper, 0.0) for p in range(4)]
        leaves = [
            jnp.concatenate([grouped[h, pl.ds(o, 128, stride=16), :].T for h in range(3)], axis=0)
            for o in numbers
        ]
        for operator, leaf, upper in zip(
            eight_operators(far_ref, numbers, 16), eight_columns(leaves), eight_columns(uppers)
        ):
            operator_high, operator_low = split(operator)
            leaf_high, leaf_low = split(leaf)
            upper_high, upper_low = split(upper)
            first = nn(operator_high, jnp.concatenate([leaf_high, leaf_low], axis=1))
            second = nn(operator_high, jnp.concatenate([upper_high, upper_low], axis=1))
            third = nn(operator_low, jnp.concatenate([leaf_high, upper_high], axis=1))
            leaf_total = leaf_total + (first[:, 0:128] + (first[:, 128:256] + third[:, 0:128]))
            upper_total = upper_total + (
                second[:, 0:128] + (second[:, 128:256] + third[:, 128:256])
            )
    upper_total = upper_total + turn(upper_total, 32)
    upper_total = upper_total + turn(upper_total, 64)
    down_copy.wait()
    cut(stored_down, down_ref)
    column[0:COEF, :] = upper_total
    coarse = jnp.broadcast_to(column[:, 16:17], (384, 128))
    first = lax.rem(2 * dev_ref[0], 8)
    grand = apply_operator(operator_at(down_ref, first, 8), jnp.where(tall < 8, coarse, 0.0))
    grand = grand + apply_operator(
        operator_at(down_ref, first + 1, 8), jnp.where((tall >= 8) & (tall < 16), coarse, 0.0)
    )
    loc[0:COEF, :] = grand
    grand = loc[...]
    upper_total = apply_eight(
        down_ref,
        [jnp.where((tall % 8 == c) & (tall < 16), grand, 0.0) for c in range(8)],
        upper_total,
    )
    column[0:COEF, :] = upper_total
    parents = split(jnp.where(tall < 16, column[...], 0.0))
    repeat = lax.broadcasted_iota(jnp.int32, (128, 128), 0) == lane // 8
    repeat = jnp.where(repeat, 1.0, 0.0).astype(BF16)
    parents = [nn(part, repeat) for part in parents]
    high, low = [
        eight_columns([jnp.where(tall % 8 == c, part, 0.0) for c in range(8)]) for part in parents
    ]
    for operator, high_part, low_part in zip(eight_operators(down_ref, range(8), 8), high, low):
        leaf_total = leaf_total + apply_parts(operator, high_part.astype(BF16), low_part.astype(BF16))
    loc[0:COEF, :] = leaf_total
    x_all, y_all, z_all = [2.0 * pos_ref[d].T for d in range(3)]
    for part in range(2):
        piece = slice(64 * part, 64 * part + 64)
        x, y, z = x_all[piece], y_all[piece], z_all[piece]
        over_i = None
        for i in range(ORDER, -1, -1):
            over_j = None
            for j in range(ORDER - i, -1, -1):
                over_k = None
                for k in range(ORDER - i - j, -1, -1):
                    a = INDEX[(i, j, k)]
                    value = loc[a : a + 1, :]
                    over_k = value if over_k is None else over_k * z + value
                over_j = over_k if over_j is None else over_j * y + over_k
            over_i = over_j if over_i is None else over_i * x + over_j
        result[piece, :] = over_i
    out_ref[...] = near_ref[...] + result[...].T


def cost(flops, moved):
    return pl.CostEstimate(flops=flops, bytes_accessed=moved, transcendentals=0)


def shape(*dims, dtype=F32):
    return jax.ShapeDtypeStruct(dims, dtype)


def limits(mib):
    return pltpu.CompilerParams(vmem_limit_bytes=mib * 1024 * 1024)


def upward_call(dev, pos, chg, up_shift):
    return pl.pallas_call(
        upward_kernel,
        out_shape=(shape(3, 128, 128), shape(3, 16, 128), shape(3, 128)),
        in_specs=[SMEM] + [VMEM] * 2 + [HBM],
        out_specs=(VMEM, VMEM, VMEM),
        scratch_shapes=[
            pltpu.VMEM((384, 128), F32),
            pltpu.VMEM((384, 128), F32),
            pltpu.VMEM((3, 8 * COEF, 128), F32),
            pltpu.VMEM((8 * COEF, COEF), F32),
            pltpu.SemaphoreType.DMA(()),
        ],
        compiler_params=limits(60),
        cost_estimate=cost(8 * 10**9, 3 * 10**6),
        name="upward",
    )(dev, pos, chg, up_shift)


def pack_call(asked, lt, pt, lift):
    return pl.pallas_call(
        pack_kernel,
        out_shape=shape(128 * ROWS, 128),
        in_specs=[VMEM] * 4,
        out_specs=VMEM,
        compiler_params=limits(PACK_MIB),
        cost_estimate=cost(10**9, 4 * 10**6),
        name="pack",
    )(asked, lt, pt, lift)


def near_call(dev, near_leaves, near_offsets, pos, chg, before, after):
    return pl.pallas_call(
        near_kernel,
        out_shape=shape(128, 128),
        in_specs=[SMEM] + [VMEM] * 6,
        out_specs=VMEM,
        scratch_shapes=[
            pltpu.VMEM((LEAF + 2 * RIM, 8, 128), F32),
            pltpu.VMEM((LEAF + 2 * RIM, 128), F32),
            pltpu.VMEM((27, 8, 128), F32),
            pltpu.VMEM((NOBODY + 1, 128, 128), BF16),
            pltpu.VMEM((NOBODY + 1, 128, 128), F32),
            pltpu.VMEM((LEAF, 8, 128), F32),
            pltpu.VMEM((GROUP, 48, 128), BF16),
            pltpu.VMEM((40, 128), jnp.int32),
            pltpu.SMEM((40, 128), jnp.int32),
            pltpu.SemaphoreType.DMA(()),
        ],
        compiler_params=limits(60),
        cost_estimate=cost(30 * 10**9, 10**6),
        name="near",
    )(dev, near_leaves, near_offsets, pos, chg, before, after)


def far_call(dev, lists, classes, leaves, leaf_class, parents, parent_class, lt, pt, pos, near, arrived,
             down_shift, far_shift):
    return pl.pallas_call(
        far_kernel,
        out_shape=shape(128, 128),
        in_specs=[SMEM] * 3 + [VMEM] * 8 + [HBM] * 3,
        out_specs=VMEM,
        scratch_shapes=[
            pltpu.VMEM((2176, 640), BF16),
            pltpu.VMEM((640, 640), BF16),
            pltpu.VMEM((256, 2176), BF16),
            pltpu.VMEM((256, 2176), BF16),
            pltpu.VMEM((256, 640), BF16),
            pltpu.VMEM((3, 16 * TARGETS, 128), F32),
            pltpu.VMEM((144, 256), jnp.int32),
            pltpu.VMEM((144, 256), jnp.int32),
            pltpu.VMEM((256, 128), F32),
            pltpu.VMEM((384, 128), F32),
            pltpu.VMEM((384, 128), F32),
            pltpu.VMEM((128, 128), F32),
            pltpu.VMEM((128 * ROWS, 128), F32),
            pltpu.VMEM((3, 8 * COEF, 128), F32),
            pltpu.VMEM((8 * COEF, COEF), F32),
            pltpu.VMEM((3, 16 * COEF, 128), F32),
            pltpu.VMEM((16 * COEF, COEF), F32),
            pltpu.SemaphoreType.DMA((3,)),
        ],
        compiler_params=limits(60),
        cost_estimate=cost(20 * 10**9, 20 * 10**6),
        name="far",
    )(dev, lists, classes, leaves, leaf_class, parents, parent_class, lt, pt, pos, near, arrived,
      down_shift, far_shift)


def by_rows(operators):
    return jnp.swapaxes(operators, 0, 1).reshape(-1, operators.shape[2])


def per_device(
    positions,
    charges,
    near_leaves,
    near_offsets,
    far_leaves,
    far_leaf_class,
    leaf_plan,
    far_parents,
    far_parent_class,
    parent_plan,
    coarse_lists,
    coarse_class,
    up_shift,
    down_shift,
    far_shift,
):
    device = lax.axis_index(AXES)
    dev = device.reshape(1).astype(jnp.int32)
    plans = jnp.concatenate([leaf_plan[0], parent_plan[0]], 1)
    asked = lax.all_to_all(plans, AXES, split_axis=0, concat_axis=0, tiled=True)
    pos = positions.reshape(3, LEAF, 128)
    chg = charges.reshape(LEAF, 128)
    rims = [
        jnp.concatenate([pos[:, rows], chg[None, rows]], 0)
        for rows in (slice(LEAF - RIM, LEAF), slice(0, RIM))
    ]
    size = lax.axis_size(AXES)
    up = [(i, i + 1) for i in range(size - 1)]
    down = [(j, i) for i, j in up]
    before = lax.ppermute(rims[0], AXES, up)
    after = lax.ppermute(rims[1], AXES, down)
    lt, pt, lift = upward_call(dev, pos, chg, by_rows(up_shift))
    before, after, asked, lt = lax.optimization_barrier((before, after, asked, lt))
    outgoing = pack_call(asked, lt, pt, lift)
    outgoing = outgoing.reshape(LEAF, ROWS, 128)
    near_leaves, outgoing = lax.optimization_barrier((near_leaves, outgoing))
    arrived = lax.all_to_all(outgoing, AXES, split_axis=0, concat_axis=0, tiled=True)
    arrived = arrived.reshape(LEAF * ROWS, 128)
    near = near_call(dev, near_leaves.T, near_offsets.T, pos, chg, before, after)
    potential = far_call(
        dev, coarse_lists.reshape(-1), coarse_class.reshape(-1), far_leaves.T, far_leaf_class.T,
        far_parents, far_parent_class, lt, pt, pos, near, arrived,
        by_rows(down_shift), by_rows(far_shift),
    )
    return potential.reshape(-1)


def solution(mesh):
    row = P(AXES, None)
    placed = (
        P(None, AXES), P(AXES), row, row, row, row, P(AXES, None, None), row, row,
        P(AXES, None, None), P(), P(), P(), P(), P(),
    )
    return jax.shard_map(
        per_device, mesh=mesh, in_specs=placed, out_specs=P(AXES), check_vma=False
    )
```

```python
import jax
import jax.numpy as jnp
import numpy as np
from jax import lax
from jax.experimental import pallas as pl
from jax.experimental.pallas import tpu as pltpu
from jax.sharding import PartitionSpec as P

ORDER = 10
COEF = 286
RIM = 32
LEAF = 128
K_NEAR = 27
CAP_L = 16
CAP_P = 4
ROWS = 48
PACK_MIB = 24
TARGETS = 160
GROUP = 128
NOBODY = LEAF + 2 * RIM
SOFT = 0.05 * 0.05
AXES = ("gx", "gy")
F32 = jnp.float32
BF16 = jnp.bfloat16
VMEM = pl.BlockSpec(memory_space=pltpu.VMEM)
SMEM = pl.BlockSpec(memory_space=pltpu.SMEM)
HBM = pl.BlockSpec(memory_space=pl.ANY)


def exponents(order):
    entries = []
    for degree in range(order + 1):
        for first_power in range(degree, -1, -1):
            for second_power in range(degree - first_power, -1, -1):
                entries.append((first_power, second_power, degree - first_power - second_power))
    return entries


INDEX = {powers: number for number, powers in enumerate(exponents(ORDER))}


def split(x):
    high = x.astype(BF16)
    return high, (x - high.astype(F32)).astype(BF16)


def nt(a, b):
    return lax.dot_general(a, b, (((1,), (1,)), ((), ())), preferred_element_type=F32)


def nn(a, b):
    return jnp.dot(a, b, preferred_element_type=F32)


def turn(x, left):
    return pltpu.roll(x, 128 - left, 1)


def apply_parts(operator, high, low):
    operator_high, operator_low = split(operator)
    both = nn(operator_high, jnp.concatenate([high, low], axis=1))
    return both[:, 0:128] + (both[:, 128:256] + nn(operator_low, high))


def apply_operator(operator, columns):
    return apply_parts(operator, *split(columns))


def pieces(origin, scratch, sems, first):
    rows = scratch.shape[0]
    size = (rows // 4 + 7) // 8 * 8
    return [
        pltpu.make_async_copy(
            origin.at[pl.ds(size * i, min(size, rows - size * i))],
            scratch.at[pl.ds(size * i, min(size, rows - size * i))],
            sems.at[first + i],
        )
        for i in range(4)
    ]


def start(copies):
    for copy in copies:
        copy.start()


def wait(copies):
    for copy in copies:
        copy.wait()


def cut(source, chunks):
    chunks[0] = source[:, 0:128]
    chunks[1] = source[:, 128:256]
    chunks[2] = jnp.zeros(chunks.shape[1:], F32)
    chunks[2, :, 0 : COEF - 256] = source[:, 256:COEF]


def chunk_at(chunks, h, number, count):
    return chunks[h, pl.ds(number, COEF, stride=count), :]


def operator_at(chunks, number, count):
    return jnp.concatenate([chunk_at(chunks, h, number, count) for h in range(3)], axis=1)


def eight_operators(chunks, numbers, count):
    parts = [
        jnp.concatenate([chunk_at(chunks, h, number, count) for h in range(2)], axis=1)
        for number in numbers
    ]
    halves = []
    for g in range(2):
        half = chunk_at(chunks, 2, numbers[4 * g], count)
        for p in range(1, 4):
            half = half + pltpu.roll(chunk_at(chunks, 2, numbers[4 * g + p], count), 32 * p, 1)
        halves.append(half)
    return parts + [jnp.concatenate(halves, axis=1)]


def eight_columns(columns):
    return [c[0:256] for c in columns] + [jnp.concatenate([c[256:288] for c in columns], axis=0)]


def apply_eight(chunks, columns, total):
    operators = eight_operators(chunks, range(8), 8)
    for operator, part in zip(operators, eight_columns(columns)):
        total = total + apply_operator(operator, part)
    return total


def upward_kernel(dev_ref, pos_ref, chg_ref, up_hbm, lt_ref, pt_ref, lift_ref, moments, column, up_ref,
                  stored_up, sems):
    copies = pieces(up_hbm, stored_up, sems, 0)
    start(copies)
    x, y, z = [2.0 * pos_ref[d].T for d in range(3)]
    with_x = chg_ref[...].T
    z_powers = [None, z]
    for k in range(ORDER - 1):
        z_powers.append(z_powers[-1] * z)
    moments[COEF - 6 : 384, :] = jnp.zeros((384 - COEF + 6, LEAF), F32)
    for i in range(ORDER + 1):
        if i:
            with_x = with_x * x
        with_xy = with_x
        for j in range(ORDER + 1 - i):
            if j:
                with_xy = with_xy * y
            for k in range(ORDER + 1 - i - j):
                term = with_xy * z_powers[k] if k else with_xy
                a = INDEX[(i, j, k)]
                moments[a : a + 1, :] = jnp.sum(term, axis=0, keepdims=True)
    for h in range(3):
        lt_ref[h] = moments[128 * h : 128 * h + 128, :].T
    column[...] = jnp.zeros_like(column)
    wait(copies)
    cut(stored_up, up_ref)
    lane = lax.broadcasted_iota(jnp.int32, (384, 128), 1)
    leaves = moments[...]
    total = jnp.zeros((COEF, 128), F32)
    total = apply_eight(up_ref, [jnp.where(lane % 8 == c, leaves, 0.0) for c in range(8)], total)
    for left in (4, 2, 1):
        total = total + turn(total, left)
    column[0:COEF, :] = total
    parents = column[...]
    total = jnp.zeros((COEF, 128), F32)
    total = apply_eight(
        up_ref, [jnp.where(lane % 64 == 8 * c, parents, 0.0) for c in range(8)], total
    )
    for h in range(3):
        moments[0:128, :] = column[128 * h : 128 * h + 128, :].T
        pt_ref[h] = moments[pl.ds(0, 16, stride=8), :]
    for left in (8, 16, 32):
        total = total + turn(total, left)
    column[0:COEF, :] = total
    grand = column[...]
    first = lax.rem(2 * dev_ref[0], 8)
    total = apply_operator(operator_at(up_ref, first, 8), jnp.where(lane == 0, grand, 0.0))
    total = total + apply_operator(
        operator_at(up_ref, first + 1, 8), jnp.where(lane == 64, grand, 0.0)
    )
    column[0:COEF, :] = total + turn(total, 64)
    for h in range(3):
        lift_ref[h : h + 1, :] = column[128 * h : 128 * h + 128, :].T[0:1, :]


def pack_kernel(asked_ref, lt_ref, pt_ref, lift_ref, out_ref):
    for h in range(3):
        out_ref[pl.ds(45 + h, 128, stride=ROWS), :] = jnp.broadcast_to(
            lift_ref[h : h + 1, :], (128, 128)
        )
    lane = lax.broadcasted_iota(jnp.int32, (128, 128), 1)
    leaf_rows = jnp.concatenate([lt_ref[h] for h in range(3)], axis=1)
    parent_rows = jnp.concatenate([pt_ref[h] for h in range(3)], axis=1)
    parent_rows = jnp.concatenate([parent_rows, jnp.zeros((112, 384), F32)], axis=0)
    leaf_rows = jnp.concatenate(split(leaf_rows), axis=0)
    parent_rows = jnp.concatenate(split(parent_rows), axis=0)
    for q in range(5):
        tail = jnp.zeros((128, 128), F32)
        for p in range(4):
            j = 4 * q + p
            chosen = jnp.where(asked_ref[:, j : j + 1] == lane, 1.0, 0.0).astype(BF16)
            chosen = jnp.concatenate([chosen, chosen], axis=1)
            rows = nn(chosen, leaf_rows if q < 4 else parent_rows)
            out_ref[pl.ds(2 * j, 128, stride=ROWS), :] = rows[:, 0:128]
            out_ref[pl.ds(2 * j + 1, 128, stride=ROWS), :] = rows[:, 128:256]
            part = rows[:, 256:384]
            tail = tail + (pltpu.roll(part, 32 * p, 1) if p else part)
        out_ref[pl.ds(40 + q, 128, stride=ROWS), :] = tail


def near_kernel(dev_ref, leaves_ref, offsets_ref, pos_ref, chg_ref, before_ref, after_ref, out_ref,
                eight, charge, offsets, features, spread, sums, ready, lists, plan, sem):
    sub = lax.broadcasted_iota(jnp.int32, (8, 128), 0)
    named = leaves_ref[...]
    first_leaf = dev_ref[0] * LEAF
    present = named >= 0
    own_id = first_leaf + lax.broadcasted_iota(jnp.int32, (K_NEAR, LEAF), 1)
    itself = (named == own_id) & (offsets_ref[...] == 13)
    counted = present & jnp.logical_not(itself)
    code = jnp.where(counted, (named - first_leaf + RIM) * 32 + offsets_ref[...], NOBODY * 32 + 13)
    count = jnp.sum(jnp.where(present, 1.0, 0.0), axis=0, keepdims=True).astype(jnp.int32)
    quads = jnp.maximum((count + 2) // 4, 1)
    selves = jnp.sum(jnp.where(itself, 1.0, 0.0), axis=0, keepdims=True).astype(jnp.int32)
    total = jnp.sum(quads.astype(F32), axis=1, keepdims=True).astype(jnp.int32)
    lists[...] = jnp.full_like(lists, NOBODY * 32 + 13)
    lists[0:K_NEAR, :] = code
    lists[37:38, :] = quads
    lists[38:39, :] = selves
    lists[39:40, :] = jnp.broadcast_to(total, (1, 128))
    copy = pltpu.make_async_copy(lists, plan, sem)
    copy.start()
    eight[:, 3, :] = jnp.full((LEAF + 2 * RIM, 128), 1.0, F32)
    eight[:, 7, :] = jnp.full((LEAF + 2 * RIM, 128), SOFT, F32)
    eight3 = ((0, 4), (1, 5), (2, 6))
    for d in range(3):
        for row in eight3[d]:
            eight[0:RIM, row, :] = before_ref[d]
            eight[RIM : RIM + LEAF, row, :] = pos_ref[d]
            eight[RIM + LEAF : 2 * RIM + LEAF, row, :] = after_ref[d]
    charge[0:RIM, :] = before_ref[3]
    charge[RIM : RIM + LEAF, :] = chg_ref[...]
    charge[RIM + LEAF : 2 * RIM + LEAF, :] = after_ref[3]
    lane = lax.broadcasted_iota(jnp.int32, (128, 128), 1)
    features[NOBODY] = jnp.where(lane == 7, 1.0, 0.0).astype(BF16)
    spread[NOBODY] = jnp.zeros((128, 128), F32)
    for o in range(27):
        shift = (o // 9 - 1, o // 3 % 3 - 1, o % 3 - 1)
        table = jnp.zeros((8, 128), F32)
        for d in range(3):
            table = jnp.where((sub == d) | (sub == d + 4), -float(shift[d]), table)
        offsets[o] = table
    squares = (sub >= 4) & (sub < 7)

    def thirds(v):
        high = v.astype(BF16).astype(F32)
        rest = v - high
        middle = rest.astype(BF16).astype(F32)
        return high, middle, rest - middle

    def target(leaf, offset):
        v = eight[RIM + leaf] + offsets[offset]
        v = jnp.where(squares, v * v, v)
        high, middle, low = thirds(v)
        return jnp.concatenate([high, high, high, middle, middle, low], axis=0).astype(BF16)

    def separations(leaf, rows):
        padded = jnp.concatenate([rows, jnp.zeros((80, 128), BF16)], axis=0)
        return nn(features[leaf], padded)

    row = lax.broadcasted_iota(jnp.int32, (128, 128), 0)
    three = jnp.where((row >= 48) & (row < 51), 1.0, 0.0).astype(BF16)
    diagonal = row == lane
    identity = jnp.where(diagonal, 1.0, 0.0).astype(BF16)

    def source(leaf):
        v = eight[leaf]
        norm = jnp.sum(jnp.where(sub < 3, v * v, 0.0), axis=0, keepdims=True)
        v = jnp.where(sub < 3, -2.0 * v, jnp.where(sub == 3, norm, 1.0))
        high, middle, low = thirds(v)
        first, second, third = thirds(charge[pl.ds(leaf, 1), :])
        parts = jnp.where(sub == 0, first, jnp.where(sub == 1, second, jnp.where(sub == 2, third, 0.0)))
        rows = jnp.concatenate([high, middle, low, high, middle, high, parts], axis=0)
        rows = jnp.concatenate([rows, jnp.zeros((72, 128), F32)], axis=0)
        rows = rows.T.astype(BF16)
        features[leaf] = rows
        spread[leaf] = nn(rows, three)

    def prepare(step, carry):
        for u in range(48):
            source(48 * step + u)
        return carry

    lax.fori_loop(0, (LEAF + 2 * RIM) // 48, prepare, 0)
    copy.wait()

    def own_leaf(step, carry):
        for u in range(32):
            leaf = 32 * step + u
            squared = separations(RIM + leaf, target(leaf, 13))
            terms = jnp.where(diagonal, 0.0, spread[RIM + leaf] * lax.rsqrt(squared))
            sums[leaf] = jnp.sum(terms.reshape(16, 8, 128), axis=0) * plan[38, leaf].astype(F32)
        return carry

    lax.fori_loop(0, LEAF // 32, own_leaf, 0)

    def advance(state):
        leaf, quad = state
        last = quad + 1 >= plan[37, leaf]
        return (
            jnp.where(last, jnp.minimum(leaf + 1, LEAF - 1), leaf),
            jnp.where(last, jnp.where(leaf == LEAF - 1, 7, 0), quad + 1),
        )

    def produce(states):
        for g, (leaf, quad) in enumerate(states):
            for u in range(4):
                code = plan[4 * quad + u + 1, leaf]
                ready[4 * g + u] = target(leaf, code & 31)

    def consume(states):
        for g, (leaf, quad) in enumerate(states):
            part = sums[leaf]
            for u in range(4):
                code = plan[4 * quad + u + 1, leaf]
                squared = separations(code >> 5, ready[4 * g + u])
                terms = spread[code >> 5] * lax.rsqrt(squared)
                part = part + jnp.sum(terms.reshape(16, 8, 128), axis=0)
            sums[leaf] = part

    def following(state, number):
        made = []
        for _ in range(number):
            state = advance(state)
            made.append(state)
        return tuple(made)

    first = (jnp.int32(0), jnp.int32(0))
    states = (first,) + following(first, GROUP // 4 - 1)
    produce(states)

    def one_group(step, states):
        after = following(states[-1], GROUP // 4)
        consume(states)
        produce(after)
        return after

    quads = GROUP // 4
    lax.fori_loop(0, (plan[39, 0] + quads - 1) // quads, one_group, states)
    out_ref[...] = jnp.sum(sums[...], axis=1)


def count_rows(code, low, rows):
    wide = lax.broadcasted_iota(jnp.int32, (rows, 256), 0) == code
    narrow = lax.broadcasted_iota(jnp.int32, (128, 256), 0) == low
    return nt(
        jnp.where(wide, 1.0, 0.0).astype(BF16), jnp.where(narrow, 1.0, 0.0).astype(BF16)
    ).astype(BF16)


def encode(slots, classes, cells, capacity):
    ghost = jnp.maximum(slots - cells, 0)
    own = slots < cells
    code = jnp.where(own, 0, 1 + lax.rem(ghost, capacity)) * 16 + classes
    return jnp.where(slots < 0, -1, code), jnp.where(own, slots, lax.div(ghost, capacity))


def far_kernel(dev_ref, lists_ref, class_ref, leaf_ref, leaf_class_ref, parent_ref, parent_class_ref,
               lt_ref, pt_ref, pos_ref, near_ref, arrived_ref, down_hbm, far_hbm, out_ref,
               src, src_parent, even, odd, even_parent, grouped, code_scr, low_scr, turned, column, loc,
               result, down_ref, stored_down, far_ref, stored_far, sems):
    far_copies = pieces(far_hbm, stored_far, sems, 0)
    down_copies = pieces(down_hbm, stored_down, sems, 4)
    start(far_copies)
    start(down_copies)
    lane = lax.broadcasted_iota(jnp.int32, (128, 128), 1)

    def count(first, capacity, table_ref):
        blocks = capacity + 1
        for t in range(16):
            rows = pl.ds(first + t, 1)
            table = count_rows(code_scr[rows, :], low_scr[rows, :], 16 * blocks)
            for b in range(blocks):
                table_ref[16 * t : 16 * t + 16, 128 * b : 128 * b + 128] = table[
                    16 * b : 16 * b + 16
                ]

    def place(ref, row, parts):
        count = parts[0].shape[0]
        (h0, l0), (h1, l1) = split(parts[0]), split(parts[1])
        tail = parts[2]
        high = tail.astype(BF16).astype(F32)
        low = pltpu.roll(tail - high, 32, 1)
        ref[row : row + count, 0:128] = h0
        ref[row : row + count, 128:256] = h1
        ref[row : row + count, 256:384] = l0
        ref[row : row + count, 384:512] = l1
        ref[row : row + count, 512:640] = (high + low).astype(BF16)

    def collect(product, row, count):
        grouped[0, pl.ds(row, count), :] = product[:, 0:128] + product[:, 256:384]
        grouped[1, pl.ds(row, count), :] = product[:, 128:256] + product[:, 384:512]
        tail = product[:, 512:640]
        grouped[2, pl.ds(row, count), :] = tail + pltpu.roll(tail, 96, 1)

    def arrived_tail(row, p):
        part = arrived_ref[pl.ds(row, 128, stride=ROWS), :]
        part = pltpu.roll(part, 128 - 32 * p, 1) if p else part
        return jnp.where(lane < 32, part, 0.0)

    width = leaf_ref.shape[0]
    code_scr[...] = jnp.full_like(code_scr, -1)
    low_scr[...] = jnp.full_like(low_scr, -1)
    for part, scratch in zip(
        encode(leaf_ref[...], leaf_class_ref[...], LEAF, CAP_L), (code_scr, low_scr)
    ):
        turned[...] = jnp.full_like(turned, -1.0)
        turned[:width, :] = part.astype(F32)
        scratch[0:128, 0:128] = turned[0:128, :].T.astype(jnp.int32)
        scratch[0:128, 128:256] = turned[128:256, :].T.astype(jnp.int32)
    for part, scratch in zip(
        encode(parent_ref[...], parent_class_ref[...], 16, CAP_P), (code_scr, low_scr)
    ):
        scratch[128:144, :width] = part
    count(128, CAP_P, even_parent)
    count(0, CAP_L, even)
    place(src, 0, [lt_ref[h] for h in range(3)])
    for c in range(CAP_L):
        place(
            src,
            128 * (c + 1),
            [arrived_ref[pl.ds(2 * c, 128, stride=ROWS), :], arrived_ref[pl.ds(2 * c + 1, 128, stride=ROWS), :], arrived_tail(40 + c // 4, c % 4)],
        )
    own = [jnp.concatenate([pt_ref[h], jnp.zeros((112, 128), F32)], axis=0) for h in range(3)]
    place(src_parent, 0, own)
    for c in range(CAP_P):
        place(
            src_parent,
            128 * (c + 1),
            [arrived_ref[pl.ds(32 + 2 * c, 128, stride=ROWS), :], arrived_ref[pl.ds(33 + 2 * c, 128, stride=ROWS), :], arrived_tail(44, c)],
        )
    collect(nn(even_parent[...], src_parent[...]), 2048, 256)
    mine = dev_ref[0] // 4
    operator = lax.broadcasted_iota(jnp.int32, (16, 128), 0)
    cell = lax.broadcasted_iota(jnp.int32, (16, 128), 1) // 4
    chosen = jnp.zeros((16, 128), F32)
    for k in range(7):
        hit = (operator == class_ref[mine * 7 + k]) & (cell == lists_ref[mine * 7 + k])
        chosen = chosen + jnp.where(hit, 1.0, 0.0)
    chosen = chosen.astype(BF16)
    for h in range(3):
        high, low = split(arrived_ref[pl.ds(45 + h, 128, stride=ROWS), :])
        grouped[h, 2304:2320, :] = nn(chosen, high) + nn(chosen, low)
        grouped[h, 2320:2560, :] = jnp.zeros((240, 128), F32)

    def two_blocks(step, carry):
        row = pl.multiple_of(step * 512, 512)
        count(32 * step + 16, CAP_L, odd)
        collect(nn(even[...], src[...]), row, 256)
        count(jnp.minimum(32 * step + 32, 112), CAP_L, even)
        collect(nn(odd[...], src[...]), row + 256, 256)
        return carry

    lax.fori_loop(0, 4, two_blocks, 0)

    wait(far_copies)
    cut(stored_far, far_ref)
    column[...] = jnp.zeros_like(column)
    loc[...] = jnp.zeros_like(loc)
    tall = lax.broadcasted_iota(jnp.int32, (384, 128), 1)
    leaf_total = jnp.zeros((COEF, 128), F32)
    upper_total = jnp.zeros((COEF, 128), F32)
    for half in range(2):
        numbers = range(8 * half, 8 * half + 8)
        uppers = []
        for q in (2 * half, 2 * half + 1):
            upper = jnp.concatenate(
                [
                    jnp.concatenate(
                        [grouped[h, pl.ds(2048 + 4 * q + p, 32, stride=16), :] for p in range(4)],
                        axis=0,
                    ).T
                    for h in range(3)
                ],
                axis=0,
            )
            uppers += [jnp.where(tall // 32 == p, upper, 0.0) for p in range(4)]
        leaves = [
            jnp.concatenate([grouped[h, pl.ds(o, 128, stride=16), :].T for h in range(3)], axis=0)
            for o in numbers
        ]
        for operator, leaf, upper in zip(
            eight_operators(far_ref, numbers, 16), eight_columns(leaves), eight_columns(uppers)
        ):
            operator_high, operator_low = split(operator)
            leaf_high, leaf_low = split(leaf)
            upper_high, upper_low = split(upper)
            first = nn(operator_high, jnp.concatenate([leaf_high, leaf_low], axis=1))
            second = nn(operator_high, jnp.concatenate([upper_high, upper_low], axis=1))
            third = nn(operator_low, jnp.concatenate([leaf_high, upper_high], axis=1))
            leaf_total = leaf_total + (first[:, 0:128] + (first[:, 128:256] + third[:, 0:128]))
            upper_total = upper_total + (
                second[:, 0:128] + (second[:, 128:256] + third[:, 128:256])
            )
    upper_total = upper_total + turn(upper_total, 32)
    upper_total = upper_total + turn(upper_total, 64)
    wait(down_copies)
    cut(stored_down, down_ref)
    column[0:COEF, :] = upper_total
    coarse = jnp.broadcast_to(column[:, 16:17], (384, 128))
    first = lax.rem(2 * dev_ref[0], 8)
    grand = apply_operator(operator_at(down_ref, first, 8), jnp.where(tall < 8, coarse, 0.0))
    grand = grand + apply_operator(
        operator_at(down_ref, first + 1, 8), jnp.where((tall >= 8) & (tall < 16), coarse, 0.0)
    )
    loc[0:COEF, :] = grand
    grand = loc[...]
    upper_total = apply_eight(
        down_ref,
        [jnp.where((tall % 8 == c) & (tall < 16), grand, 0.0) for c in range(8)],
        upper_total,
    )
    column[0:COEF, :] = upper_total
    parents = split(jnp.where(tall < 16, column[...], 0.0))
    repeat = lax.broadcasted_iota(jnp.int32, (128, 128), 0) == lane // 8
    repeat = jnp.where(repeat, 1.0, 0.0).astype(BF16)
    parents = [nn(part, repeat) for part in parents]
    high, low = [
        eight_columns([jnp.where(tall % 8 == c, part, 0.0) for c in range(8)]) for part in parents
    ]
    for operator, high_part, low_part in zip(eight_operators(down_ref, range(8), 8), high, low):
        leaf_total = leaf_total + apply_parts(operator, high_part.astype(BF16), low_part.astype(BF16))
    loc[0:COEF, :] = leaf_total
    x_all, y_all, z_all = [2.0 * pos_ref[d].T for d in range(3)]
    for part in range(2):
        piece = slice(64 * part, 64 * part + 64)
        x, y, z = x_all[piece], y_all[piece], z_all[piece]
        over_i = None
        for i in range(ORDER, -1, -1):
            over_j = None
            for j in range(ORDER - i, -1, -1):
                over_k = None
                for k in range(ORDER - i - j, -1, -1):
                    a = INDEX[(i, j, k)]
                    value = loc[a : a + 1, :]
                    over_k = value if over_k is None else over_k * z + value
                over_j = over_k if over_j is None else over_j * y + over_k
            over_i = over_j if over_i is None else over_i * x + over_j
        result[piece, :] = over_i
    out_ref[...] = near_ref[...] + result[...].T


def cost(flops, moved):
    return pl.CostEstimate(flops=flops, bytes_accessed=moved, transcendentals=0)


def shape(*dims, dtype=F32):
    return jax.ShapeDtypeStruct(dims, dtype)


def limits(mib):
    return pltpu.CompilerParams(vmem_limit_bytes=mib * 1024 * 1024)


def upward_call(dev, pos, chg, up_shift):
    return pl.pallas_call(
        upward_kernel,
        out_shape=(shape(3, 128, 128), shape(3, 16, 128), shape(3, 128)),
        in_specs=[SMEM] + [VMEM] * 2 + [HBM],
        out_specs=(VMEM, VMEM, VMEM),
        scratch_shapes=[
            pltpu.VMEM((384, 128), F32),
            pltpu.VMEM((384, 128), F32),
            pltpu.VMEM((3, 8 * COEF, 128), F32),
            pltpu.VMEM((8 * COEF, COEF), F32),
            pltpu.SemaphoreType.DMA((4,)),
        ],
        compiler_params=limits(40),
        cost_estimate=cost(8 * 10**9, 3 * 10**6),
        name="upward",
    )(dev, pos, chg, up_shift)


def pack_call(asked, lt, pt, lift):
    return pl.pallas_call(
        pack_kernel,
        out_shape=shape(128 * ROWS, 128),
        in_specs=[VMEM] * 4,
        out_specs=VMEM,
        compiler_params=limits(PACK_MIB),
        cost_estimate=cost(10**9, 4 * 10**6),
        name="pack",
    )(asked, lt, pt, lift)


def near_call(dev, near_leaves, near_offsets, pos, chg, before, after):
    return pl.pallas_call(
        near_kernel,
        out_shape=shape(128, 128),
        in_specs=[SMEM] + [VMEM] * 6,
        out_specs=VMEM,
        scratch_shapes=[
            pltpu.VMEM((LEAF + 2 * RIM, 8, 128), F32),
            pltpu.VMEM((LEAF + 2 * RIM, 128), F32),
            pltpu.VMEM((27, 8, 128), F32),
            pltpu.VMEM((NOBODY + 1, 128, 128), BF16),
            pltpu.VMEM((NOBODY + 1, 128, 128), F32),
            pltpu.VMEM((LEAF, 8, 128), F32),
            pltpu.VMEM((GROUP, 48, 128), BF16),
            pltpu.VMEM((40, 128), jnp.int32),
            pltpu.SMEM((40, 128), jnp.int32),
            pltpu.SemaphoreType.DMA(()),
        ],
        compiler_params=limits(56),
        cost_estimate=cost(30 * 10**9, 10**6),
        name="near",
    )(dev, near_leaves, near_offsets, pos, chg, before, after)


def far_call(dev, lists, classes, leaves, leaf_class, parents, parent_class, lt, pt, pos, near, arrived,
             down_shift, far_shift):
    return pl.pallas_call(
        far_kernel,
        out_shape=shape(128, 128),
        in_specs=[SMEM] * 3 + [VMEM] * 9 + [HBM] * 2,
        out_specs=VMEM,
        scratch_shapes=[
            pltpu.VMEM((2176, 640), BF16),
            pltpu.VMEM((640, 640), BF16),
            pltpu.VMEM((256, 2176), BF16),
            pltpu.VMEM((256, 2176), BF16),
            pltpu.VMEM((256, 640), BF16),
            pltpu.VMEM((3, 16 * TARGETS, 128), F32),
            pltpu.VMEM((144, 256), jnp.int32),
            pltpu.VMEM((144, 256), jnp.int32),
            pltpu.VMEM((256, 128), F32),
            pltpu.VMEM((384, 128), F32),
            pltpu.VMEM((384, 128), F32),
            pltpu.VMEM((128, 128), F32),
            pltpu.VMEM((3, 8 * COEF, 128), F32),
            pltpu.VMEM((8 * COEF, COEF), F32),
            pltpu.VMEM((3, 16 * COEF, 128), F32),
            pltpu.VMEM((16 * COEF, COEF), F32),
            pltpu.SemaphoreType.DMA((8,)),
        ],
        compiler_params=limits(52),
        cost_estimate=cost(20 * 10**9, 20 * 10**6),
        name="far",
    )(dev, lists, classes, leaves, leaf_class, parents, parent_class, lt, pt, pos, near, arrived,
      down_shift, far_shift)


def by_rows(operators):
    return jnp.swapaxes(operators, 0, 1).reshape(-1, operators.shape[2])


def per_device(
    positions,
    charges,
    near_leaves,
    near_offsets,
    far_leaves,
    far_leaf_class,
    leaf_plan,
    far_parents,
    far_parent_class,
    parent_plan,
    coarse_lists,
    coarse_class,
    up_shift,
    down_shift,
    far_shift,
):
    device = lax.axis_index(AXES)
    dev = device.reshape(1).astype(jnp.int32)
    plans = jnp.concatenate([leaf_plan[0], parent_plan[0]], 1)
    asked = lax.all_to_all(plans, AXES, split_axis=0, concat_axis=0, tiled=True)
    pos = positions.reshape(3, LEAF, 128)
    chg = charges.reshape(LEAF, 128)
    rims = [
        jnp.concatenate([pos[:, rows], chg[None, rows]], 0)
        for rows in (slice(LEAF - RIM, LEAF), slice(0, RIM))
    ]
    size = lax.axis_size(AXES)
    up = [(i, i + 1) for i in range(size - 1)]
    down = [(j, i) for i, j in up]
    before = lax.ppermute(rims[0], AXES, up)
    after = lax.ppermute(rims[1], AXES, down)
    lt, pt, lift = upward_call(dev, pos, chg, by_rows(up_shift))
    before, after, asked, lt = lax.optimization_barrier((before, after, asked, lt))
    outgoing = pack_call(asked, lt, pt, lift)
    outgoing = outgoing.reshape(LEAF, ROWS, 128)
    near_leaves, outgoing = lax.optimization_barrier((near_leaves, outgoing))
    arrived = lax.all_to_all(outgoing, AXES, split_axis=0, concat_axis=0, tiled=True)
    arrived = arrived.reshape(LEAF * ROWS, 128)
    near = near_call(dev, near_leaves.T, near_offsets.T, pos, chg, before, after)
    potential = far_call(
        dev, coarse_lists.reshape(-1), coarse_class.reshape(-1), far_leaves.T, far_leaf_class.T,
        far_parents, far_parent_class, lt, pt, pos, near, arrived,
        by_rows(down_shift), by_rows(far_shift),
    )
    return potential.reshape(-1)


def solution(mesh):
    row = P(AXES, None)
    placed = (
        P(None, AXES), P(AXES), row, row, row, row, P(AXES, None, None), row, row,
        P(AXES, None, None), P(), P(), P(), P(), P(),
    )
    return jax.shard_map(
        per_device, mesh=mesh, in_specs=placed, out_specs=P(AXES), check_vma=False
    )
```

```python
import jax
import jax.numpy as jnp
import numpy as np
from jax import lax
from jax.experimental import pallas as pl
from jax.experimental.pallas import tpu as pltpu
from jax.sharding import PartitionSpec as P

ORDER = 10
COEF = 286
RIM = 32
LEAF = 128
K_NEAR = 27
CAP_L = 16
CAP_P = 4
ROWS = 48
PACK_MIB = 24
TARGETS = 160
GROUP = 128
NOBODY = LEAF + 2 * RIM
SOFT = 0.05 * 0.05
AXES = ("gx", "gy")
F32 = jnp.float32
BF16 = jnp.bfloat16
VMEM = pl.BlockSpec(memory_space=pltpu.VMEM)
SMEM = pl.BlockSpec(memory_space=pltpu.SMEM)
HBM = pl.BlockSpec(memory_space=pl.ANY)


def exponents(order):
    entries = []
    for degree in range(order + 1):
        for first_power in range(degree, -1, -1):
            for second_power in range(degree - first_power, -1, -1):
                entries.append((first_power, second_power, degree - first_power - second_power))
    return entries


INDEX = {powers: number for number, powers in enumerate(exponents(ORDER))}


def split(x):
    high = x.astype(BF16)
    return high, (x - high.astype(F32)).astype(BF16)


def nt(a, b):
    return lax.dot_general(a, b, (((1,), (1,)), ((), ())), preferred_element_type=F32)


def nn(a, b):
    return jnp.dot(a, b, preferred_element_type=F32)


def turn(x, left):
    return pltpu.roll(x, 128 - left, 1)


def apply_parts(operator, high, low):
    operator_high, operator_low = split(operator)
    both = nn(operator_high, jnp.concatenate([high, low], axis=1))
    return both[:, 0:128] + (both[:, 128:256] + nn(operator_low, high))


def apply_operator(operator, columns):
    return apply_parts(operator, *split(columns))


def pieces(origin, scratch, sems, first):
    rows = scratch.shape[0]
    size = (rows // 4 + 7) // 8 * 8
    return [
        pltpu.make_async_copy(
            origin.at[pl.ds(size * i, min(size, rows - size * i))],
            scratch.at[pl.ds(size * i, min(size, rows - size * i))],
            sems.at[first + i],
        )
        for i in range(4)
    ]


def start(copies):
    for copy in copies:
        copy.start()


def wait(copies):
    for copy in copies:
        copy.wait()


def cut(source, chunks):
    chunks[0] = source[:, 0:128]
    chunks[1] = source[:, 128:256]
    chunks[2] = jnp.zeros(chunks.shape[1:], F32)
    chunks[2, :, 0 : COEF - 256] = source[:, 256:COEF]


def chunk_at(chunks, h, number, count):
    return chunks[h, pl.ds(number, COEF, stride=count), :]


def operator_at(chunks, number, count):
    return jnp.concatenate([chunk_at(chunks, h, number, count) for h in range(3)], axis=1)


def eight_operators(chunks, numbers, count):
    parts = [
        jnp.concatenate([chunk_at(chunks, h, number, count) for h in range(2)], axis=1)
        for number in numbers
    ]
    halves = []
    for g in range(2):
        half = chunk_at(chunks, 2, numbers[4 * g], count)
        for p in range(1, 4):
            half = half + pltpu.roll(chunk_at(chunks, 2, numbers[4 * g + p], count), 32 * p, 1)
        halves.append(half)
    return parts + [jnp.concatenate(halves, axis=1)]


def eight_columns(columns):
    return [c[0:256] for c in columns] + [jnp.concatenate([c[256:288] for c in columns], axis=0)]


def apply_eight(chunks, columns, total):
    operators = eight_operators(chunks, range(8), 8)
    for operator, part in zip(operators, eight_columns(columns)):
        total = total + apply_operator(operator, part)
    return total


def upward_kernel(dev_ref, pos_ref, chg_ref, up_hbm, lt_ref, pt_ref, lift_ref, moments, column, up_ref,
                  stored_up, sems):
    copies = pieces(up_hbm, stored_up, sems, 0)
    start(copies)
    x, y, z = [2.0 * pos_ref[d].T for d in range(3)]
    with_x = chg_ref[...].T
    z_powers = [None, z]
    for k in range(ORDER - 1):
        z_powers.append(z_powers[-1] * z)
    moments[COEF - 6 : 384, :] = jnp.zeros((384 - COEF + 6, LEAF), F32)
    for i in range(ORDER + 1):
        if i:
            with_x = with_x * x
        with_xy = with_x
        for j in range(ORDER + 1 - i):
            if j:
                with_xy = with_xy * y
            for k in range(ORDER + 1 - i - j):
                term = with_xy * z_powers[k] if k else with_xy
                a = INDEX[(i, j, k)]
                moments[a : a + 1, :] = jnp.sum(term, axis=0, keepdims=True)
    for h in range(3):
        lt_ref[h] = moments[128 * h : 128 * h + 128, :].T
    column[...] = jnp.zeros_like(column)
    wait(copies)
    cut(stored_up, up_ref)
    lane = lax.broadcasted_iota(jnp.int32, (384, 128), 1)
    leaves = moments[...]
    total = jnp.zeros((COEF, 128), F32)
    total = apply_eight(up_ref, [jnp.where(lane % 8 == c, leaves, 0.0) for c in range(8)], total)
    for left in (4, 2, 1):
        total = total + turn(total, left)
    column[0:COEF, :] = total
    parents = column[...]
    total = jnp.zeros((COEF, 128), F32)
    total = apply_eight(
        up_ref, [jnp.where(lane % 64 == 8 * c, parents, 0.0) for c in range(8)], total
    )
    for h in range(3):
        moments[0:128, :] = column[128 * h : 128 * h + 128, :].T
        pt_ref[h] = moments[pl.ds(0, 16, stride=8), :]
    for left in (8, 16, 32):
        total = total + turn(total, left)
    column[0:COEF, :] = total
    grand = column[...]
    first = lax.rem(2 * dev_ref[0], 8)
    total = apply_operator(operator_at(up_ref, first, 8), jnp.where(lane == 0, grand, 0.0))
    total = total + apply_operator(
        operator_at(up_ref, first + 1, 8), jnp.where(lane == 64, grand, 0.0)
    )
    column[0:COEF, :] = total + turn(total, 64)
    for h in range(3):
        lift_ref[h : h + 1, :] = column[128 * h : 128 * h + 128, :].T[0:1, :]


def pack_kernel(asked_ref, lt_ref, pt_ref, lift_ref, out_ref):
    for h in range(3):
        out_ref[pl.ds(45 + h, 128, stride=ROWS), :] = jnp.broadcast_to(
            lift_ref[h : h + 1, :], (128, 128)
        )
    lane = lax.broadcasted_iota(jnp.int32, (128, 128), 1)
    leaf_rows = jnp.concatenate([lt_ref[h] for h in range(3)], axis=1)
    parent_rows = jnp.concatenate([pt_ref[h] for h in range(3)], axis=1)
    parent_rows = jnp.concatenate([parent_rows, jnp.zeros((112, 384), F32)], axis=0)
    leaf_rows = jnp.concatenate(split(leaf_rows), axis=0)
    parent_rows = jnp.concatenate(split(parent_rows), axis=0)
    for q in range(5):
        tail = jnp.zeros((128, 128), F32)
        for p in range(4):
            j = 4 * q + p
            chosen = jnp.where(asked_ref[:, j : j + 1] == lane, 1.0, 0.0).astype(BF16)
            chosen = jnp.concatenate([chosen, chosen], axis=1)
            rows = nn(chosen, leaf_rows if q < 4 else parent_rows)
            out_ref[pl.ds(2 * j, 128, stride=ROWS), :] = rows[:, 0:128]
            out_ref[pl.ds(2 * j + 1, 128, stride=ROWS), :] = rows[:, 128:256]
            part = rows[:, 256:384]
            tail = tail + (pltpu.roll(part, 32 * p, 1) if p else part)
        out_ref[pl.ds(40 + q, 128, stride=ROWS), :] = tail


def near_kernel(dev_ref, leaves_ref, offsets_ref, pos_ref, chg_ref, before_ref, after_ref, out_ref,
                eight, charge, offsets, features, spread, sums, ready, lists, plan, sem):
    sub = lax.broadcasted_iota(jnp.int32, (8, 128), 0)
    named = leaves_ref[...]
    first_leaf = dev_ref[0] * LEAF
    present = named >= 0
    own_id = first_leaf + lax.broadcasted_iota(jnp.int32, (K_NEAR, LEAF), 1)
    itself = (named == own_id) & (offsets_ref[...] == 13)
    counted = present & jnp.logical_not(itself)
    code = jnp.where(counted, (named - first_leaf + RIM) * 32 + offsets_ref[...], NOBODY * 32 + 13)
    count = jnp.sum(jnp.where(present, 1.0, 0.0), axis=0, keepdims=True).astype(jnp.int32)
    quads = jnp.maximum((count + 2) // 4, 1)
    selves = jnp.sum(jnp.where(itself, 1.0, 0.0), axis=0, keepdims=True).astype(jnp.int32)
    total = jnp.sum(quads.astype(F32), axis=1, keepdims=True).astype(jnp.int32)
    lists[...] = jnp.full_like(lists, NOBODY * 32 + 13)
    lists[0:K_NEAR, :] = code
    lists[37:38, :] = quads
    lists[38:39, :] = selves
    lists[39:40, :] = jnp.broadcast_to(total, (1, 128))
    copy = pltpu.make_async_copy(lists, plan, sem)
    copy.start()
    eight[:, 3, :] = jnp.full((LEAF + 2 * RIM, 128), 1.0, F32)
    eight[:, 7, :] = jnp.full((LEAF + 2 * RIM, 128), SOFT, F32)
    eight3 = ((0, 4), (1, 5), (2, 6))
    for d in range(3):
        for row in eight3[d]:
            eight[0:RIM, row, :] = before_ref[d]
            eight[RIM : RIM + LEAF, row, :] = pos_ref[d]
            eight[RIM + LEAF : 2 * RIM + LEAF, row, :] = after_ref[d]
    charge[0:RIM, :] = before_ref[3]
    charge[RIM : RIM + LEAF, :] = chg_ref[...]
    charge[RIM + LEAF : 2 * RIM + LEAF, :] = after_ref[3]
    lane = lax.broadcasted_iota(jnp.int32, (128, 128), 1)
    features[NOBODY] = jnp.where(lane == 7, 1.0, 0.0).astype(BF16)
    spread[NOBODY] = jnp.zeros((128, 128), F32)
    for o in range(27):
        shift = (o // 9 - 1, o // 3 % 3 - 1, o % 3 - 1)
        table = jnp.zeros((8, 128), F32)
        for d in range(3):
            table = jnp.where((sub == d) | (sub == d + 4), -float(shift[d]), table)
        offsets[o] = table
    squares = (sub >= 4) & (sub < 7)

    def thirds(v):
        high = v.astype(BF16).astype(F32)
        rest = v - high
        middle = rest.astype(BF16).astype(F32)
        return high, middle, rest - middle

    def target(leaf, offset):
        v = eight[RIM + leaf] + offsets[offset]
        v = jnp.where(squares, v * v, v)
        high, middle, low = thirds(v)
        return jnp.concatenate([high, high, high, middle, middle, low], axis=0).astype(BF16)

    def separations(leaf, rows):
        padded = jnp.concatenate([rows, jnp.zeros((80, 128), BF16)], axis=0)
        return nn(features[leaf], padded)

    row = lax.broadcasted_iota(jnp.int32, (128, 128), 0)
    three = jnp.where((row >= 48) & (row < 51), 1.0, 0.0).astype(BF16)
    diagonal = row == lane
    identity = jnp.where(diagonal, 1.0, 0.0).astype(BF16)

    def source(leaf):
        v = eight[leaf]
        norm = jnp.sum(jnp.where(sub < 3, v * v, 0.0), axis=0, keepdims=True)
        v = jnp.where(sub < 3, -2.0 * v, jnp.where(sub == 3, norm, 1.0))
        high, middle, low = thirds(v)
        first, second, third = thirds(charge[pl.ds(leaf, 1), :])
        parts = jnp.where(sub == 0, first, jnp.where(sub == 1, second, jnp.where(sub == 2, third, 0.0)))
        rows = jnp.concatenate([high, middle, low, high, middle, high, parts], axis=0)
        rows = jnp.concatenate([rows, jnp.zeros((72, 128), F32)], axis=0)
        rows = rows.T.astype(BF16)
        features[leaf] = rows
        spread[leaf] = nn(rows, three)

    def prepare(step, carry):
        for u in range(48):
            source(48 * step + u)
        return carry

    lax.fori_loop(0, (LEAF + 2 * RIM) // 48, prepare, 0)
    copy.wait()

    def own_leaf(step, carry):
        for u in range(32):
            leaf = 32 * step + u
            squared = separations(RIM + leaf, target(leaf, 13))
            terms = jnp.where(diagonal, 0.0, spread[RIM + leaf] * lax.rsqrt(squared))
            sums[leaf] = jnp.sum(terms.reshape(16, 8, 128), axis=0) * plan[38, leaf].astype(F32)
        return carry

    lax.fori_loop(0, LEAF // 32, own_leaf, 0)

    def advance(state):
        leaf, quad = state
        last = quad + 1 >= plan[37, leaf]
        return (
            jnp.where(last, jnp.minimum(leaf + 1, LEAF - 1), leaf),
            jnp.where(last, jnp.where(leaf == LEAF - 1, 7, 0), quad + 1),
        )

    def produce(states):
        for g, (leaf, quad) in enumerate(states):
            for u in range(4):
                code = plan[4 * quad + u + 1, leaf]
                ready[4 * g + u] = target(leaf, code & 31)

    def consume(states):
        for g, (leaf, quad) in enumerate(states):
            part = sums[leaf]
            for u in range(4):
                code = plan[4 * quad + u + 1, leaf]
                squared = separations(code >> 5, ready[4 * g + u])
                terms = spread[code >> 5] * lax.rsqrt(squared)
                part = part + jnp.sum(terms.reshape(16, 8, 128), axis=0)
            sums[leaf] = part

    def following(state, number):
        made = []
        for _ in range(number):
            state = advance(state)
            made.append(state)
        return tuple(made)

    first = (jnp.int32(0), jnp.int32(0))
    states = (first,) + following(first, GROUP // 4 - 1)
    produce(states)

    def one_group(step, states):
        after = following(states[-1], GROUP // 4)
        consume(states)
        produce(after)
        return after

    quads = GROUP // 4
    lax.fori_loop(0, (plan[39, 0] + quads - 1) // quads, one_group, states)
    out_ref[...] = jnp.sum(sums[...], axis=1)


def count_rows(code, low, rows):
    wide = lax.broadcasted_iota(jnp.int32, (rows, 256), 0) == code
    narrow = lax.broadcasted_iota(jnp.int32, (128, 256), 0) == low
    return nt(
        jnp.where(wide, 1.0, 0.0).astype(BF16), jnp.where(narrow, 1.0, 0.0).astype(BF16)
    ).astype(BF16)


def encode(slots, classes, cells, capacity):
    ghost = jnp.maximum(slots - cells, 0)
    own = slots < cells
    code = jnp.where(own, 0, 1 + lax.rem(ghost, capacity)) * 16 + classes
    return jnp.where(slots < 0, -1, code), jnp.where(own, slots, lax.div(ghost, capacity))


def count(code_ref, low_ref, first, capacity, table_ref):
    blocks = capacity + 1
    for t in range(16):
        rows = pl.ds(first + t, 1)
        table = count_rows(code_ref[rows, :], low_ref[rows, :], 16 * blocks)
        for b in range(blocks):
            table_ref[16 * t : 16 * t + 16, 128 * b : 128 * b + 128] = table[16 * b : 16 * b + 16]


def counts_kernel(leaf_ref, leaf_class_ref, parent_ref, parent_class_ref, parent_table_ref, code_ref,
                  low_ref, turned):
    width = leaf_ref.shape[0]
    code_ref[...] = jnp.full_like(code_ref, -1)
    low_ref[...] = jnp.full_like(low_ref, -1)
    for part, rows in zip(
        encode(leaf_ref[...], leaf_class_ref[...], LEAF, CAP_L), (code_ref, low_ref)
    ):
        turned[...] = jnp.full_like(turned, -1.0)
        turned[:width, :] = part.astype(F32)
        rows[0:128, 0:128] = turned[0:128, :].T.astype(jnp.int32)
        rows[0:128, 128:256] = turned[128:256, :].T.astype(jnp.int32)
    for part, rows in zip(
        encode(parent_ref[...], parent_class_ref[...], 16, CAP_P), (code_ref, low_ref)
    ):
        rows[128:144, :width] = part
    count(code_ref, low_ref, 128, CAP_P, parent_table_ref)


def far_kernel(dev_ref, lists_ref, class_ref, code_ref, low_ref, parent_table_ref, lt_ref, pt_ref,
               pos_ref, near_ref, arrived_ref, down_hbm, far_hbm, out_ref,
               src, src_parent, even, odd, grouped, column, loc, result, down_ref, stored_down,
               far_ref, stored_far, sems):
    far_copies = pieces(far_hbm, stored_far, sems, 0)
    down_copies = pieces(down_hbm, stored_down, sems, 4)
    lane = lax.broadcasted_iota(jnp.int32, (128, 128), 1)

    def place(ref, row, parts):
        count = parts[0].shape[0]
        (h0, l0), (h1, l1) = split(parts[0]), split(parts[1])
        tail = parts[2]
        high = tail.astype(BF16).astype(F32)
        low = pltpu.roll(tail - high, 32, 1)
        ref[row : row + count, 0:128] = h0
        ref[row : row + count, 128:256] = h1
        ref[row : row + count, 256:384] = l0
        ref[row : row + count, 384:512] = l1
        ref[row : row + count, 512:640] = (high + low).astype(BF16)

    def collect(product, row, count):
        grouped[0, pl.ds(row, count), :] = product[:, 0:128] + product[:, 256:384]
        grouped[1, pl.ds(row, count), :] = product[:, 128:256] + product[:, 384:512]
        tail = product[:, 512:640]
        grouped[2, pl.ds(row, count), :] = tail + pltpu.roll(tail, 96, 1)

    def arrived_tail(row, p):
        part = arrived_ref[pl.ds(row, 128, stride=ROWS), :]
        part = pltpu.roll(part, 128 - 32 * p, 1) if p else part
        return jnp.where(lane < 32, part, 0.0)

    start(far_copies)
    start(down_copies)
    count(code_ref, low_ref, 0, CAP_L, even)
    place(src, 0, [lt_ref[h] for h in range(3)])
    for c in range(CAP_L):
        place(
            src,
            128 * (c + 1),
            [arrived_ref[pl.ds(2 * c, 128, stride=ROWS), :], arrived_ref[pl.ds(2 * c + 1, 128, stride=ROWS), :], arrived_tail(40 + c // 4, c % 4)],
        )
    own = [jnp.concatenate([pt_ref[h], jnp.zeros((112, 128), F32)], axis=0) for h in range(3)]
    place(src_parent, 0, own)
    for c in range(CAP_P):
        place(
            src_parent,
            128 * (c + 1),
            [arrived_ref[pl.ds(32 + 2 * c, 128, stride=ROWS), :], arrived_ref[pl.ds(33 + 2 * c, 128, stride=ROWS), :], arrived_tail(44, c)],
        )
    collect(nn(parent_table_ref[...], src_parent[...]), 2048, 256)
    mine = dev_ref[0] // 4
    operator = lax.broadcasted_iota(jnp.int32, (16, 128), 0)
    cell = lax.broadcasted_iota(jnp.int32, (16, 128), 1) // 4
    chosen = jnp.zeros((16, 128), F32)
    for k in range(7):
        hit = (operator == class_ref[mine * 7 + k]) & (cell == lists_ref[mine * 7 + k])
        chosen = chosen + jnp.where(hit, 1.0, 0.0)
    chosen = chosen.astype(BF16)
    for h in range(3):
        high, low = split(arrived_ref[pl.ds(45 + h, 128, stride=ROWS), :])
        grouped[h, 2304:2320, :] = nn(chosen, high) + nn(chosen, low)
        grouped[h, 2320:2560, :] = jnp.zeros((240, 128), F32)

    def two_blocks(step, carry):
        row = pl.multiple_of(step * 512, 512)
        count(code_ref, low_ref, 32 * step + 16, CAP_L, odd)
        collect(nn(even[...], src[...]), row, 256)
        count(code_ref, low_ref, jnp.minimum(32 * step + 32, 112), CAP_L, even)
        collect(nn(odd[...], src[...]), row + 256, 256)
        return carry

    lax.fori_loop(0, 4, two_blocks, 0)

    wait(far_copies)
    cut(stored_far, far_ref)
    column[...] = jnp.zeros_like(column)
    loc[...] = jnp.zeros_like(loc)
    tall = lax.broadcasted_iota(jnp.int32, (384, 128), 1)
    leaf_total = jnp.zeros((COEF, 128), F32)
    upper_total = jnp.zeros((COEF, 128), F32)
    for half in range(2):
        numbers = range(8 * half, 8 * half + 8)
        uppers = []
        for q in (2 * half, 2 * half + 1):
            upper = jnp.concatenate(
                [
                    jnp.concatenate(
                        [grouped[h, pl.ds(2048 + 4 * q + p, 32, stride=16), :] for p in range(4)],
                        axis=0,
                    ).T
                    for h in range(3)
                ],
                axis=0,
            )
            uppers += [jnp.where(tall // 32 == p, upper, 0.0) for p in range(4)]
        leaves = [
            jnp.concatenate([grouped[h, pl.ds(o, 128, stride=16), :].T for h in range(3)], axis=0)
            for o in numbers
        ]
        for operator, leaf, upper in zip(
            eight_operators(far_ref, numbers, 16), eight_columns(leaves), eight_columns(uppers)
        ):
            operator_high, operator_low = split(operator)
            leaf_high, leaf_low = split(leaf)
            upper_high, upper_low = split(upper)
            first = nn(operator_high, jnp.concatenate([leaf_high, leaf_low], axis=1))
            second = nn(operator_high, jnp.concatenate([upper_high, upper_low], axis=1))
            third = nn(operator_low, jnp.concatenate([leaf_high, upper_high], axis=1))
            leaf_total = leaf_total + (first[:, 0:128] + (first[:, 128:256] + third[:, 0:128]))
            upper_total = upper_total + (
                second[:, 0:128] + (second[:, 128:256] + third[:, 128:256])
            )
    upper_total = upper_total + turn(upper_total, 32)
    upper_total = upper_total + turn(upper_total, 64)
    wait(down_copies)
    cut(stored_down, down_ref)
    column[0:COEF, :] = upper_total
    coarse = jnp.broadcast_to(column[:, 16:17], (384, 128))
    first = lax.rem(2 * dev_ref[0], 8)
    grand = apply_operator(operator_at(down_ref, first, 8), jnp.where(tall < 8, coarse, 0.0))
    grand = grand + apply_operator(
        operator_at(down_ref, first + 1, 8), jnp.where((tall >= 8) & (tall < 16), coarse, 0.0)
    )
    loc[0:COEF, :] = grand
    grand = loc[...]
    upper_total = apply_eight(
        down_ref,
        [jnp.where((tall % 8 == c) & (tall < 16), grand, 0.0) for c in range(8)],
        upper_total,
    )
    column[0:COEF, :] = upper_total
    parents = split(jnp.where(tall < 16, column[...], 0.0))
    repeat = lax.broadcasted_iota(jnp.int32, (128, 128), 0) == lane // 8
    repeat = jnp.where(repeat, 1.0, 0.0).astype(BF16)
    parents = [nn(part, repeat) for part in parents]
    high, low = [
        eight_columns([jnp.where(tall % 8 == c, part, 0.0) for c in range(8)]) for part in parents
    ]
    for operator, high_part, low_part in zip(eight_operators(down_ref, range(8), 8), high, low):
        leaf_total = leaf_total + apply_parts(operator, high_part.astype(BF16), low_part.astype(BF16))
    loc[0:COEF, :] = leaf_total
    x_all, y_all, z_all = [2.0 * pos_ref[d].T for d in range(3)]
    for part in range(2):
        piece = slice(64 * part, 64 * part + 64)
        x, y, z = x_all[piece], y_all[piece], z_all[piece]
        over_i = None
        for i in range(ORDER, -1, -1):
            over_j = None
            for j in range(ORDER - i, -1, -1):
                over_k = None
                for k in range(ORDER - i - j, -1, -1):
                    a = INDEX[(i, j, k)]
                    value = loc[a : a + 1, :]
                    over_k = value if over_k is None else over_k * z + value
                over_j = over_k if over_j is None else over_j * y + over_k
            over_i = over_j if over_i is None else over_i * x + over_j
        result[piece, :] = over_i
    out_ref[...] = near_ref[...] + result[...].T


def cost(flops, moved):
    return pl.CostEstimate(flops=flops, bytes_accessed=moved, transcendentals=0)


def shape(*dims, dtype=F32):
    return jax.ShapeDtypeStruct(dims, dtype)


def limits(mib):
    return pltpu.CompilerParams(vmem_limit_bytes=mib * 1024 * 1024)


def upward_call(dev, pos, chg, up_shift):
    return pl.pallas_call(
        upward_kernel,
        out_shape=(shape(3, 128, 128), shape(3, 16, 128), shape(3, 128)),
        in_specs=[SMEM] + [VMEM] * 2 + [HBM],
        out_specs=(VMEM, VMEM, VMEM),
        scratch_shapes=[
            pltpu.VMEM((384, 128), F32),
            pltpu.VMEM((384, 128), F32),
            pltpu.VMEM((3, 8 * COEF, 128), F32),
            pltpu.VMEM((8 * COEF, COEF), F32),
            pltpu.SemaphoreType.DMA((4,)),
        ],
        compiler_params=limits(40),
        cost_estimate=cost(8 * 10**9, 3 * 10**6),
        name="upward",
    )(dev, pos, chg, up_shift)


def pack_call(asked, lt, pt, lift):
    return pl.pallas_call(
        pack_kernel,
        out_shape=shape(128 * ROWS, 128),
        in_specs=[VMEM] * 4,
        out_specs=VMEM,
        compiler_params=limits(PACK_MIB),
        cost_estimate=cost(10**9, 4 * 10**6),
        name="pack",
    )(asked, lt, pt, lift)


def near_call(dev, near_leaves, near_offsets, pos, chg, before, after):
    return pl.pallas_call(
        near_kernel,
        out_shape=shape(128, 128),
        in_specs=[SMEM] + [VMEM] * 6,
        out_specs=VMEM,
        scratch_shapes=[
            pltpu.VMEM((LEAF + 2 * RIM, 8, 128), F32),
            pltpu.VMEM((LEAF + 2 * RIM, 128), F32),
            pltpu.VMEM((27, 8, 128), F32),
            pltpu.VMEM((NOBODY + 1, 128, 128), BF16),
            pltpu.VMEM((NOBODY + 1, 128, 128), F32),
            pltpu.VMEM((LEAF, 8, 128), F32),
            pltpu.VMEM((GROUP, 48, 128), BF16),
            pltpu.VMEM((40, 128), jnp.int32),
            pltpu.SMEM((40, 128), jnp.int32),
            pltpu.SemaphoreType.DMA(()),
        ],
        compiler_params=limits(56),
        cost_estimate=cost(30 * 10**9, 10**6),
        name="near",
    )(dev, near_leaves, near_offsets, pos, chg, before, after)


def counts_call(leaves, leaf_class, parents, parent_class):
    return pl.pallas_call(
        counts_kernel,
        out_shape=(
            shape(256, 640, dtype=BF16),
            shape(144, 256, dtype=jnp.int32),
            shape(144, 256, dtype=jnp.int32),
        ),
        in_specs=[VMEM] * 4,
        out_specs=(VMEM,) * 3,
        scratch_shapes=[pltpu.VMEM((256, 128), F32)],
        compiler_params=limits(40),
        cost_estimate=cost(4 * 10**9, 10**6),
        name="counts",
    )(leaves, leaf_class, parents, parent_class)


def far_call(dev, lists, classes, code, low, parent_table, lt, pt, pos, near, arrived, down_shift,
             far_shift):
    return pl.pallas_call(
        far_kernel,
        out_shape=shape(128, 128),
        in_specs=[SMEM] * 3 + [VMEM] * 8 + [HBM] * 2,
        out_specs=VMEM,
        scratch_shapes=[
            pltpu.VMEM((2176, 640), BF16),
            pltpu.VMEM((640, 640), BF16),
            pltpu.VMEM((256, 2176), BF16),
            pltpu.VMEM((256, 2176), BF16),
            pltpu.VMEM((3, 16 * TARGETS, 128), F32),
            pltpu.VMEM((384, 128), F32),
            pltpu.VMEM((384, 128), F32),
            pltpu.VMEM((128, 128), F32),
            pltpu.VMEM((3, 8 * COEF, 128), F32),
            pltpu.VMEM((8 * COEF, COEF), F32),
            pltpu.VMEM((3, 16 * COEF, 128), F32),
            pltpu.VMEM((16 * COEF, COEF), F32),
            pltpu.SemaphoreType.DMA((8,)),
        ],
        compiler_params=limits(52),
        cost_estimate=cost(20 * 10**9, 20 * 10**6),
        name="far",
    )(dev, lists, classes, code, low, parent_table, lt, pt, pos, near, arrived, down_shift,
      far_shift)


def by_rows(operators):
    return jnp.swapaxes(operators, 0, 1).reshape(-1, operators.shape[2])


def per_device(
    positions,
    charges,
    near_leaves,
    near_offsets,
    far_leaves,
    far_leaf_class,
    leaf_plan,
    far_parents,
    far_parent_class,
    parent_plan,
    coarse_lists,
    coarse_class,
    up_shift,
    down_shift,
    far_shift,
):
    device = lax.axis_index(AXES)
    dev = device.reshape(1).astype(jnp.int32)
    plans = jnp.concatenate([leaf_plan[0], parent_plan[0]], 1)
    asked = lax.all_to_all(plans, AXES, split_axis=0, concat_axis=0, tiled=True)
    pos = positions.reshape(3, LEAF, 128)
    chg = charges.reshape(LEAF, 128)
    rims = [
        jnp.concatenate([pos[:, rows], chg[None, rows]], 0)
        for rows in (slice(LEAF - RIM, LEAF), slice(0, RIM))
    ]
    size = lax.axis_size(AXES)
    up = [(i, i + 1) for i in range(size - 1)]
    down = [(j, i) for i, j in up]
    before = lax.ppermute(rims[0], AXES, up)
    after = lax.ppermute(rims[1], AXES, down)
    lt, pt, lift = upward_call(dev, pos, chg, by_rows(up_shift))
    before, after, asked, lt = lax.optimization_barrier((before, after, asked, lt))
    outgoing = pack_call(asked, lt, pt, lift)
    outgoing = outgoing.reshape(LEAF, ROWS, 128)
    near_leaves, far_leaves, outgoing = lax.optimization_barrier(
        (near_leaves, far_leaves, outgoing)
    )
    arrived = lax.all_to_all(outgoing, AXES, split_axis=0, concat_axis=0, tiled=True)
    arrived = arrived.reshape(LEAF * ROWS, 128)
    near = near_call(dev, near_leaves.T, near_offsets.T, pos, chg, before, after)
    parent_table, code, low = counts_call(
        far_leaves.T, far_leaf_class.T, far_parents, far_parent_class
    )
    potential = far_call(
        dev, coarse_lists.reshape(-1), coarse_class.reshape(-1), code, low, parent_table, lt, pt, pos,
        near, arrived, by_rows(down_shift), by_rows(far_shift),
    )
    return potential.reshape(-1)


def solution(mesh):
    row = P(AXES, None)
    placed = (
        P(None, AXES), P(AXES), row, row, row, row, P(AXES, None, None), row, row,
        P(AXES, None, None), P(), P(), P(), P(), P(),
    )
    return jax.shard_map(
        per_device, mesh=mesh, in_specs=placed, out_specs=P(AXES), check_vma=False
    )
```
